32 devices in a mesh: runs: 2 (over x), mesh: 16 (over z, y, core).
Axes of the slice: x: 2, y: 2, z: 4, core: 2. Of those that a mesh axis runs over, the one named last changes fastest.
Arguments:
- velocity: float32 [6, 256, 2048], P('runs', None, 'mesh'), parts along dimension 0, may hold values from -4 to 4
- magnetic: float32 [6, 256, 2048], P('runs', None, 'mesh'), parts along dimension 0, may hold values from -4 to 4
- mass_blocks: float32 [6, 6, 2048], P(None, None, 'mesh'), may hold values from -1 to 12, as said below
- stiff_blocks: float32 [6, 6, 2048], P(None, None, 'mesh'), may hold values from -2 to 24, as said below
- twist_blocks: float32 [6, 6, 2048], P(None, None, 'mesh'), may hold values from -0.00024414062 to 0.0029296875, as said below
- diffusivity: float32 [4096], P(('runs', 'mesh')), parts along dimension 0, may hold values from 1 to 8, as said below
- connectivity: int32 [6, 2048], P(None, 'mesh'), may hold values from 0 to 191, as said below
- ghost_lists: int32 [2, 512], P(None, 'mesh'), may hold values from 0 to 127, as said below
Outputs:
- new_velocity: float32 [6, 256, 2048], P('runs', None, 'mesh'), parts along dimension 0
- new_magnetic: float32 [6, 256, 2048], P('runs', None, 'mesh'), parts along dimension 0
The draws below stay inside these ranges and needn't reach their ends.
There are 2 independent parts, one for each index of `runs`. The reference program is written for one: setup_inputs(seed, part) draws one part's arguments, and reference() takes and returns one part's arrays. A program takes and returns all parts, laid end to end along the dimension named above; an argument that names none is the same for every part. Nothing has to cross between parts.
Inputs may be any that keep to these rules, and one draw needn't show every extreme that they name: `mass_blocks`: symmetric blocks; each diagonal entry exceeds the sum of magnitudes of the other entries of its row. An element that names ghost slots appears on both neighbouring devices with the same blocks, so the assembled operators are symmetric positive definite. `stiff_blocks`: as mass_blocks. `twist_blocks`: as mass_blocks. An element shared by two devices has the same diffusivity on both. `connectivity`: local indices as in the reference program: below 128 own nodes, then 32 ghost slots from the device below and 32 from the device above; every own node and every ghost slot is named by some element of its device. `ghost_lists`: within each row of one device the 32 entries are distinct; row 0 names nodes of the device below, row 1 nodes of the device above.
All inputs are finite; a program needn't handle non-finite values.
Results may differ from the reference program's by a relative error of at most 0.0001.
Values sent between devices are 32-bit elements; how exact they have to be, the bound alone decides.
No kernel may reach another device: no remote copies, remote signals or barrier semaphores. Data moves between devices by JAX's collectives and lax.ppermute only.
A program may use at most 64 MiB of HBM per device.

```python
import math
import jax
import jax.numpy as jnp
from jax import lax

MODES = 128
COEFS = 256
NODES_DEV = 128
GHOST = 32
IFACE = 11
ELEMS_DEV = 128
ITERS = 3
NODES = 2048
N_MESH = 16


def boundary_lists(key):
    device_keys = jax.random.split(key, N_MESH)
    shuffled = jax.vmap(lambda device_key: jax.random.permutation(device_key, NODES_DEV - 2) + 1)(device_keys)
    shuffled = shuffled.astype(jnp.int32)
    lower_side = jnp.concatenate([jnp.zeros((N_MESH, 1), jnp.int32), shuffled[:, :GHOST - 1]], axis=1)
    upper_side = jnp.concatenate([jnp.full((N_MESH, 1), NODES_DEV - 1, jnp.int32), shuffled[:, GHOST - 1:2 * GHOST - 2]], axis=1)
    return (lower_side, upper_side)


def one_block(key, leading, scale_factor):
    first_key, second_key = jax.random.split(key)
    raw_values = jax.random.uniform(first_key, leading + (6, 6), jnp.float32, -1.0, 1.0)
    symmetric = 0.5 * (raw_values + jnp.swapaxes(raw_values, -1, -2))
    diagonal = jax.random.uniform(second_key, leading + (6,), jnp.float32, 5.2, 12.0)
    on_diagonal = jnp.eye(6, dtype=jnp.bool_)
    return scale_factor * jnp.where(on_diagonal, diagonal[..., None], symmetric)


def element_blocks(key, scale_factor):
    first_key, second_key = jax.random.split(key)
    interior_count = ELEMS_DEV - 2 * IFACE
    shared = one_block(first_key, (N_MESH, IFACE), scale_factor)
    inner = one_block(second_key, (N_MESH, interior_count), scale_factor)
    merged = jnp.concatenate([jnp.roll(shared, 1, axis=0), shared, inner], axis=1)
    return jnp.moveaxis(merged.reshape((N_MESH * ELEMS_DEV, 6, 6)), 0, -1)


def node_scales(key, spread):
    position = jnp.arange(NODES, dtype=jnp.float32) / NODES
    rising = jnp.exp(0.5 * math.log(3.0) * position)
    roughness = jnp.exp(jax.random.uniform(key, (NODES,), jnp.float32, 0.0, math.log(spread)))
    return rising * roughness


def draw_velocity(key, part):
    key = jax.random.fold_in(key, 21)
    first_key, second_key = jax.random.split(key)
    noise_values = jnp.clip(jax.random.normal(first_key, (3, COEFS, NODES), jnp.float32), -4.0, 4.0)
    return noise_values * node_scales(second_key, 2.0) * 0.25


def draw_magnetic(key, part):
    key = jax.random.fold_in(key, 37)
    first_key, second_key = jax.random.split(key)
    noise_values = jnp.clip(jax.random.normal(first_key, (3, COEFS, NODES), jnp.float32), -4.0, 4.0)
    return noise_values * node_scales(second_key, 2.0) * 0.2


def draw_mass_blocks(key, part):
    key = jax.random.fold_in(key, 5)
    return element_blocks(key, 1.0)


def draw_stiff_blocks(key, part):
    key = jax.random.fold_in(key, 6)
    return element_blocks(key, 2.0)


def draw_twist_blocks(key, part):
    key = jax.random.fold_in(key, 7)
    return element_blocks(key, 4.0 / (MODES * MODES))


def draw_diffusivity(key, part):
    key = jax.random.fold_in(key, 9)
    first_key, second_key = jax.random.split(key)
    interior_count = ELEMS_DEV - 2 * IFACE
    shared = jnp.exp(jax.random.uniform(first_key, (N_MESH, IFACE), jnp.float32, 0.0, math.log(8.0)))
    inner = jnp.exp(jax.random.uniform(second_key, (N_MESH, interior_count), jnp.float32, 0.0, math.log(8.0)))
    merged = jnp.concatenate([jnp.roll(shared, 1, axis=0), shared, inner], axis=1)
    return merged.reshape((N_MESH * ELEMS_DEV,))


def draw_connectivity(key, part):
    lower_side, upper_side = boundary_lists(key)
    key = jax.random.fold_in(key, 11)
    slots = (3 * jnp.arange(IFACE, dtype=jnp.int32)[:, None] + jnp.arange(3, dtype=jnp.int32)[None, :]) % GHOST
    ghost_below = jnp.broadcast_to(NODES_DEV + slots, (N_MESH, IFACE, 3))
    ghost_above = jnp.broadcast_to(NODES_DEV + GHOST + slots, (N_MESH, IFACE, 3))
    below_elements = jnp.concatenate([ghost_below, lower_side[:, slots]], axis=2)
    above_elements = jnp.concatenate([upper_side[:, slots], ghost_above], axis=2)
    interior_count = ELEMS_DEV - 2 * IFACE
    positions = jnp.arange(interior_count, dtype=jnp.int32)
    first_nodes = jnp.broadcast_to((positions % NODES_DEV)[None, :, None], (N_MESH, interior_count, 1))
    second_nodes = jnp.broadcast_to(((positions + NODES_DEV // 2) % NODES_DEV)[None, :, None], (N_MESH, interior_count, 1))
    random_nodes = jax.random.randint(key, (N_MESH, interior_count, 4), 0, NODES_DEV, jnp.int32)
    interior = jnp.concatenate([first_nodes, second_nodes, random_nodes], axis=2)
    merged = jnp.concatenate([below_elements, above_elements, interior], axis=1).astype(jnp.int32)
    return jnp.moveaxis(merged, -1, 0).reshape((6, N_MESH * ELEMS_DEV))


def draw_ghost_lists(key, part):
    lower_side, upper_side = boundary_lists(key)
    from_below = jnp.roll(upper_side, 1, axis=0)
    from_above = jnp.roll(lower_side, -1, axis=0)
    return jnp.stack([from_below.reshape((-1,)), from_above.reshape((-1,))]).astype(jnp.int32)


def setup_inputs(seed: int = 0, part: int = 0) -> dict:
    keys = jax.random.split(jax.random.key(seed), 9)
    part_keys = jax.random.split(jax.random.fold_in(keys[8], part), 9)
    velocity = draw_velocity(jax.random.fold_in(jax.random.fold_in(keys[8], part), 71), part)
    magnetic = draw_magnetic(jax.random.fold_in(jax.random.fold_in(keys[8], part), 71), part)
    mass_blocks = draw_mass_blocks(jax.random.fold_in(keys[8], 71), part)
    stiff_blocks = draw_stiff_blocks(jax.random.fold_in(keys[8], 71), part)
    twist_blocks = draw_twist_blocks(jax.random.fold_in(keys[8], 71), part)
    diffusivity = draw_diffusivity(jax.random.fold_in(jax.random.fold_in(keys[8], part), 71), part)
    connectivity = draw_connectivity(jax.random.fold_in(keys[8], 71), part)
    ghost_lists = draw_ghost_lists(jax.random.fold_in(keys[8], 71), part)
    return {"velocity": velocity, "magnetic": magnetic, "mass_blocks": mass_blocks, "stiff_blocks": stiff_blocks, "twist_blocks": twist_blocks, "diffusivity": diffusivity, "connectivity": connectivity, "ghost_lists": ghost_lists}


time_step = 0.1
viscosity = 2.0
tilt_factor = 0.5
axial_factor = 1.0
lorentz_factor = 0.005
epsilon = 1e-6
highest = lax.Precision.HIGHEST


def transform_tables(coef_count, plane_count):
    mode_index = jnp.arange(coef_count, dtype=jnp.int32) // 2
    parity = jnp.arange(coef_count, dtype=jnp.int32) % 2
    planes = jnp.arange(plane_count, dtype=jnp.int32)
    phase_turns = (planes[:, None] * mode_index[None, :]) % plane_count
    angles = (2.0 * math.pi / plane_count) * phase_turns.astype(jnp.float32)
    inverse = jnp.where(parity[None, :] == 0, jnp.cos(angles), jnp.sin(angles))
    weight = jnp.where(mode_index == 0, 1.0, 2.0).astype(jnp.float32) / plane_count
    forward = jnp.transpose(inverse * weight[None, :])
    return inverse, forward


def cross_product(first_field, second_field):
    return jnp.stack([
        first_field[1] * second_field[2] - first_field[2] * second_field[1],
        first_field[2] * second_field[0] - first_field[0] * second_field[2],
        first_field[0] * second_field[1] - first_field[1] * second_field[0]])


def forcing_terms(velocity, magnetic):
    inverse, forward = transform_tables(velocity.shape[1], 2 * velocity.shape[1])
    plane_count = inverse.shape[0]
    phys_velocity = jnp.einsum('jc,kcn->kjn', inverse, velocity, precision=highest)
    phys_magnetic = jnp.einsum('jc,kcn->kjn', inverse, magnetic, precision=highest)
    induction = cross_product(phys_velocity, phys_magnetic)
    angles = (2.0 * math.pi / plane_count) * jnp.arange(plane_count, dtype=jnp.int32).astype(jnp.float32)
    rotation = jnp.stack([tilt_factor * jnp.cos(angles), -tilt_factor * jnp.sin(angles),
                          axial_factor * jnp.ones_like(angles)])[:, :, None]
    force_phys = -2.0 * cross_product(rotation, phys_velocity) - lorentz_factor * cross_product(phys_magnetic, induction)
    forcing_velocity = jnp.einsum('cj,kjn->kcn', forward, force_phys, precision=highest)
    forcing_magnetic = jnp.einsum('cj,kjn->kcn', forward, induction, precision=highest)
    return forcing_velocity, forcing_magnetic


def squared_modes(coef_count):
    mode_index = jnp.arange(coef_count, dtype=jnp.int32) // 2
    return (mode_index * mode_index).astype(jnp.float32)


def element_values(widened, connectivity):
    return jnp.take(widened, connectivity, axis=-1)


def mass_part(values, mass_blocks):
    return jnp.einsum('abe,fkcbe->fkcae', mass_blocks, values, precision=highest)


def diffusion_part(values, stiff_blocks, twist_blocks, rates, mode_square):
    stiff_terms = jnp.einsum('abe,fkcbe->fkcae', stiff_blocks, values, precision=highest)
    twist_terms = jnp.einsum('abe,fkcbe->fkcae', twist_blocks, values, precision=highest)
    return rates[:, None, None, None, :] * (stiff_terms + mode_square[None, None, :, None, None] * twist_terms)


def assemble(element_terms, connectivity, node_count):
    empty = jnp.zeros(element_terms.shape[:3] + (node_count,), jnp.float32)
    return empty.at[..., connectivity].add(element_terms, mode="drop")


def per_device(array):
    shaped = array.reshape(array.shape[:-1] + (N_MESH, array.shape[-1] // N_MESH))
    return jnp.moveaxis(shaped, -2, 0)


def whole_array(array):
    moved = jnp.moveaxis(array, 0, -2)
    return moved.reshape(moved.shape[:-2] + (moved.shape[-2] * moved.shape[-1],))


def neighbours(field_dev):
    zero_shard = jnp.zeros_like(field_dev[:1])
    lower_shards = jnp.concatenate([zero_shard, field_dev[:-1]], axis=0)
    upper_shards = jnp.concatenate([field_dev[1:], zero_shard], axis=0)
    return lower_shards, upper_shards


def widen(own_values, lower_shard, upper_shard, lists):
    return jnp.concatenate([own_values, jnp.take(lower_shard, lists[0], axis=-1),
                            jnp.take(upper_shard, lists[1], axis=-1)], axis=-1)


def reference(velocity, magnetic, mass_blocks, stiff_blocks, twist_blocks, diffusivity, connectivity, ghost_lists):
    state_now = jnp.stack([velocity, magnetic])
    forcing = jnp.stack(list(forcing_terms(velocity, magnetic)))
    rates = jnp.stack([viscosity * jnp.ones_like(diffusivity), diffusivity])
    mode_square = squared_modes(velocity.shape[1])
    mass_dev = per_device(mass_blocks)
    stiff_dev = per_device(stiff_blocks)
    twist_dev = per_device(twist_blocks)
    conn_dev = per_device(connectivity)
    rates_dev = per_device(rates)
    lists_dev = per_device(ghost_lists)
    tables = (conn_dev, mass_dev, stiff_dev, twist_dev, rates_dev, lists_dev)

    def apply_all(field_dev):
        lower_shards, upper_shards = neighbours(field_dev)

        def device_apply(items):
            own_values, lower_shard, upper_shard, conn, mass, stiff, twist, rate, lists = items
            values = element_values(widen(own_values, lower_shard, upper_shard, lists), conn)
            terms = mass_part(values, mass) / time_step + diffusion_part(values, stiff, twist, rate, mode_square)
            return assemble(terms, conn, own_values.shape[-1])

        return lax.map(device_apply, (field_dev, lower_shards, upper_shards) + tables)

    state_dev = per_device(state_now)
    forcing_dev = per_device(forcing)
    state_lower, state_upper = neighbours(state_dev)
    forcing_lower, forcing_upper = neighbours(forcing_dev)

    def device_residual(items):
        own_state, low_state, up_state, own_force, low_force, up_force, conn, mass, stiff, twist, rate, lists = items
        force_values = element_values(widen(own_force, low_force, up_force, lists), conn)
        state_values = element_values(widen(own_state, low_state, up_state, lists), conn)
        terms = mass_part(force_values, mass) - diffusion_part(state_values, stiff, twist, rate, mode_square)
        return assemble(terms, conn, own_state.shape[-1])

    residual = lax.map(device_residual, (state_dev, state_lower, state_upper,
                                         forcing_dev, forcing_lower, forcing_upper) + tables)

    def inner(first_field, second_field):
        return jnp.sum(first_field * second_field, axis=(0, 4))

    solution = state_dev
    direction = residual
    norm_now = inner(residual, residual)
    for iteration in range(ITERS):
        image = apply_all(direction)
        step_size = norm_now / (inner(direction, image) + epsilon)
        solution = solution + step_size[None, :, :, :, None] * direction
        residual = residual - step_size[None, :, :, :, None] * image
        if iteration + 1 < ITERS:
            norm_next = inner(residual, residual)
            conjugacy = norm_next / (norm_now + epsilon)
            direction = residual + conjugacy[None, :, :, :, None] * direction
            norm_now = norm_next
    result = whole_array(solution)
    return result[0], result[1]
```

```python
import functools
import math

import jax
import jax.numpy as jnp
import ml_dtypes
import numpy as np
from jax import lax
from jax.experimental import pallas as pl
from jax.experimental.pallas import tpu as pltpu
from jax.sharding import PartitionSpec as P

viscosity = 2.0
inverse_step = 10.0
tilt_factor = 0.5
axial_factor = 1.0
lorentz_factor = 0.005
epsilon = 1e-06
basis_scale = 512.0

f32 = jnp.float32
bf16 = jnp.bfloat16
VMEM = pl.BlockSpec(memory_space=pltpu.VMEM)
SMEM = pl.BlockSpec(memory_space=pltpu.SMEM)


def split_table(table):
    high = table.astype(np.float32).astype(ml_dtypes.bfloat16)
    low = (table - high.astype(np.float64)).astype(np.float32).astype(ml_dtypes.bfloat16)
    return high, low


def transform_tables(coefs):
    planes = 2 * coefs
    mode = np.arange(coefs) // 2
    turns = (np.arange(planes)[:, None] * mode[None, :]) % planes
    angles = 2.0 * math.pi / planes * turns
    inverse = np.where(np.arange(coefs)[None, :] % 2 == 0, np.cos(angles), np.sin(angles))
    weight = np.where(mode == 0, 1.0, 2.0) / planes
    to_planes = np.concatenate(split_table(inverse.T.copy()), axis=0)
    to_coefs = np.concatenate(split_table(inverse * weight[None, :]), axis=0)
    phi = 2.0 * math.pi / planes * np.arange(planes)
    rows = np.zeros((8, planes), np.float32)
    rows[0] = -2.0 * tilt_factor * np.cos(phi)
    rows[1] = 2.0 * tilt_factor * np.sin(phi)
    rows[2] = -2.0 * axial_factor
    squares = np.zeros((8, coefs), np.float32)
    squares[:] = (mode * mode).astype(np.float32)[None, :]
    return to_planes, to_coefs, rows, squares


def halves(value):
    high = value.astype(bf16)
    return high, (value - high.astype(f32)).astype(bf16)


def dot(first, second):
    return lax.dot_general(first, second, (((1,), (0,)), ((), ())), preferred_element_type=f32)


def dot_nt(first, second):
    return lax.dot_general(first, second, (((1,), (1,)), ((), ())), preferred_element_type=f32)


def stacked_columns(value):
    high, low = halves(value)
    return jnp.concatenate([high, low, high], axis=1)


def stacked_rows(value):
    high, low = halves(value)
    return jnp.concatenate([high, high, low], axis=0)


def iota(shape, dim):
    return lax.broadcasted_iota(jnp.int32, shape, dim)


def element_sides(conn, nodes, ghosts):
    own = jnp.max((conn < nodes).astype(f32), axis=0, keepdims=True)
    low = jnp.max(((conn >= nodes) & (conn < nodes + ghosts)).astype(f32), axis=0, keepdims=True)
    high = jnp.max((conn >= nodes + ghosts).astype(f32), axis=0, keepdims=True)
    return own, low, high


def pack_matrix(conn, odd, nodes, ghosts):
    _, low, high = element_sides(conn, nodes, ghosts)
    node_of_row = iota((nodes, conn.shape[1]), 0)
    flag_low = jnp.zeros((nodes, conn.shape[1]), f32)
    flag_high = jnp.zeros((nodes, conn.shape[1]), f32)
    for a in range(conn.shape[0]):
        hit = node_of_row == conn[a : a + 1, :]
        flag_low = jnp.maximum(flag_low, jnp.where(hit, low, 0.0))
        flag_high = jnp.maximum(flag_high, jnp.where(hit, high, 0.0))
    flag_low = jnp.max(flag_low, axis=1, keepdims=True)
    flag_high = jnp.max(flag_high, axis=1, keepdims=True)
    before = (iota((nodes, nodes), 1) < iota((nodes, nodes), 0)).astype(bf16)
    lane = iota((nodes, nodes), 1)
    flags = jnp.where(lane == 0, flag_low, jnp.where(lane == 1, flag_high, 0.0))
    ranks = dot(before, flags.astype(bf16))
    rank_low = jnp.sum(jnp.where(lane == 0, ranks, 0.0), axis=1, keepdims=True).astype(jnp.int32)
    rank_high = jnp.sum(jnp.where(lane == 1, ranks, 0.0), axis=1, keepdims=True).astype(jnp.int32)
    rows = iota((nodes, 2 * ghosts), 1)
    low_row = rank_low + (1 - odd) * ghosts
    high_row = rank_high + odd * ghosts
    fits_low = (flag_low > 0.0) & (rank_low < ghosts) & (rows == low_row)
    fits_high = (flag_high > 0.0) & (rank_high < ghosts) & (rows == high_row)
    return jnp.where(fits_low | fits_high, 1.0, 0.0)


def to_row(column, size):
    eye = iota((size, size), 0) == iota((size, size), 1)
    return jnp.sum(jnp.where(eye, column, 0.0), axis=0, keepdims=True)


def to_column(row, size):
    eye = iota((size, size), 0) == iota((size, size), 1)
    return jnp.sum(jnp.where(eye, row, 0.0), axis=1, keepdims=True)


def slot_matrix(conn, lists, odd, low_valid, high_valid, nodes, ghosts):
    own, _, _ = element_sides(conn, nodes, ghosts)
    slot = iota((2 * ghosts, conn.shape[1]), 0) + nodes
    active = jnp.zeros((2 * ghosts, conn.shape[1]), f32)
    for a in range(conn.shape[0]):
        active = jnp.maximum(active, jnp.where(slot == conn[a : a + 1, :], own, 0.0))
    active = jnp.max(active, axis=1, keepdims=True)
    parts = []
    for side in range(2):
        flag = active[side * ghosts : (side + 1) * ghosts]
        node_row = lists[side : side + 1, :].astype(f32)
        node_column = to_column(node_row, ghosts)
        smaller = (node_row < node_column).astype(f32) * to_row(flag, ghosts)
        rank = jnp.sum(smaller, axis=1, keepdims=True).astype(jnp.int32)
        offset = (1 - odd) * ghosts if side == 0 else odd * ghosts
        valid = low_valid if side == 0 else high_valid
        live = (flag > 0.0) & (valid > 0)
        rows = iota((ghosts, 2 * ghosts), 1)
        parts.append(jnp.where(live & (rows == rank + offset), 1.0, 0.0))
    return jnp.concatenate(parts, axis=0)


def pack_kernel(info, velocity, magnetic, conn_ref, near_ref, far_ref, state_ref):
    nodes = velocity.shape[2]
    ghosts = near_ref.shape[1]
    pick = pack_matrix(conn_ref[...], info[0], nodes, ghosts)
    pick = jnp.transpose(pick).astype(bf16)
    for k in range(6):
        source = velocity if k < 3 else magnetic
        block = jnp.transpose(source[k % 3])
        state_ref[k] = block
        first, rest = halves(block)
        second = (block - first.astype(f32) - rest.astype(f32)).astype(bf16)
        packed = dot(pick, first) + dot(pick, rest) + dot(pick, second)
        near_ref[k] = packed[:ghosts]
        far_ref[k] = packed[ghosts:]


def to_planes(high, low, table):
    coefs = high.shape[1]
    return dot(high, table[:coefs]) + dot(low, table[:coefs]) + dot(high, table[coefs:])


def to_coefs(high, low, table):
    planes = high.shape[1]
    return dot(high, table[:planes]) + dot(low, table[:planes]) + dot(high, table[planes:])


def cross(a, b):
    return [
        a[1] * b[2] - a[2] * b[1],
        a[2] * b[0] - a[0] * b[2],
        a[0] * b[1] - a[1] * b[0],
    ]


def forcing(value, rows, planes_ref, coefs_ref, rotation_ref, phys_ref, high_ref, low_ref):
    planes = planes_ref.shape[1]
    high, low = halves(value)
    phys_ref[...] = to_planes(high, low, planes_ref)
    step_rows, step_lanes = 16, 256
    for row in range(0, rows, step_rows):
        for lane in range(0, planes, step_lanes):
            lanes = pl.ds(lane, step_lanes)
            u = [phys_ref[pl.ds(k * rows + row, step_rows), lanes] for k in range(3)]
            b = [phys_ref[pl.ds((3 + k) * rows + row, step_rows), lanes] for k in range(3)]
            turn = [rotation_ref[k : k + 1, lanes] for k in range(3)]
            induction = cross(u, b)
            twisted = cross(turn, u)
            lorentz = cross(b, induction)
            force = [twisted[k] - lorentz_factor * lorentz[k] for k in range(3)]
            for k, item in enumerate(force + induction):
                item_high, item_low = halves(item)
                at = pl.ds(k * rows + row, step_rows)
                high_ref[at, lanes] = item_high
                low_ref[at, lanes] = item_low
    return to_coefs(high_ref[...], low_ref[...], coefs_ref)


def build_kernel(
    info, state, planes_ref, coefs_ref, rotation_ref, squares_ref,
    mass_ref, stiff_ref, twist_ref, rates_ref, conn_ref, lists_ref,
    own_ref, ghost_ref, back_ref, mass_ghost_ref, rest_ghost_ref, residual_ref, packed_ref,
    phys_ref, high_ref, low_ref, force_ref, z_ref,
):
    nodes = state.shape[1]
    elements = conn_ref.shape[1]
    ghosts = lists_ref.shape[1]
    width = nodes + 2 * ghosts
    conn = conn_ref[...]
    pick = jnp.transpose(pack_matrix(conn, info[0], nodes, ghosts)).astype(bf16)
    remap = slot_matrix(conn, lists_ref[...], info[0], info[1], info[2], nodes, ghosts).astype(bf16)

    node_of_row = iota((nodes, elements), 0)
    hits = [node_of_row == conn[a : a + 1, :] for a in range(6)]
    rates = rates_ref[0:1, :]
    for g, block in enumerate((mass_ref, stiff_ref, twist_ref)):
        for b in range(6):
            total = jnp.zeros((nodes, elements), f32)
            for a in range(6):
                total = total + jnp.where(hits[a], block[a, b : b + 1, :], 0.0)
            lanes = pl.ds(b * elements, elements)
            z_ref[pl.ds(g * nodes, nodes), lanes] = total
            if g > 0:
                z_ref[pl.ds((g + 2) * nodes, nodes), lanes] = total * rates
    column = jnp.concatenate(
        [(iota((width, elements), 0) == conn[b : b + 1, :]).astype(bf16) for b in range(6)], axis=1
    )
    z = z_ref[...]
    first, second = halves(z)
    third = (z - first.astype(f32) - second.astype(f32)).astype(bf16)
    dense = dot_nt(first, column) + dot_nt(second, column) + dot_nt(third, column)
    mass, stiff, twist, rate_stiff, rate_twist = [dense[g * nodes : (g + 1) * nodes] for g in range(5)]

    def picked(pair):
        return [dot(pick, item).astype(bf16) for item in pair]

    def moved(pair):
        return [dot(item[:, nodes:], remap).astype(bf16) for item in pair]

    def triple(pair):
        return jnp.concatenate([pair[0], pair[1], pair[0]], axis=1)

    def own_part(pair):
        return [item[:, :nodes] for item in pair]

    mass_pair = halves(mass)
    mass_packed = picked(mass_pair)
    mass_own = jnp.concatenate([triple(own_part(mass_pair)), triple(own_part(mass_packed))], axis=0)
    mass_ghost_ref[...] = jnp.concatenate([triple(moved(mass_pair)), triple(moved(mass_packed))], axis=0)
    rest_own = []
    for f in range(2):
        still = viscosity * stiff if f == 0 else rate_stiff
        turn = viscosity * twist if f == 0 else rate_twist
        image = (inverse_step * mass + still) * (1.0 / basis_scale)
        turn_image = turn * (1.0 / basis_scale)
        pairs = [halves(image), halves(turn_image)]
        pairs = pairs + [picked(pair) for pair in pairs]
        own_ref[f] = jnp.concatenate([triple(own_part(pair)) for pair in pairs], axis=0)
        moves = [moved(pair) for pair in pairs]
        ghost_ref[f] = jnp.concatenate([triple(pair) for pair in moves], axis=0)
        back = [
            jnp.transpose(moves[i][0].astype(f32) + moves[i][1].astype(f32)) for i in range(2)
        ]
        back_ref[f] = jnp.concatenate([stacked_columns(item) for item in back], axis=0)
        pairs = [halves(still), halves(turn)]
        pairs = pairs + [picked(pair) for pair in pairs]
        rest_own.append(jnp.concatenate([triple(own_part(pair)) for pair in pairs], axis=0))
        rest_ghost_ref[f] = jnp.concatenate([triple(moved(pair)) for pair in pairs], axis=0)

    value = state[...].reshape(6 * nodes, state.shape[2])
    force_ref[...] = forcing(
        value, nodes, planes_ref, coefs_ref, rotation_ref, phys_ref, high_ref, low_ref
    )
    square = squares_ref[0:1, :]
    for k in range(6):
        from_force = dot(mass_own, stacked_rows(force_ref[pl.ds(k * nodes, nodes), :]))
        from_state = dot(rest_own[k // 3], stacked_rows(state[k]))
        residual_ref[k] = from_force[:nodes] - (from_state[:nodes] + square * from_state[nodes : 2 * nodes])
        packed = from_state[2 * nodes :]
        packed_ref[k] = from_force[nodes:] - (packed[: 2 * ghosts] + square * packed[2 * ghosts :])


def ghost_block(info, near, far, k):
    distant = jnp.where(info[3] > 0, far[k], 0.0)
    return jnp.concatenate([near[k], distant], axis=0)


def start_kernel(
    info, near, far, packed, planes_ref, coefs_ref, rotation_ref, squares_ref, mass_ghost, rest_ghost,
    near_out, far_out, force_out, phys_ref, high_ref, low_ref,
):
    ghosts = near.shape[1]
    count = 2 * ghosts
    nodes = mass_ghost.shape[0] - count
    blocks = [ghost_block(info, near, far, k) for k in range(6)]
    value = jnp.concatenate(blocks, axis=0)
    force = forcing(value, count, planes_ref, coefs_ref, rotation_ref, phys_ref, high_ref, low_ref)
    square = squares_ref[0:1, :]
    for k in range(6):
        item = force[k * count : (k + 1) * count]
        force_out[k] = item
        from_force = dot(mass_ghost[nodes:], stacked_rows(item))
        from_state = dot(rest_ghost[k // 3, 2 * nodes :], stacked_rows(blocks[k]))
        total = packed[k] + from_force - (from_state[:count] + square * from_state[count:])
        near_out[k] = total[:ghosts]
        far_out[k] = total[ghosts:]


def apply_own(own, value, k, square, nodes, count):
    image = dot(own[k // 3], stacked_rows(value))
    full = image[:nodes] + square * image[nodes : 2 * nodes]
    packed = image[2 * nodes : 2 * nodes + count] + square * image[2 * nodes + count :]
    return full, packed


def first_kernel(
    info, near, far, force, residual, mass_ghost, rest_ghost, own, squares_ref,
    vector_out, image_out, packed_out, moments_out,
):
    nodes = residual.shape[1]
    count = force.shape[1]
    square = squares_ref[0:1, :]
    for k in range(6):
        from_force = dot(mass_ghost[:nodes], stacked_rows(force[k]))
        from_state = dot(rest_ghost[k // 3, : 2 * nodes], stacked_rows(ghost_block(info, near, far, k)))
        total = residual[k] + from_force - (from_state[:nodes] + square * from_state[nodes:])
        vector_out[k] = total
        full, packed = apply_own(own, total, k, square, nodes, count)
        image_out[k] = full
        packed_out[k] = packed
        moments_out[k : k + 1, :] = jnp.sum(total * total, axis=0, keepdims=True)
    moments_out[6:8, :] = jnp.zeros((2, moments_out.shape[1]), f32)


def send_kernel(info, near, far, packed, ghost_ops, squares_ref, near_out, far_out):
    ghosts = near.shape[1]
    count = 2 * ghosts
    top = ghost_ops.shape[1] - 2 * count
    square = squares_ref[0:1, :]
    for k in range(6):
        image = dot(ghost_ops[k // 3, top:], stacked_rows(ghost_block(info, near, far, k)))
        total = packed[k] + image[:count] + square * image[count:]
        near_out[k] = total[:ghosts]
        far_out[k] = total[ghosts:]


def next_kernel(
    info, near, far, image, before, own, ghost_ops, squares_ref,
    vector_out, image_out, packed_out, moments_out,
):
    nodes = image.shape[1]
    count = 2 * near.shape[1]
    square = squares_ref[0:1, :]
    for k in range(6):
        part = dot(ghost_ops[k // 3, : 2 * nodes], stacked_rows(ghost_block(info, near, far, k)))
        total = image[k] + part[:nodes] + square * part[nodes:]
        vector_out[k] = total
        full, packed = apply_own(own, total, k, square, nodes, count)
        image_out[k] = full
        packed_out[k] = packed
        moments_out[k : k + 1, :] = jnp.sum(before[k] * total, axis=0, keepdims=True)
        moments_out[6 + k : 7 + k, :] = jnp.sum(total * total, axis=0, keepdims=True)
    moments_out[12:16, :] = jnp.zeros((4, moments_out.shape[1]), f32)


def last_kernel(
    info, near, far, image, before, own, ghost_ops, back_ops, squares_ref,
    vector_out, back_out, moments_out,
):
    nodes = image.shape[1]
    count = 2 * near.shape[1]
    square = squares_ref[0:1, :]
    for k in range(6):
        part = dot(ghost_ops[k // 3, : 2 * nodes], stacked_rows(ghost_block(info, near, far, k)))
        total = image[k] + part[:nodes] + square * part[nodes:]
        vector_out[k] = total
        rows = stacked_rows(total)
        after = dot(own[k // 3, : 2 * nodes], rows)
        after = after[:nodes] + square * after[nodes:]
        back = dot(back_ops[k // 3], rows)
        back_out[k] = back[:count] + square * back[count:]
        moments_out[k : k + 1, :] = jnp.sum(before[k] * total, axis=0, keepdims=True)
        moments_out[6 + k : 7 + k, :] = jnp.sum(total * total, axis=0, keepdims=True)
        moments_out[12 + k : 13 + k, :] = jnp.sum(after * total, axis=0, keepdims=True)
    moments_out[18:24, :] = jnp.zeros((6, moments_out.shape[1]), f32)


def join_kernel(info, near, far, back, first, second, third, out):
    out[0:6] = first[0:6]
    out[6:18] = second[0:12]
    out[18:36] = third[0:18]
    out[36:40] = jnp.zeros((4, out.shape[1]), f32)
    for k in range(6):
        part = ghost_block(info, near, far, k) * back[k]
        out[30 + k : 31 + k, :] += jnp.sum(part, axis=0, keepdims=True)


def finish_kernel(moments, velocity, magnetic, first, second, third, velocity_out, magnetic_out):
    m0, m1, m2, m3, m4, m5 = [moments[6 * j : 6 * j + 6, :] for j in range(6)]
    scale = basis_scale
    alpha0 = m0 / (scale * m1 + epsilon)
    q1 = -alpha0 * scale
    rr1 = m0 + 2.0 * q1 * m1 + q1 * q1 * m2
    beta0 = rr1 / (m0 + epsilon)
    p0 = 1.0 + beta0
    p1 = q1
    alpha1 = rr1 / (scale * (p0 * p0 * m1 + 2.0 * p0 * p1 * m2 + p1 * p1 * m3) + epsilon)
    step1 = alpha1 * scale
    r1 = q1 - step1 * p0
    r2 = -step1 * p1
    rr2 = m0 + r1 * r1 * m2 + r2 * r2 * m4 + 2.0 * (r1 * m1 + r2 * m2 + r1 * r2 * m3)
    beta1 = rr2 / (rr1 + epsilon)
    d0 = 1.0 + beta1 * p0
    d1 = r1 + beta1 * p1
    d2 = r2
    curve = d0 * d0 * m1 + d1 * d1 * m3 + d2 * d2 * m5
    curve = curve + 2.0 * (d0 * d1 * m2 + d0 * d2 * m3 + d1 * d2 * m4)
    alpha2 = rr2 / (scale * curve + epsilon)
    c0 = alpha0 + alpha1 * p0 + alpha2 * d0
    c1 = alpha1 * p1 + alpha2 * d1
    c2 = alpha2 * d2
    for k in range(6):
        source, out = (velocity, velocity_out) if k < 3 else (magnetic, magnetic_out)
        change = (
            c0[k : k + 1, :] * first[k] + c1[k : k + 1, :] * second[k] + c2[k : k + 1, :] * third[k]
        )
        out[k % 3] = source[k % 3] + jnp.transpose(change)


def call(kernel, outs, operands, scratch=(), flops=0, limit=24):
    specs = [SMEM if operand.dtype == jnp.int32 and operand.ndim == 1 else VMEM for operand in operands]
    single = not isinstance(outs, list)
    shapes = [outs] if single else outs
    moved = sum(math.prod(o.shape) * o.dtype.itemsize for o in list(operands) + shapes)
    result = pl.pallas_call(
        kernel,
        out_shape=outs,
        in_specs=specs,
        out_specs=VMEM if single else [VMEM] * len(outs),
        scratch_shapes=list(scratch),
        compiler_params=pltpu.CompilerParams(vmem_limit_bytes=limit * 1024 * 1024),
        cost_estimate=pl.CostEstimate(flops=flops, bytes_accessed=moved, transcendentals=0),
    )(*operands)
    return result


def shape(*sizes, dtype=f32):
    return jax.ShapeDtypeStruct(sizes, dtype)


def involution(pairs):
    return [edge for a, b in pairs for edge in ((a, b), (b, a))]


def local(runs, count, velocity, magnetic, mass_blocks, stiff_blocks, twist_blocks, diffusivity, conn, lists):
    coefs, nodes = velocity.shape[1:]
    ghosts = lists.shape[1]
    elements = conn.shape[1]
    both = 2 * ghosts
    planes = 2 * coefs
    index = lax.axis_index("mesh")
    odd = index % 2
    low_valid = (index > 0).astype(jnp.int32)
    high_valid = (index < count - 1).astype(jnp.int32)
    far_valid = jnp.where(odd == 1, high_valid, low_valid)
    info = jnp.stack([odd, low_valid, high_valid, far_valid]).astype(jnp.int32)

    near_pairs = [(i, i ^ 1) for i in range(count)]
    far_pairs = []
    for run in range(runs):
        base = run * count
        far_pairs += involution([(base + i, base + i + 1) for i in range(1, count - 1, 2)])
    if runs % 2 == 0:
        for run in range(0, runs, 2):
            for end in (0, count - 1):
                far_pairs += involution([(run * count + end, (run + 1) * count + end)])

    def swap_near(value):
        return lax.ppermute(value, "mesh", near_pairs)

    def swap_far(value):
        return lax.ppermute(value, ("runs", "mesh"), far_pairs)

    def swapped(value, even_mask, odd_mask):
        pairs = [(i, i ^ (odd_mask if i % 2 else even_mask)) for i in range(count)]
        return lax.ppermute(value, "mesh", pairs)

    plane_table, coef_table, rotation, squares = transform_tables(coefs)
    plane_table, coef_table = jnp.asarray(plane_table), jnp.asarray(coef_table)
    rotation, squares = jnp.asarray(rotation), jnp.asarray(squares)
    ends = shape(6, ghosts, coefs)
    whole = shape(6, nodes, coefs)
    packs = shape(6, both, coefs)

    near, far, state = call(pack_kernel, [ends, ends, whole], [info, velocity, magnetic, conn])
    near_state, far_state = swap_near(near), swap_far(far)

    rates = jnp.broadcast_to(diffusivity[None, :], (8, elements))
    own, ghost_ops, back_ops, mass_ghost, rest_ghost, residual, packed = call(
        build_kernel,
        [
            shape(2, 2 * nodes + 2 * both, 3 * nodes, dtype=bf16),
            shape(2, 2 * nodes + 2 * both, 3 * both, dtype=bf16),
            shape(2, 2 * both, 3 * nodes, dtype=bf16),
            shape(nodes + both, 3 * both, dtype=bf16),
            shape(2, 2 * nodes + 2 * both, 3 * both, dtype=bf16),
            whole,
            packs,
        ],
        [info, state, plane_table, coef_table, rotation, squares, mass_blocks, stiff_blocks, twist_blocks, rates, conn, lists],
        scratch=[
            pltpu.VMEM((6 * nodes, planes), f32),
            pltpu.VMEM((6 * nodes, planes), bf16),
            pltpu.VMEM((6 * nodes, planes), bf16),
            pltpu.VMEM((6 * nodes, coefs), f32),
            pltpu.VMEM((5 * nodes, 6 * elements), f32),
        ],
        flops=6_000_000_000,
    )
    near, far, force = call(
        start_kernel,
        [ends, ends, packs],
        [info, near_state, far_state, packed, plane_table, coef_table, rotation, squares, mass_ghost, rest_ghost],
        scratch=[
            pltpu.VMEM((6 * both, planes), f32),
            pltpu.VMEM((6 * both, planes), bf16),
            pltpu.VMEM((6 * both, planes), bf16),
        ],
        flops=1_000_000_000,
    )
    near_now, far_now = swap_near(near), swap_far(far)
    vector0, image, packed, moments0 = call(
        first_kernel,
        [whole, whole, packs, shape(8, coefs)],
        [info, near_state, far_state, force, residual, mass_ghost, rest_ghost, own, squares],
        flops=2_000_000_000,
    )
    near, far = call(
        send_kernel, [ends, ends], [info, near_now, far_now, packed, ghost_ops, squares], flops=100_000_000
    )
    near_next, far_next = swap_near(near), swap_far(far)
    vector1, image, packed, moments1 = call(
        next_kernel,
        [whole, whole, packs, shape(16, coefs)],
        [info, near_now, far_now, image, vector0, own, ghost_ops, squares],
        flops=2_000_000_000,
    )
    near, far = call(
        send_kernel, [ends, ends], [info, near_next, far_next, packed, ghost_ops, squares], flops=100_000_000
    )
    near_last, far_last = swap_near(near), swap_far(far)
    vector2, back, moments2 = call(
        last_kernel,
        [whole, packs, shape(24, coefs)],
        [info, near_next, far_next, image, vector1, own, ghost_ops, back_ops, squares],
        flops=2_000_000_000,
    )
    moments = call(
        join_kernel, shape(40, coefs), [info, near_last, far_last, back, moments0, moments1, moments2]
    )
    if count == 16:
        total = moments + swap_near(moments)
        terms = [swapped(total, e, o) for e, o in ((4, 2), (8, 6), (12, 10), (2, 14))]
        others = jnp.where(odd == 1, terms[3], total)
        half = others + terms[0] + terms[1] + terms[2]
        total = half + swap_near(half)
    else:
        total = lax.psum(moments, "mesh")
    new_velocity, new_magnetic = call(
        finish_kernel,
        [shape(3, coefs, nodes), shape(3, coefs, nodes)],
        [total, velocity, magnetic, vector0, vector1, vector2],
        flops=10_000_000,
    )
    return new_velocity, new_magnetic


def solution(mesh):
    in_specs = (
        P("runs", None, "mesh"),
        P("runs", None, "mesh"),
        P(None, None, "mesh"),
        P(None, None, "mesh"),
        P(None, None, "mesh"),
        P(("runs", "mesh")),
        P(None, "mesh"),
        P(None, "mesh"),
    )
    out_specs = (P("runs", None, "mesh"), P("runs", None, "mesh"))
    sizes = dict(mesh.shape)
    step = functools.partial(local, sizes["runs"], sizes["mesh"])
    return jax.shard_map(step, mesh=mesh, in_specs=in_specs, out_specs=out_specs, check_vma=False)
```

```python
import functools
import math

import jax
import jax.numpy as jnp
import ml_dtypes
import numpy as np
from jax import lax
from jax.experimental import pallas as pl
from jax.experimental.pallas import tpu as pltpu
from jax.sharding import PartitionSpec as P

viscosity = 2.0
inverse_step = 10.0
tilt_factor = 0.5
axial_factor = 1.0
lorentz_factor = 0.005
epsilon = 1e-06
basis_scale = 512.0

f32 = jnp.float32
bf16 = jnp.bfloat16
VMEM = pl.BlockSpec(memory_space=pltpu.VMEM)
SMEM = pl.BlockSpec(memory_space=pltpu.SMEM)


def split_table(table):
    high = table.astype(np.float32).astype(ml_dtypes.bfloat16)
    low = (table - high.astype(np.float64)).astype(np.float32).astype(ml_dtypes.bfloat16)
    return high, low


def transform_tables(coefs):
    planes = 2 * coefs
    mode = np.arange(coefs) // 2
    turns = (np.arange(planes)[:, None] * mode[None, :]) % planes
    angles = 2.0 * math.pi / planes * turns
    inverse = np.where(np.arange(coefs)[None, :] % 2 == 0, np.cos(angles), np.sin(angles))
    weight = np.where(mode == 0, 1.0, 2.0) / planes
    to_planes = np.concatenate(split_table(inverse.T.copy()), axis=0)
    to_coefs = np.concatenate(split_table(inverse * weight[None, :]), axis=0)
    phi = 2.0 * math.pi / planes * np.arange(planes)
    rows = np.zeros((8, planes), np.float32)
    rows[0] = -2.0 * tilt_factor * np.cos(phi)
    rows[1] = 2.0 * tilt_factor * np.sin(phi)
    rows[2] = -2.0 * axial_factor
    squares = np.zeros((8, coefs), np.float32)
    squares[:] = (mode * mode).astype(np.float32)[None, :]
    return to_planes, to_coefs, rows, squares


def halves(value):
    high = value.astype(bf16)
    return high, (value - high.astype(f32)).astype(bf16)


def dot(first, second):
    return lax.dot_general(first, second, (((1,), (0,)), ((), ())), preferred_element_type=f32)


def dot_nt(first, second):
    return lax.dot_general(first, second, (((1,), (1,)), ((), ())), preferred_element_type=f32)


def stacked_columns(value):
    high, low = halves(value)
    return jnp.concatenate([high, low, high], axis=1)


def stacked_rows(value):
    high, low = halves(value)
    return jnp.concatenate([high, high, low], axis=0)


def iota(shape, dim):
    return lax.broadcasted_iota(jnp.int32, shape, dim)


def one_hot(conn, first, count):
    row = iota((count, conn.shape[1]), 0) + first
    return jnp.concatenate([(row == conn[a : a + 1, :]).astype(bf16) for a in range(6)], axis=1)


def element_sides(conn, nodes, ghosts):
    own = jnp.max((conn < nodes).astype(f32), axis=0, keepdims=True)
    low = jnp.max(((conn >= nodes) & (conn < nodes + ghosts)).astype(f32), axis=0, keepdims=True)
    high = jnp.max((conn >= nodes + ghosts).astype(f32), axis=0, keepdims=True)
    return own, low, high


def eight_rows(items):
    row = iota((8, items[0].shape[1]), 0)
    total = jnp.zeros(row.shape, f32)
    for i, item in enumerate(items):
        total = jnp.where(row == i, item, total)
    return total


def pack_matrix(conn, odd, nodes, ghosts):
    _, low, high = element_sides(conn, nodes, ghosts)
    sides = eight_rows([low, high]).astype(bf16)
    sides = jnp.concatenate([sides] * 6, axis=1)
    named = dot_nt(sides, one_hot(conn, 0, nodes))
    flags = jnp.where(named > 0.0, 1.0, 0.0)
    before = (iota((nodes, nodes), 0) < iota((nodes, nodes), 1)).astype(bf16)
    ranks = dot(flags.astype(bf16), before).astype(jnp.int32)
    rows = iota((2 * ghosts, nodes), 0)
    picks = []
    for side in range(2):
        offset = (1 - odd) * ghosts if side == 0 else odd * ghosts
        rank = ranks[side : side + 1, :]
        rank = jnp.where((flags[side : side + 1, :] > 0.0) & (rank < ghosts), rank + offset, -1)
        picks.append(rows == rank)
    return jnp.where(picks[0] | picks[1], 1.0, 0.0).astype(bf16)


def slot_matrix(conn, lists, odd, low_valid, high_valid, nodes, ghosts):
    own, _, _ = element_sides(conn, nodes, ghosts)
    owns = jnp.concatenate([eight_rows([own]).astype(bf16)] * 6, axis=1)
    slots = one_hot(conn, nodes, 2 * ghosts)
    active_rows = jnp.where(dot_nt(owns, slots) > 0.0, 1.0, 0.0)
    active_columns = jnp.where(dot_nt(slots, owns) > 0.0, 1.0, 0.0)
    numbers = eight_rows([lists[0:1, :].astype(f32), lists[1:2, :].astype(f32)]).astype(bf16)
    eye = (iota((ghosts, ghosts), 0) == iota((ghosts, ghosts), 1)).astype(bf16)
    columns = dot_nt(eye, numbers)
    parts = []
    for side in range(2):
        span = slice(side * ghosts, (side + 1) * ghosts)
        smaller = (lists[side : side + 1, :].astype(f32) < columns[:, side : side + 1]).astype(bf16)
        rank = dot_nt(smaller, active_rows[:, span].astype(bf16))[:, 0:1].astype(jnp.int32)
        offset = (1 - odd) * ghosts if side == 0 else odd * ghosts
        valid = low_valid if side == 0 else high_valid
        live = (active_columns[span, 0:1] > 0.0) & (valid > 0)
        rows = iota((ghosts, 2 * ghosts), 1)
        parts.append(jnp.where(live & (rows == rank + offset), 1.0, 0.0))
    return jnp.concatenate(parts, axis=0).astype(bf16)


def pack_kernel(
    info, velocity, magnetic, conn_ref, near_ref, far_ref, state_ref, pick_ref, values, arrived
):
    nodes = velocity.shape[2]
    ghosts = near_ref.shape[1]
    copies = []
    for k in range(6):
        source = velocity if k < 3 else magnetic
        copy = pltpu.make_async_copy(source.at[k % 3], values.at[k], arrived.at[k])
        copy.start()
        copies.append(copy)
    pick = pack_matrix(conn_ref[...], info[0], nodes, ghosts)
    pick_ref[...] = pick
    for k in range(6):
        copies[k].wait()
        block = jnp.transpose(values[k])
        state_ref[k] = block
        first, rest = halves(block)
        second = (block - first.astype(f32) - rest.astype(f32)).astype(bf16)
        packed = dot(pick, first) + dot(pick, rest) + dot(pick, second)
        near_ref[k] = packed[:ghosts]
        far_ref[k] = packed[ghosts:]


def to_planes(high, low, table):
    coefs = high.shape[1]
    return dot(high, table[:coefs]) + dot(low, table[:coefs]) + dot(high, table[coefs:])


def to_coefs(high, low, table):
    planes = high.shape[1]
    return dot(high, table[:planes]) + dot(low, table[:planes]) + dot(high, table[planes:])


def cross(a, b):
    return [
        a[1] * b[2] - a[2] * b[1],
        a[2] * b[0] - a[0] * b[2],
        a[0] * b[1] - a[1] * b[0],
    ]


def forcing(value, rows, planes_ref, coefs_ref, rotation_ref, phys_ref, high_ref, low_ref):
    planes = planes_ref.shape[1]
    high, low = halves(value)
    phys_ref[...] = to_planes(high, low, planes_ref)
    step_rows, step_lanes = 16, 256
    for row in range(0, rows, step_rows):
        for lane in range(0, planes, step_lanes):
            lanes = pl.ds(lane, step_lanes)
            u = [phys_ref[pl.ds(k * rows + row, step_rows), lanes] for k in range(3)]
            b = [phys_ref[pl.ds((3 + k) * rows + row, step_rows), lanes] for k in range(3)]
            turn = [rotation_ref[k : k + 1, lanes] for k in range(3)]
            induction = cross(u, b)
            twisted = cross(turn, u)
            lorentz = cross(b, induction)
            force = [twisted[k] - lorentz_factor * lorentz[k] for k in range(3)]
            for k, item in enumerate(force + induction):
                item_high, item_low = halves(item)
                at = pl.ds(k * rows + row, step_rows)
                high_ref[at, lanes] = item_high
                low_ref[at, lanes] = item_low
    return to_coefs(high_ref[...], low_ref[...], coefs_ref)


def triple(pair):
    return jnp.concatenate([pair[0], pair[1], pair[0]], axis=1)


def build_kernel(
    info, state, pick_ref, planes_hbm, coefs_hbm, rotation_ref, squares_ref,
    mass_ref, stiff_ref, twist_ref, rates_ref, conn_ref, lists_ref,
    dense_ref, force_ref, mass_ghost_ref, rest_ghost_ref, packed_ref,
    planes_ref, coefs_ref, phys_ref, high_ref, low_ref, z_ref, arrived,
):
    nodes = state.shape[1]
    elements = conn_ref.shape[1]
    ghosts = lists_ref.shape[1]
    count = 2 * ghosts
    tables = [
        pltpu.make_async_copy(planes_hbm, planes_ref, arrived.at[0]),
        pltpu.make_async_copy(coefs_hbm, coefs_ref, arrived.at[1]),
    ]
    for copy in tables:
        copy.start()
    conn = conn_ref[...]
    pick = pick_ref[...]
    remap = slot_matrix(conn, lists_ref[...], info[0], info[1], info[2], nodes, ghosts)
    rates = rates_ref[0:1, :]
    step = 16
    for row in range(0, nodes, step):
        number = iota((step, elements), 0) + row
        hits = [(number == conn[a : a + 1, :]).astype(f32) for a in range(6)]
        for g, block in enumerate((mass_ref, stiff_ref, twist_ref)):
            for b in range(6):
                total = hits[0] * block[0, b : b + 1, :]
                for a in range(1, 6):
                    total = total + hits[a] * block[a, b : b + 1, :]
                lanes = pl.ds(b * elements, elements)
                z_ref[pl.ds(g * nodes + row, step), lanes] = total
                if g > 0:
                    z_ref[pl.ds((g + 2) * nodes + row, step), lanes] = total * rates
    arrives = lax.dot_general(
        remap, one_hot(conn, nodes, count), (((0,), (0,)), ((), ())), preferred_element_type=f32
    )
    column = jnp.concatenate([one_hot(conn, 0, nodes), arrives.astype(bf16)], axis=0)
    z = z_ref[...]
    first, second = halves(z)
    third = (z - first.astype(f32) - second.astype(f32)).astype(bf16)
    dense = dot_nt(first, column) + dot_nt(second, column) + dot_nt(third, column)
    dense_ref[...] = dense
    high, low = halves(dense)
    pairs = []
    for g in range(5):
        rows = slice(g * nodes, (g + 1) * nodes)
        factor = viscosity if g in (1, 2) else 1.0
        pairs.append([(factor * dot(pick, item[rows])).astype(bf16) for item in (high, low)])

    def own_part(pair):
        return triple([item[:, :nodes] for item in pair])

    def ghost_part(pair):
        return triple([item[:, nodes:] for item in pair])

    mass_own = own_part(pairs[0])
    mass_ghost_ref[...] = ghost_part(pairs[0])
    rest_own = []
    for f in range(2):
        used = (pairs[1], pairs[2]) if f == 0 else (pairs[3], pairs[4])
        rest_own.append(jnp.concatenate([own_part(pair) for pair in used], axis=0))
        rest_ghost_ref[f] = jnp.concatenate([ghost_part(pair) for pair in used], axis=0)

    for copy in tables:
        copy.wait()
    value = state[...].reshape(6 * nodes, state.shape[2])
    force_ref[...] = forcing(
        value, nodes, planes_ref, coefs_ref, rotation_ref, phys_ref, high_ref, low_ref
    ).reshape(force_ref.shape)
    square = squares_ref[0:1, :]
    for k in range(6):
        from_force = dot(mass_own, stacked_rows(force_ref[k]))
        from_state = dot(rest_own[k // 3], stacked_rows(state[k]))
        packed_ref[k] = from_force - (from_state[:count] + square * from_state[count:])


def ghost_block(info, near, far, k):
    distant = jnp.where(info[3] > 0, far[k], 0.0)
    return jnp.concatenate([near[k], distant], axis=0)


def start_kernel(
    info, near, far, packed, planes_ref, coefs_ref, rotation_ref, squares_ref, mass_ghost, rest_ghost,
    near_out, far_out, force_out, phys_ref, high_ref, low_ref,
):
    ghosts = near.shape[1]
    count = 2 * ghosts
    blocks = [ghost_block(info, near, far, k) for k in range(6)]
    value = jnp.concatenate(blocks, axis=0)
    force = forcing(value, count, planes_ref, coefs_ref, rotation_ref, phys_ref, high_ref, low_ref)
    square = squares_ref[0:1, :]
    for k in range(6):
        item = force[k * count : (k + 1) * count]
        force_out[k] = item
        from_force = dot(mass_ghost[...], stacked_rows(item))
        from_state = dot(rest_ghost[k // 3], stacked_rows(blocks[k]))
        total = packed[k] + from_force - (from_state[:count] + square * from_state[count:])
        near_out[k] = total[:ghosts]
        far_out[k] = total[ghosts:]


def apply_own(own, value, k, square, nodes, count):
    image = dot(own[k // 3], stacked_rows(value))
    full = image[:nodes] + square * image[nodes : 2 * nodes]
    packed = image[2 * nodes : 2 * nodes + count] + square * image[2 * nodes + count :]
    return full, packed


def first_kernel(
    info, near, far, force_ghost, force, state, dense_ref, pick_ref, squares_ref,
    own_ref, ghost_ref, back_ref, vector_out, image_out, packed_out, moments_out,
):
    nodes = state.shape[1]
    count = force_ghost.shape[1]
    square = squares_ref[0:1, :]
    pick = pick_ref[...]
    mass, stiff, twist, rate_stiff, rate_twist = [
        dense_ref[pl.ds(g * nodes, nodes), :] for g in range(5)
    ]
    mass_op = stacked_columns(mass)
    rest_ops = []
    for f in range(2):
        still = viscosity * stiff if f == 0 else rate_stiff
        turn = viscosity * twist if f == 0 else rate_twist
        rest_ops.append(jnp.concatenate([stacked_columns(still), stacked_columns(turn)], axis=0))
        image = (inverse_step * mass + still) * (1.0 / basis_scale)
        turn = turn * (1.0 / basis_scale)
        pairs = [halves(image), halves(turn)]
        pairs = pairs + [[dot(pick, item).astype(bf16) for item in pair] for pair in pairs]
        own_ref[f] = jnp.concatenate(
            [triple([item[:, :nodes] for item in pair]) for pair in pairs], axis=0
        )
        ghost_ref[f] = jnp.concatenate(
            [triple([item[:, nodes:] for item in pair]) for pair in pairs], axis=0
        )
        back = [jnp.transpose(item[:, nodes:]) for item in (image, turn)]
        back_ref[f] = jnp.concatenate([stacked_columns(item) for item in back], axis=0)
    for k in range(6):
        wide_force = jnp.concatenate([force[k], force_ghost[k]], axis=0)
        wide_state = jnp.concatenate([state[k], ghost_block(info, near, far, k)], axis=0)
        from_force = dot(mass_op, stacked_rows(wide_force))
        from_state = dot(rest_ops[k // 3], stacked_rows(wide_state))
        total = from_force - (from_state[:nodes] + square * from_state[nodes:])
        vector_out[k] = total
        full, packed = apply_own(own_ref, total, k, square, nodes, count)
        image_out[k] = full
        packed_out[k] = packed
        moments_out[k : k + 1, :] = jnp.sum(total * total, axis=0, keepdims=True)
    moments_out[6:8, :] = jnp.zeros((2, moments_out.shape[1]), f32)


def send_kernel(info, near, far, packed, ghost_ops, squares_ref, near_out, far_out):
    ghosts = near.shape[1]
    count = 2 * ghosts
    top = ghost_ops.shape[1] - 2 * count
    square = squares_ref[0:1, :]
    for k in range(6):
        image = dot(ghost_ops[k // 3, top:], stacked_rows(ghost_block(info, near, far, k)))
        total = packed[k] + image[:count] + square * image[count:]
        near_out[k] = total[:ghosts]
        far_out[k] = total[ghosts:]


def next_kernel(
    info, near, far, image, before, own, ghost_ops, squares_ref,
    vector_out, image_out, packed_out, moments_out,
):
    nodes = image.shape[1]
    count = 2 * near.shape[1]
    square = squares_ref[0:1, :]
    for k in range(6):
        part = dot(ghost_ops[k // 3, : 2 * nodes], stacked_rows(ghost_block(info, near, far, k)))
        total = image[k] + part[:nodes] + square * part[nodes:]
        vector_out[k] = total
        full, packed = apply_own(own, total, k, square, nodes, count)
        image_out[k] = full
        packed_out[k] = packed
        moments_out[k : k + 1, :] = jnp.sum(before[k] * total, axis=0, keepdims=True)
        moments_out[6 + k : 7 + k, :] = jnp.sum(total * total, axis=0, keepdims=True)
    moments_out[12:16, :] = jnp.zeros((4, moments_out.shape[1]), f32)


def last_kernel(
    info, near, far, near_last, image, before, own, ghost_ops, back_ops, squares_ref, first, second,
    vector_out, back_out, moments_out,
):
    nodes = image.shape[1]
    ghosts = near.shape[1]
    count = 2 * ghosts
    square = squares_ref[0:1, :]
    moments_out[0:6] = first[0:6]
    moments_out[6:18] = second[0:12]
    for k in range(6):
        part = dot(ghost_ops[k // 3, : 2 * nodes], stacked_rows(ghost_block(info, near, far, k)))
        total = image[k] + part[:nodes] + square * part[nodes:]
        vector_out[k] = total
        rows = stacked_rows(total)
        after = dot(own[k // 3, : 2 * nodes], rows)
        after = after[:nodes] + square * after[nodes:]
        back = dot(back_ops[k // 3], rows)
        back = back[:count] + square * back[count:]
        back_out[k] = back[ghosts:]
        moments_out[18 + k : 19 + k, :] = jnp.sum(before[k] * total, axis=0, keepdims=True)
        moments_out[24 + k : 25 + k, :] = jnp.sum(total * total, axis=0, keepdims=True)
        moments_out[30 + k : 31 + k, :] = jnp.sum(after * total, axis=0, keepdims=True) + jnp.sum(
            near_last[k] * back[:ghosts], axis=0, keepdims=True
        )
    moments_out[36:40, :] = jnp.zeros((4, moments_out.shape[1]), f32)


def join_kernel(weight, info, far, back, moments, *rest):
    out = rest[-1]
    total = moments[...]
    for other in rest[:-1]:
        total = total + other[...]
    out[...] = total
    for k in range(6):
        distant = jnp.where(info[3] > 0, far[k], 0.0)
        out[30 + k : 31 + k, :] += weight * jnp.sum(distant * back[k], axis=0, keepdims=True)


def finish_kernel(moments, other, velocity, magnetic, first, second, third, velocity_out, magnetic_out):
    total = moments[...] + other[...]
    m0, m1, m2, m3, m4, m5 = [total[6 * j : 6 * j + 6, :] for j in range(6)]
    scale = basis_scale
    alpha0 = m0 / (scale * m1 + epsilon)
    q1 = -alpha0 * scale
    rr1 = m0 + 2.0 * q1 * m1 + q1 * q1 * m2
    beta0 = rr1 / (m0 + epsilon)
    p0 = 1.0 + beta0
    p1 = q1
    alpha1 = rr1 / (scale * (p0 * p0 * m1 + 2.0 * p0 * p1 * m2 + p1 * p1 * m3) + epsilon)
    step1 = alpha1 * scale
    r1 = q1 - step1 * p0
    r2 = -step1 * p1
    rr2 = m0 + r1 * r1 * m2 + r2 * r2 * m4 + 2.0 * (r1 * m1 + r2 * m2 + r1 * r2 * m3)
    beta1 = rr2 / (rr1 + epsilon)
    d0 = 1.0 + beta1 * p0
    d1 = r1 + beta1 * p1
    d2 = r2
    curve = d0 * d0 * m1 + d1 * d1 * m3 + d2 * d2 * m5
    curve = curve + 2.0 * (d0 * d1 * m2 + d0 * d2 * m3 + d1 * d2 * m4)
    alpha2 = rr2 / (scale * curve + epsilon)
    c0 = alpha0 + alpha1 * p0 + alpha2 * d0
    c1 = alpha1 * p1 + alpha2 * d1
    c2 = alpha2 * d2
    for k in range(6):
        source, out = (velocity, velocity_out) if k < 3 else (magnetic, magnetic_out)
        change = (
            c0[k : k + 1, :] * first[k] + c1[k : k + 1, :] * second[k] + c2[k : k + 1, :] * third[k]
        )
        out[k % 3] = source[k % 3] + jnp.transpose(change)


def call(kernel, outs, operands, scratch=(), flops=0, limit=24, distant=()):
    specs = [SMEM if operand.dtype == jnp.int32 and operand.ndim == 1 else VMEM for operand in operands]
    for i in distant:
        specs[i] = pl.BlockSpec(memory_space=pl.ANY)
    single = not isinstance(outs, list)
    shapes = [outs] if single else outs
    moved = sum(math.prod(o.shape) * o.dtype.itemsize for o in list(operands) + shapes)
    return pl.pallas_call(
        kernel,
        out_shape=outs,
        in_specs=specs,
        out_specs=VMEM if single else [VMEM] * len(outs),
        scratch_shapes=list(scratch),
        compiler_params=pltpu.CompilerParams(vmem_limit_bytes=limit * 1024 * 1024),
        cost_estimate=pl.CostEstimate(flops=flops, bytes_accessed=moved, transcendentals=0),
    )(*operands)


def shape(*sizes, dtype=f32):
    return jax.ShapeDtypeStruct(sizes, dtype)


def involution(pairs):
    return [edge for a, b in pairs for edge in ((a, b), (b, a))]


def local(runs, count, velocity, magnetic, mass_blocks, stiff_blocks, twist_blocks, diffusivity, conn, lists):
    coefs, nodes = velocity.shape[1:]
    ghosts = lists.shape[1]
    elements = conn.shape[1]
    both = 2 * ghosts
    planes = 2 * coefs
    index = lax.axis_index("mesh")
    odd = index % 2
    low_valid = (index > 0).astype(jnp.int32)
    high_valid = (index < count - 1).astype(jnp.int32)
    far_valid = jnp.where(odd == 1, high_valid, low_valid)
    info = jnp.stack([odd, low_valid, high_valid, far_valid]).astype(jnp.int32)

    near_pairs = [(i, i ^ 1) for i in range(count)]
    far_pairs = []
    for run in range(runs):
        base = run * count
        far_pairs += involution([(base + i, base + i + 1) for i in range(1, count - 1, 2)])
    if runs % 2 == 0:
        for run in range(0, runs, 2):
            for end in (0, count - 1):
                far_pairs += involution([(run * count + end, (run + 1) * count + end)])

    def swap_near(value):
        return lax.ppermute(value, "mesh", near_pairs)

    def swap_far(value):
        return lax.ppermute(value, ("runs", "mesh"), far_pairs)

    plane_table, coef_table, rotation, squares = transform_tables(coefs)
    plane_table, coef_table = jnp.asarray(plane_table), jnp.asarray(coef_table)
    rotation, squares = jnp.asarray(rotation), jnp.asarray(squares)
    ends = shape(6, ghosts, coefs)
    whole = shape(6, nodes, coefs)
    packs = shape(6, both, coefs)

    def exchange(near, far):
        far = swap_far(far)
        return swap_near(near), far

    near, far, state, pick = call(
        pack_kernel,
        [ends, ends, whole, shape(both, nodes, dtype=bf16)],
        [info, velocity, magnetic, conn],
        scratch=[pltpu.VMEM((6, coefs, nodes), f32), pltpu.SemaphoreType.DMA((6,))],
        distant=(1, 2),
    )
    near_state, far_state = exchange(near, far)
    dense, force, mass_ghost, rest_ghost, packed = call(
        build_kernel,
        [
            shape(5 * nodes, nodes + both),
            whole,
            shape(both, 3 * both, dtype=bf16),
            shape(2, 2 * both, 3 * both, dtype=bf16),
            packs,
        ],
        [info, state, pick, plane_table, coef_table, rotation, squares]
        + [mass_blocks, stiff_blocks, twist_blocks, diffusivity.reshape(1, elements), conn, lists],
        scratch=[
            pltpu.VMEM(plane_table.shape, bf16),
            pltpu.VMEM(coef_table.shape, bf16),
            pltpu.VMEM((6 * nodes, planes), f32),
            pltpu.VMEM((6 * nodes, planes), bf16),
            pltpu.VMEM((6 * nodes, planes), bf16),
            pltpu.VMEM((5 * nodes, 6 * elements), f32),
            pltpu.SemaphoreType.DMA((2,)),
        ],
        flops=6_000_000_000,
        distant=(3, 4),
    )
    near, far, force_ghost = call(
        start_kernel,
        [ends, ends, packs],
        [info, near_state, far_state, packed, plane_table, coef_table, rotation, squares]
        + [mass_ghost, rest_ghost],
        scratch=[
            pltpu.VMEM((6 * both, planes), f32),
            pltpu.VMEM((6 * both, planes), bf16),
            pltpu.VMEM((6 * both, planes), bf16),
        ],
        flops=1_000_000_000,
    )
    near_now, far_now = exchange(near, far)
    own, ghost_ops, back_ops, vector0, image, packed, moments0 = call(
        first_kernel,
        [
            shape(2, 2 * nodes + 2 * both, 3 * nodes, dtype=bf16),
            shape(2, 2 * nodes + 2 * both, 3 * both, dtype=bf16),
            shape(2, 2 * both, 3 * nodes, dtype=bf16),
            whole,
            whole,
            packs,
            shape(8, coefs),
        ],
        [info, near_state, far_state, force_ghost, force, state, dense, pick, squares],
        flops=2_000_000_000,
    )
    near, far = call(
        send_kernel, [ends, ends], [info, near_now, far_now, packed, ghost_ops, squares], flops=100_000_000
    )
    near_next, far_next = exchange(near, far)
    vector1, image, packed, moments1 = call(
        next_kernel,
        [whole, whole, packs, shape(16, coefs)],
        [info, near_now, far_now, image, vector0, own, ghost_ops, squares],
        flops=2_000_000_000,
    )
    near, far = call(
        send_kernel, [ends, ends], [info, near_next, far_next, packed, ghost_ops, squares], flops=100_000_000
    )
    near_last, far_last = exchange(near, far)
    vector2, back, moments = call(
        last_kernel,
        [whole, ends, shape(40, coefs)],
        [info, near_next, far_next, near_last, image, vector1, own, ghost_ops, back_ops, squares]
        + [moments0, moments1],
        flops=2_000_000_000,
    )
    if count % 8 == 0 and count <= 16:
        joined = call(
            functools.partial(join_kernel, 2.0),
            shape(40, coefs),
            [info, far_last, back, moments, swap_near(moments)],
        )
        target = (2, 0, 3, 1)
        lines = count // 4
        half = None
        for step in range(lines):
            pairs = [(i, ((i // 4) ^ step) * 4 + target[i % 4]) for i in range(count)]
            term = lax.ppermute(joined, "mesh", pairs)
            half = term if half is None else half + term
        other = swap_near(half)
    else:
        joined = call(
            functools.partial(join_kernel, 1.0), shape(40, coefs), [info, far_last, back, moments]
        )
        half = lax.psum(joined, "mesh")
        other = jnp.zeros_like(half)
    new_velocity, new_magnetic = call(
        finish_kernel,
        [shape(3, coefs, nodes), shape(3, coefs, nodes)],
        [half, other, velocity, magnetic, vector0, vector1, vector2],
        flops=10_000_000,
    )
    return new_velocity, new_magnetic


def solution(mesh):
    in_specs = (
        P("runs", None, "mesh"),
        P("runs", None, "mesh"),
        P(None, None, "mesh"),
        P(None, None, "mesh"),
        P(None, None, "mesh"),
        P(("runs", "mesh")),
        P(None, "mesh"),
        P(None, "mesh"),
    )
    out_specs = (P("runs", None, "mesh"), P("runs", None, "mesh"))
    sizes = dict(mesh.shape)
    step = functools.partial(local, sizes["runs"], sizes["mesh"])
    return jax.shard_map(step, mesh=mesh, in_specs=in_specs, out_specs=out_specs, check_vma=False)
```

```python
import functools
import math

import jax
import jax.numpy as jnp
import ml_dtypes
import numpy as np
from jax import lax
from jax.experimental import pallas as pl
from jax.experimental.pallas import tpu as pltpu
from jax.sharding import PartitionSpec as P

viscosity = 2.0
inverse_step = 10.0
tilt_factor = 0.5
axial_factor = 1.0
lorentz_factor = 0.005
epsilon = 1e-06
basis_scale = 512.0

f32 = jnp.float32
bf16 = jnp.bfloat16
VMEM = pl.BlockSpec(memory_space=pltpu.VMEM)
SMEM = pl.BlockSpec(memory_space=pltpu.SMEM)


def split_table(table):
    high = table.astype(np.float32).astype(ml_dtypes.bfloat16)
    low = (table - high.astype(np.float64)).astype(np.float32).astype(ml_dtypes.bfloat16)
    return high, low


def transform_tables(coefs):
    planes = 2 * coefs
    mode = np.arange(coefs) // 2
    turns = (np.arange(planes)[:, None] * mode[None, :]) % planes
    angles = 2.0 * math.pi / planes * turns
    inverse = np.where(np.arange(coefs)[None, :] % 2 == 0, np.cos(angles), np.sin(angles))
    weight = np.where(mode == 0, 1.0, 2.0) / planes
    to_planes = np.concatenate(split_table(inverse.T.copy()), axis=0)
    to_coefs = np.concatenate(split_table(inverse * weight[None, :]), axis=0)
    phi = 2.0 * math.pi / planes * np.arange(planes)
    rows = np.zeros((8, planes), np.float32)
    rows[0] = -2.0 * tilt_factor * np.cos(phi)
    rows[1] = 2.0 * tilt_factor * np.sin(phi)
    rows[2] = -2.0 * axial_factor
    squares = np.zeros((8, coefs), np.float32)
    squares[:] = (mode * mode).astype(np.float32)[None, :]
    return to_planes, to_coefs, rows, squares


def halves(value):
    high = value.astype(bf16)
    return high, (value - high.astype(f32)).astype(bf16)


def dot(first, second):
    return lax.dot_general(first, second, (((1,), (0,)), ((), ())), preferred_element_type=f32)


def dot_nt(first, second):
    return lax.dot_general(first, second, (((1,), (1,)), ((), ())), preferred_element_type=f32)


def stacked_columns(value):
    high, low = halves(value)
    return jnp.concatenate([high, low, high], axis=1)


def stacked_rows(value):
    high, low = halves(value)
    return jnp.concatenate([high, high, low], axis=0)


def iota(shape, dim):
    return lax.broadcasted_iota(jnp.int32, shape, dim)


def one_hot(conn, first, count):
    row = iota((count, conn.shape[1]), 0) + first
    return jnp.concatenate([(row == conn[a : a + 1, :]).astype(bf16) for a in range(6)], axis=1)


def element_sides(conn, nodes, ghosts):
    own = jnp.max((conn < nodes).astype(f32), axis=0, keepdims=True)
    low = jnp.max(((conn >= nodes) & (conn < nodes + ghosts)).astype(f32), axis=0, keepdims=True)
    high = jnp.max((conn >= nodes + ghosts).astype(f32), axis=0, keepdims=True)
    return own, low, high


def eight_rows(items):
    row = iota((8, items[0].shape[1]), 0)
    total = jnp.zeros(row.shape, f32)
    for i, item in enumerate(items):
        total = jnp.where(row == i, item, total)
    return total


def pack_matrix(conn, odd, nodes, ghosts):
    _, low, high = element_sides(conn, nodes, ghosts)
    sides = eight_rows([low, high]).astype(bf16)
    sides = jnp.concatenate([sides] * 6, axis=1)
    named = dot_nt(sides, one_hot(conn, 0, nodes))
    flags = jnp.where(named > 0.0, 1.0, 0.0)
    before = (iota((nodes, nodes), 0) < iota((nodes, nodes), 1)).astype(bf16)
    ranks = dot(flags.astype(bf16), before).astype(jnp.int32)
    rows = iota((2 * ghosts, nodes), 0)
    picks = []
    for side in range(2):
        offset = (1 - odd) * ghosts if side == 0 else odd * ghosts
        rank = ranks[side : side + 1, :]
        rank = jnp.where((flags[side : side + 1, :] > 0.0) & (rank < ghosts), rank + offset, -1)
        picks.append(rows == rank)
    return jnp.where(picks[0] | picks[1], 1.0, 0.0).astype(bf16)


def to_row(column, size):
    eye = iota((size, size), 0) == iota((size, size), 1)
    return jnp.sum(jnp.where(eye, column, 0.0), axis=0, keepdims=True)


def to_column(row, size):
    eye = iota((size, size), 0) == iota((size, size), 1)
    return jnp.sum(jnp.where(eye, row, 0.0), axis=1, keepdims=True)


def slot_matrix(conn, lists, odd, low_valid, high_valid, nodes, ghosts):
    own, _, _ = element_sides(conn, nodes, ghosts)
    slot = iota((2 * ghosts, conn.shape[1]), 0) + nodes
    active = jnp.zeros((2 * ghosts, conn.shape[1]), f32)
    for a in range(conn.shape[0]):
        active = jnp.maximum(active, jnp.where(slot == conn[a : a + 1, :], own, 0.0))
    active = jnp.max(active, axis=1, keepdims=True)
    parts = []
    for side in range(2):
        flag = active[side * ghosts : (side + 1) * ghosts]
        node_row = lists[side : side + 1, :].astype(f32)
        node_column = to_column(node_row, ghosts)
        smaller = (node_row < node_column).astype(f32) * to_row(flag, ghosts)
        rank = jnp.sum(smaller, axis=1, keepdims=True).astype(jnp.int32)
        offset = (1 - odd) * ghosts if side == 0 else odd * ghosts
        valid = low_valid if side == 0 else high_valid
        live = (flag > 0.0) & (valid > 0)
        rows = iota((ghosts, 2 * ghosts), 1)
        parts.append(jnp.where(live & (rows == rank + offset), 1.0, 0.0))
    return jnp.concatenate(parts, axis=0).astype(bf16)


def pack_field(field, at, pick, near_ref, far_ref, state_ref):
    ghosts = near_ref.shape[1]
    for k in range(3):
        block = jnp.transpose(field[k])
        state_ref[at + k] = block
        first, rest = halves(block)
        second = (block - first.astype(f32) - rest.astype(f32)).astype(bf16)
        packed = dot(pick, first) + dot(pick, rest) + dot(pick, second)
        near_ref[at + k] = packed[:ghosts]
        far_ref[at + k] = packed[ghosts:]


def pack_velocity_kernel(info, velocity, conn_ref, near_ref, far_ref, state_ref, pick_ref):
    pick = pack_matrix(conn_ref[...], info[0], velocity.shape[2], near_ref.shape[1])
    pick_ref[...] = pick
    pack_field(velocity, 0, pick, near_ref, far_ref, state_ref)


def pack_magnetic_kernel(
    magnetic, pick_ref, near_in, far_in, state_in, near_ref, far_ref, state_ref
):
    pack_field(magnetic, 3, pick_ref[...], near_ref, far_ref, state_ref)


def to_planes(high, low, table):
    coefs = high.shape[1]
    return dot(high, table[:coefs]) + dot(low, table[:coefs]) + dot(high, table[coefs:])


def to_coefs(high, low, table):
    planes = high.shape[1]
    return dot(high, table[:planes]) + dot(low, table[:planes]) + dot(high, table[planes:])


def cross(a, b):
    return [
        a[1] * b[2] - a[2] * b[1],
        a[2] * b[0] - a[0] * b[2],
        a[0] * b[1] - a[1] * b[0],
    ]


def forcing(value, rows, planes_ref, coefs_ref, rotation_ref, phys_ref, high_ref, low_ref):
    planes = planes_ref.shape[1]
    high, low = halves(value)
    phys_ref[...] = to_planes(high, low, planes_ref)
    step_rows, step_lanes = 16, 256
    for row in range(0, rows, step_rows):
        for lane in range(0, planes, step_lanes):
            lanes = pl.ds(lane, step_lanes)
            u = [phys_ref[pl.ds(k * rows + row, step_rows), lanes] for k in range(3)]
            b = [phys_ref[pl.ds((3 + k) * rows + row, step_rows), lanes] for k in range(3)]
            turn = [rotation_ref[k : k + 1, lanes] for k in range(3)]
            induction = cross(u, b)
            twisted = cross(turn, u)
            lorentz = cross(b, induction)
            force = [twisted[k] - lorentz_factor * lorentz[k] for k in range(3)]
            for k, item in enumerate(force + induction):
                item_high, item_low = halves(item)
                at = pl.ds(k * rows + row, step_rows)
                high_ref[at, lanes] = item_high
                low_ref[at, lanes] = item_low
    return to_coefs(high_ref[...], low_ref[...], coefs_ref)


def triple(pair):
    return jnp.concatenate([pair[0], pair[1], pair[0]], axis=1)


def build_kernel(
    info, pick_ref, mass_ref, stiff_ref, twist_ref, rates_ref, conn_ref, lists_ref,
    dense_ref, mass_own_ref, rest_own_ref, mass_ghost_ref, rest_ghost_ref, z_ref,
):
    nodes = pick_ref.shape[1]
    elements = conn_ref.shape[1]
    ghosts = lists_ref.shape[1]
    count = 2 * ghosts
    conn = conn_ref[...]
    pick = pick_ref[...]
    remap = slot_matrix(conn, lists_ref[...], info[0], info[1], info[2], nodes, ghosts)
    rates = rates_ref[0:1, :]
    step = 16
    for row in range(0, nodes, step):
        number = iota((step, elements), 0) + row
        hits = [(number == conn[a : a + 1, :]).astype(f32) for a in range(6)]
        for g, block in enumerate((mass_ref, stiff_ref, twist_ref)):
            for b in range(6):
                total = hits[0] * block[0, b : b + 1, :]
                for a in range(1, 6):
                    total = total + hits[a] * block[a, b : b + 1, :]
                lanes = pl.ds(b * elements, elements)
                z_ref[pl.ds(g * nodes + row, step), lanes] = total
                if g > 0:
                    z_ref[pl.ds((g + 2) * nodes + row, step), lanes] = total * rates
    arrives = lax.dot_general(
        remap, one_hot(conn, nodes, count), (((0,), (0,)), ((), ())), preferred_element_type=f32
    )
    column = jnp.concatenate([one_hot(conn, 0, nodes), arrives.astype(bf16)], axis=0)
    z = z_ref[...]
    first, second = halves(z)
    third = (z - first.astype(f32) - second.astype(f32)).astype(bf16)
    dense = dot_nt(first, column) + dot_nt(second, column) + dot_nt(third, column)
    dense_ref[...] = dense
    high, low = halves(dense)
    pairs = []
    for g in range(5):
        rows = slice(g * nodes, (g + 1) * nodes)
        factor = viscosity if g in (1, 2) else 1.0
        pairs.append([(factor * dot(pick, item[rows])).astype(bf16) for item in (high, low)])

    def own_part(pair):
        return triple([item[:, :nodes] for item in pair])

    def ghost_part(pair):
        return triple([item[:, nodes:] for item in pair])

    mass_own_ref[...] = own_part(pairs[0])
    mass_ghost_ref[...] = ghost_part(pairs[0])
    for f in range(2):
        used = (pairs[1], pairs[2]) if f == 0 else (pairs[3], pairs[4])
        rest_own_ref[f] = jnp.concatenate([own_part(pair) for pair in used], axis=0)
        rest_ghost_ref[f] = jnp.concatenate([ghost_part(pair) for pair in used], axis=0)


def force_kernel(
    state, planes_ref, coefs_ref, rotation_ref, squares_ref, mass_own, rest_own,
    force_ref, packed_ref, phys_ref, high_ref, low_ref,
):
    nodes = state.shape[1]
    count = packed_ref.shape[1]
    value = state[...].reshape(6 * nodes, state.shape[2])
    force_ref[...] = forcing(
        value, nodes, planes_ref, coefs_ref, rotation_ref, phys_ref, high_ref, low_ref
    ).reshape(force_ref.shape)
    square = squares_ref[0:1, :]
    for k in range(6):
        from_force = dot(mass_own[...], stacked_rows(force_ref[k]))
        from_state = dot(rest_own[k // 3], stacked_rows(state[k]))
        packed_ref[k] = from_force - (from_state[:count] + square * from_state[count:])


def ghost_block(info, near, far, k):
    distant = jnp.where(info[3] > 0, far[k], 0.0)
    return jnp.concatenate([near[k], distant], axis=0)


def start_kernel(
    info, near, far, packed, planes_ref, coefs_ref, rotation_ref, squares_ref, mass_ghost, rest_ghost,
    near_out, far_out, force_out, phys_ref, high_ref, low_ref,
):
    ghosts = near.shape[1]
    count = 2 * ghosts
    blocks = [ghost_block(info, near, far, k) for k in range(6)]
    value = jnp.concatenate(blocks, axis=0)
    force = forcing(value, count, planes_ref, coefs_ref, rotation_ref, phys_ref, high_ref, low_ref)
    square = squares_ref[0:1, :]
    for k in range(6):
        item = force[k * count : (k + 1) * count]
        force_out[k] = item
        from_force = dot(mass_ghost[...], stacked_rows(item))
        from_state = dot(rest_ghost[k // 3], stacked_rows(blocks[k]))
        total = packed[k] + from_force - (from_state[:count] + square * from_state[count:])
        near_out[k] = total[:ghosts]
        far_out[k] = total[ghosts:]


def apply_own(own, value, k, square, nodes, count):
    image = dot(own[k // 3], stacked_rows(value))
    full = image[:nodes] + square * image[nodes : 2 * nodes]
    packed = image[2 * nodes : 2 * nodes + count] + square * image[2 * nodes + count :]
    return full, packed


def first_kernel(
    info, near, far, force_ghost, force, state, dense_ref, pick_ref, squares_ref,
    own_ref, ghost_ref, back_ref, vector_out, image_out, packed_out, moments_out,
):
    nodes = state.shape[1]
    count = force_ghost.shape[1]
    square = squares_ref[0:1, :]
    pick = pick_ref[...]
    mass, stiff, twist, rate_stiff, rate_twist = [
        dense_ref[pl.ds(g * nodes, nodes), :] for g in range(5)
    ]
    mass_op = stacked_columns(mass)
    rest_ops = []
    for f in range(2):
        still = viscosity * stiff if f == 0 else rate_stiff
        turn = viscosity * twist if f == 0 else rate_twist
        rest_ops.append(jnp.concatenate([stacked_columns(still), stacked_columns(turn)], axis=0))
        image = (inverse_step * mass + still) * (1.0 / basis_scale)
        turn = turn * (1.0 / basis_scale)
        pairs = [halves(image), halves(turn)]
        pairs = pairs + [[dot(pick, item).astype(bf16) for item in pair] for pair in pairs]
        own_ref[f] = jnp.concatenate(
            [triple([item[:, :nodes] for item in pair]) for pair in pairs], axis=0
        )
        ghost_ref[f] = jnp.concatenate(
            [triple([item[:, nodes:] for item in pair]) for pair in pairs], axis=0
        )
        back = [jnp.transpose(item[:, nodes:]) for item in (image, turn)]
        back_ref[f] = jnp.concatenate([stacked_columns(item) for item in back], axis=0)
    for k in range(6):
        wide_force = jnp.concatenate([force[k], force_ghost[k]], axis=0)
        wide_state = jnp.concatenate([state[k], ghost_block(info, near, far, k)], axis=0)
        from_force = dot(mass_op, stacked_rows(wide_force))
        from_state = dot(rest_ops[k // 3], stacked_rows(wide_state))
        total = from_force - (from_state[:nodes] + square * from_state[nodes:])
        vector_out[k] = total
        full, packed = apply_own(own_ref, total, k, square, nodes, count)
        image_out[k] = full
        packed_out[k] = packed
        moments_out[k : k + 1, :] = jnp.sum(total * total, axis=0, keepdims=True)
    moments_out[6:8, :] = jnp.zeros((2, moments_out.shape[1]), f32)


def send_kernel(info, near, far, packed, ghost_ops, squares_ref, near_out, far_out):
    ghosts = near.shape[1]
    count = 2 * ghosts
    top = ghost_ops.shape[1] - 2 * count
    square = squares_ref[0:1, :]
    for k in range(6):
        image = dot(ghost_ops[k // 3, top:], stacked_rows(ghost_block(info, near, far, k)))
        total = packed[k] + image[:count] + square * image[count:]
        near_out[k] = total[:ghosts]
        far_out[k] = total[ghosts:]


def next_kernel(
    info, near, far, image, before, own, ghost_ops, squares_ref,
    vector_out, image_out, packed_out, moments_out,
):
    nodes = image.shape[1]
    count = 2 * near.shape[1]
    square = squares_ref[0:1, :]
    for k in range(6):
        part = dot(ghost_ops[k // 3, : 2 * nodes], stacked_rows(ghost_block(info, near, far, k)))
        total = image[k] + part[:nodes] + square * part[nodes:]
        vector_out[k] = total
        full, packed = apply_own(own, total, k, square, nodes, count)
        image_out[k] = full
        packed_out[k] = packed
        moments_out[k : k + 1, :] = jnp.sum(before[k] * total, axis=0, keepdims=True)
        moments_out[6 + k : 7 + k, :] = jnp.sum(total * total, axis=0, keepdims=True)
    moments_out[12:16, :] = jnp.zeros((4, moments_out.shape[1]), f32)


def last_kernel(
    info, near, far, near_last, image, before, own, ghost_ops, back_ops, squares_ref, first, second,
    vector_out, back_out, moments_out,
):
    nodes = image.shape[1]
    ghosts = near.shape[1]
    count = 2 * ghosts
    square = squares_ref[0:1, :]
    moments_out[0:6] = first[0:6]
    moments_out[6:18] = second[0:12]
    for k in range(6):
        part = dot(ghost_ops[k // 3, : 2 * nodes], stacked_rows(ghost_block(info, near, far, k)))
        total = image[k] + part[:nodes] + square * part[nodes:]
        vector_out[k] = total
        rows = stacked_rows(total)
        after = dot(own[k // 3, : 2 * nodes], rows)
        after = after[:nodes] + square * after[nodes:]
        back = dot(back_ops[k // 3], rows)
        back = back[:count] + square * back[count:]
        back_out[k] = back[ghosts:]
        moments_out[18 + k : 19 + k, :] = jnp.sum(before[k] * total, axis=0, keepdims=True)
        moments_out[24 + k : 25 + k, :] = jnp.sum(total * total, axis=0, keepdims=True)
        moments_out[30 + k : 31 + k, :] = jnp.sum(after * total, axis=0, keepdims=True) + jnp.sum(
            near_last[k] * back[:ghosts], axis=0, keepdims=True
        )
    moments_out[36:40, :] = jnp.zeros((4, moments_out.shape[1]), f32)


def join_kernel(weight, info, far, back, moments, *rest):
    out = rest[-1]
    total = moments[...]
    for other in rest[:-1]:
        total = total + other[...]
    out[...] = total
    for k in range(6):
        distant = jnp.where(info[3] > 0, far[k], 0.0)
        out[30 + k : 31 + k, :] += weight * jnp.sum(distant * back[k], axis=0, keepdims=True)


def finish_kernel(moments, other, velocity, magnetic, first, second, third, velocity_out, magnetic_out):
    total = moments[...] + other[...]
    m0, m1, m2, m3, m4, m5 = [total[6 * j : 6 * j + 6, :] for j in range(6)]
    scale = basis_scale
    alpha0 = m0 / (scale * m1 + epsilon)
    q1 = -alpha0 * scale
    rr1 = m0 + 2.0 * q1 * m1 + q1 * q1 * m2
    beta0 = rr1 / (m0 + epsilon)
    p0 = 1.0 + beta0
    p1 = q1
    alpha1 = rr1 / (scale * (p0 * p0 * m1 + 2.0 * p0 * p1 * m2 + p1 * p1 * m3) + epsilon)
    step1 = alpha1 * scale
    r1 = q1 - step1 * p0
    r2 = -step1 * p1
    rr2 = m0 + r1 * r1 * m2 + r2 * r2 * m4 + 2.0 * (r1 * m1 + r2 * m2 + r1 * r2 * m3)
    beta1 = rr2 / (rr1 + epsilon)
    d0 = 1.0 + beta1 * p0
    d1 = r1 + beta1 * p1
    d2 = r2
    curve = d0 * d0 * m1 + d1 * d1 * m3 + d2 * d2 * m5
    curve = curve + 2.0 * (d0 * d1 * m2 + d0 * d2 * m3 + d1 * d2 * m4)
    alpha2 = rr2 / (scale * curve + epsilon)
    c0 = alpha0 + alpha1 * p0 + alpha2 * d0
    c1 = alpha1 * p1 + alpha2 * d1
    c2 = alpha2 * d2
    for k in range(6):
        source, out = (velocity, velocity_out) if k < 3 else (magnetic, magnetic_out)
        change = (
            c0[k : k + 1, :] * first[k] + c1[k : k + 1, :] * second[k] + c2[k : k + 1, :] * third[k]
        )
        out[k % 3] = source[k % 3] + jnp.transpose(change)


def call(kernel, outs, operands, scratch=(), flops=0, limit=24, aliases=None):
    specs = [SMEM if operand.dtype == jnp.int32 and operand.ndim == 1 else VMEM for operand in operands]
    single = not isinstance(outs, list)
    shapes = [outs] if single else outs
    moved = sum(math.prod(o.shape) * o.dtype.itemsize for o in list(operands) + shapes)
    return pl.pallas_call(
        kernel,
        out_shape=outs,
        in_specs=specs,
        out_specs=VMEM if single else [VMEM] * len(outs),
        scratch_shapes=list(scratch),
        input_output_aliases=aliases or {},
        compiler_params=pltpu.CompilerParams(vmem_limit_bytes=limit * 1024 * 1024),
        cost_estimate=pl.CostEstimate(flops=flops, bytes_accessed=moved, transcendentals=0),
    )(*operands)


def shape(*sizes, dtype=f32):
    return jax.ShapeDtypeStruct(sizes, dtype)


def involution(pairs):
    return [edge for a, b in pairs for edge in ((a, b), (b, a))]


def local(runs, count, velocity, magnetic, mass_blocks, stiff_blocks, twist_blocks, diffusivity, conn, lists):
    coefs, nodes = velocity.shape[1:]
    ghosts = lists.shape[1]
    elements = conn.shape[1]
    both = 2 * ghosts
    planes = 2 * coefs
    index = lax.axis_index("mesh")
    odd = index % 2
    low_valid = (index > 0).astype(jnp.int32)
    high_valid = (index < count - 1).astype(jnp.int32)
    far_valid = jnp.where(odd == 1, high_valid, low_valid)
    info = jnp.stack([odd, low_valid, high_valid, far_valid]).astype(jnp.int32)

    near_pairs = [(i, i ^ 1) for i in range(count)]
    far_pairs = []
    for run in range(runs):
        base = run * count
        far_pairs += involution([(base + i, base + i + 1) for i in range(1, count - 1, 2)])
    if runs % 2 == 0:
        for run in range(0, runs, 2):
            for end in (0, count - 1):
                far_pairs += involution([(run * count + end, (run + 1) * count + end)])

    def swap_near(value):
        return lax.ppermute(value, "mesh", near_pairs)

    def swap_far(value):
        return lax.ppermute(value, ("runs", "mesh"), far_pairs)

    plane_table, coef_table, rotation, squares = transform_tables(coefs)
    plane_table, coef_table = jnp.asarray(plane_table), jnp.asarray(coef_table)
    rotation, squares = jnp.asarray(rotation), jnp.asarray(squares)
    ends = shape(6, ghosts, coefs)
    whole = shape(6, nodes, coefs)
    packs = shape(6, both, coefs)

    def exchange(near, far):
        far = swap_far(far)
        return swap_near(near), far

    near, far, state, pick = call(
        pack_velocity_kernel,
        [ends, ends, whole, shape(both, nodes, dtype=bf16)],
        [info, velocity, conn],
    )
    near, far, state = call(
        pack_magnetic_kernel,
        [ends, ends, whole],
        [magnetic, pick, near, far, state],
        aliases={2: 0, 3: 1, 4: 2},
    )
    near_state, far_state = exchange(near, far)
    dense, mass_own, rest_own, mass_ghost, rest_ghost = call(
        build_kernel,
        [
            shape(5 * nodes, nodes + both),
            shape(both, 3 * nodes, dtype=bf16),
            shape(2, 2 * both, 3 * nodes, dtype=bf16),
            shape(both, 3 * both, dtype=bf16),
            shape(2, 2 * both, 3 * both, dtype=bf16),
        ],
        [info, pick, mass_blocks, stiff_blocks, twist_blocks, diffusivity.reshape(1, elements), conn, lists],
        scratch=[pltpu.VMEM((5 * nodes, 6 * elements), f32)],
        flops=1_000_000_000,
    )
    force, packed = call(
        force_kernel,
        [whole, packs],
        [state, plane_table, coef_table, rotation, squares, mass_own, rest_own],
        scratch=[
            pltpu.VMEM((6 * nodes, planes), f32),
            pltpu.VMEM((6 * nodes, planes), bf16),
            pltpu.VMEM((6 * nodes, planes), bf16),
        ],
        flops=2_000_000_000,
    )
    near, far, force_ghost = call(
        start_kernel,
        [ends, ends, packs],
        [info, near_state, far_state, packed, plane_table, coef_table, rotation, squares]
        + [mass_ghost, rest_ghost],
        scratch=[
            pltpu.VMEM((6 * both, planes), f32),
            pltpu.VMEM((6 * both, planes), bf16),
            pltpu.VMEM((6 * both, planes), bf16),
        ],
        flops=1_000_000_000,
    )
    near_now, far_now = exchange(near, far)
    own, ghost_ops, back_ops, vector0, image, packed, moments0 = call(
        first_kernel,
        [
            shape(2, 2 * nodes + 2 * both, 3 * nodes, dtype=bf16),
            shape(2, 2 * nodes + 2 * both, 3 * both, dtype=bf16),
            shape(2, 2 * both, 3 * nodes, dtype=bf16),
            whole,
            whole,
            packs,
            shape(8, coefs),
        ],
        [info, near_state, far_state, force_ghost, force, state, dense, pick, squares],
        flops=2_000_000_000,
    )
    near, far = call(
        send_kernel, [ends, ends], [info, near_now, far_now, packed, ghost_ops, squares], flops=100_000_000
    )
    near_next, far_next = exchange(near, far)
    vector1, image, packed, moments1 = call(
        next_kernel,
        [whole, whole, packs, shape(16, coefs)],
        [info, near_now, far_now, image, vector0, own, ghost_ops, squares],
        flops=2_000_000_000,
    )
    near, far = call(
        send_kernel, [ends, ends], [info, near_next, far_next, packed, ghost_ops, squares], flops=100_000_000
    )
    near_last, far_last = exchange(near, far)
    vector2, back, moments = call(
        last_kernel,
        [whole, ends, shape(40, coefs)],
        [info, near_next, far_next, near_last, image, vector1, own, ghost_ops, back_ops, squares]
        + [moments0, moments1],
        flops=2_000_000_000,
    )
    if count % 8 == 0 and count <= 16:
        joined = call(
            functools.partial(join_kernel, 2.0),
            shape(40, coefs),
            [info, far_last, back, moments, swap_near(moments)],
        )
        target = (2, 0, 3, 1)
        lines = count // 4
        half = None
        for step in range(lines):
            pairs = [(i, ((i // 4) ^ step) * 4 + target[i % 4]) for i in range(count)]
            term = lax.ppermute(joined, "mesh", pairs)
            half = term if half is None else half + term
        other = swap_near(half)
    else:
        joined = call(
            functools.partial(join_kernel, 1.0), shape(40, coefs), [info, far_last, back, moments]
        )
        half = lax.psum(joined, "mesh")
        other = jnp.zeros_like(half)
    new_velocity, new_magnetic = call(
        finish_kernel,
        [shape(3, coefs, nodes), shape(3, coefs, nodes)],
        [half, other, velocity, magnetic, vector0, vector1, vector2],
        flops=10_000_000,
    )
    return new_velocity, new_magnetic


def solution(mesh):
    in_specs = (
        P("runs", None, "mesh"),
        P("runs", None, "mesh"),
        P(None, None, "mesh"),
        P(None, None, "mesh"),
        P(None, None, "mesh"),
        P(("runs", "mesh")),
        P(None, "mesh"),
        P(None, "mesh"),
    )
    out_specs = (P("runs", None, "mesh"), P("runs", None, "mesh"))
    sizes = dict(mesh.shape)
    step = functools.partial(local, sizes["runs"], sizes["mesh"])
    return jax.shard_map(step, mesh=mesh, in_specs=in_specs, out_specs=out_specs, check_vma=False)
```

```python
import functools
import math

import jax
import jax.numpy as jnp
import ml_dtypes
import numpy as np
from jax import lax
from jax.experimental import pallas as pl
from jax.experimental.pallas import tpu as pltpu
from jax.sharding import PartitionSpec as P

viscosity = 2.0
inverse_step = 10.0
tilt_factor = 0.5
axial_factor = 1.0
lorentz_factor = 0.005
epsilon = 1e-06
basis_scale = 512.0

f32 = jnp.float32
bf16 = jnp.bfloat16
VMEM = pl.BlockSpec(memory_space=pltpu.VMEM)


def split_table(table):
    high = table.astype(np.float32).astype(ml_dtypes.bfloat16)
    low = (table - high.astype(np.float64)).astype(np.float32).astype(ml_dtypes.bfloat16)
    return high, low


def transform_tables(coefs):
    planes = 2 * coefs
    mode = np.arange(coefs) // 2
    turns = (np.arange(planes)[:, None] * mode[None, :]) % planes
    angles = 2.0 * math.pi / planes * turns
    inverse = np.where(np.arange(coefs)[None, :] % 2 == 0, np.cos(angles), np.sin(angles))
    weight = np.where(mode == 0, 1.0, 2.0) / planes
    to_planes = np.concatenate(split_table(inverse.T.copy()), axis=0)
    to_coefs = np.concatenate(split_table(inverse * weight[None, :]), axis=0)
    phi = 2.0 * math.pi / planes * np.arange(planes)
    rows = np.zeros((8, planes), np.float32)
    rows[0] = -2.0 * tilt_factor * np.cos(phi)
    rows[1] = 2.0 * tilt_factor * np.sin(phi)
    rows[2] = -2.0 * axial_factor
    squares = np.zeros((8, coefs), np.float32)
    squares[:] = (mode * mode).astype(np.float32)[None, :]
    return to_planes, to_coefs, rows, squares


def halves(value):
    high = value.astype(bf16)
    return high, (value - high.astype(f32)).astype(bf16)


def dot(first, second):
    return lax.dot_general(first, second, (((1,), (0,)), ((), ())), preferred_element_type=f32)


def dot_nt(first, second):
    return lax.dot_general(first, second, (((1,), (1,)), ((), ())), preferred_element_type=f32)


def stacked_columns(value):
    high, low = halves(value)
    return jnp.concatenate([high, low, high], axis=1)


def stacked_rows(value):
    high, low = halves(value)
    return jnp.concatenate([high, high, low], axis=0)


def iota(shape, dim):
    return lax.broadcasted_iota(jnp.int32, shape, dim)


def one_hot(conn, first, count):
    row = iota((count, conn.shape[1]), 0) + first
    return jnp.concatenate([(row == conn[a : a + 1, :]).astype(bf16) for a in range(6)], axis=1)


def element_sides(conn, nodes, ghosts):
    own = jnp.max((conn < nodes).astype(f32), axis=0, keepdims=True)
    low = jnp.max(((conn >= nodes) & (conn < nodes + ghosts)).astype(f32), axis=0, keepdims=True)
    high = jnp.max((conn >= nodes + ghosts).astype(f32), axis=0, keepdims=True)
    return own, low, high


def eight_rows(items):
    row = iota((8, items[0].shape[1]), 0)
    total = jnp.zeros(row.shape, f32)
    for i, item in enumerate(items):
        total = jnp.where(row == i, item, total)
    return total


def pack_matrix(conn, odd, nodes, ghosts):
    _, low, high = element_sides(conn, nodes, ghosts)
    sides = eight_rows([low, high]).astype(bf16)
    sides = jnp.concatenate([sides] * 6, axis=1)
    named = dot_nt(sides, one_hot(conn, 0, nodes))
    flags = jnp.where(named > 0.0, 1.0, 0.0)
    before = (iota((nodes, nodes), 0) < iota((nodes, nodes), 1)).astype(bf16)
    ranks = dot(flags.astype(bf16), before).astype(jnp.int32)
    rows = iota((2 * ghosts, nodes), 0)
    picks = []
    odd = odd[:, :nodes].astype(jnp.int32)
    for side in range(2):
        offset = (1 - odd) * ghosts if side == 0 else odd * ghosts
        rank = ranks[side : side + 1, :]
        rank = jnp.where((flags[side : side + 1, :] > 0.0) & (rank < ghosts), rank + offset, -1)
        picks.append(rows == rank)
    return jnp.where(picks[0] | picks[1], 1.0, 0.0).astype(bf16)


def to_row(column, size):
    eye = iota((size, size), 0) == iota((size, size), 1)
    return jnp.sum(jnp.where(eye, column, 0.0), axis=0, keepdims=True)


def to_column(row, size):
    eye = iota((size, size), 0) == iota((size, size), 1)
    return jnp.sum(jnp.where(eye, row, 0.0), axis=1, keepdims=True)


def slot_matrix(conn, lists, info, nodes, ghosts):
    own, _, _ = element_sides(conn, nodes, ghosts)
    slot = iota((2 * ghosts, conn.shape[1]), 0) + nodes
    active = jnp.zeros((2 * ghosts, conn.shape[1]), f32)
    for a in range(conn.shape[0]):
        active = jnp.maximum(active, jnp.where(slot == conn[a : a + 1, :], own, 0.0))
    active = jnp.max(active, axis=1, keepdims=True)
    parts = []
    for side in range(2):
        flag = active[side * ghosts : (side + 1) * ghosts]
        node_row = lists[side : side + 1, :].astype(f32)
        node_column = to_column(node_row, ghosts)
        smaller = (node_row < node_column).astype(f32) * to_row(flag, ghosts)
        rank = jnp.sum(smaller, axis=1, keepdims=True).astype(jnp.int32)
        odd = info[0:1, : 2 * ghosts].astype(jnp.int32)
        offset = (1 - odd) * ghosts if side == 0 else odd * ghosts
        live = (flag > 0.0) & (info[1 + side : 2 + side, : 2 * ghosts] > 0.0)
        rows = iota((ghosts, 2 * ghosts), 1)
        parts.append(jnp.where(live & (rows == rank + offset), 1.0, 0.0))
    return jnp.concatenate(parts, axis=0).astype(bf16)


def pack_field(field, at, pick, near_ref, far_ref, state_ref):
    ghosts = near_ref.shape[1]
    for k in range(3):
        block = jnp.transpose(field[k])
        state_ref[at + k] = block
        first, rest = halves(block)
        second = (block - first.astype(f32) - rest.astype(f32)).astype(bf16)
        packed = dot(pick, first) + dot(pick, rest) + dot(pick, second)
        near_ref[at + k] = packed[:ghosts]
        far_ref[at + k] = packed[ghosts:]


def pack_velocity_kernel(info, velocity, conn_ref, near_ref, far_ref, state_ref, pick_ref):
    pick = pack_matrix(conn_ref[...], info[0:1, :], velocity.shape[2], near_ref.shape[1])
    pick_ref[...] = pick
    pack_field(velocity, 0, pick, near_ref, far_ref, state_ref)


def pack_magnetic_kernel(
    magnetic, pick_ref, near_in, far_in, state_in, near_ref, far_ref, state_ref
):
    pack_field(magnetic, 3, pick_ref[...], near_ref, far_ref, state_ref)


def to_planes(high, low, table):
    coefs = high.shape[1]
    return dot(high, table[:coefs]) + dot(low, table[:coefs]) + dot(high, table[coefs:])


def to_coefs(high, low, table):
    planes = high.shape[1]
    return dot(high, table[:planes]) + dot(low, table[:planes]) + dot(high, table[planes:])


def cross(a, b):
    return [
        a[1] * b[2] - a[2] * b[1],
        a[2] * b[0] - a[0] * b[2],
        a[0] * b[1] - a[1] * b[0],
    ]


def forcing(value, rows, planes_ref, coefs_ref, rotation_ref, phys_ref, high_ref, low_ref):
    planes = planes_ref.shape[1]
    high, low = halves(value)
    phys_ref[...] = to_planes(high, low, planes_ref)
    step_rows, step_lanes = 16, 256
    for row in range(0, rows, step_rows):
        for lane in range(0, planes, step_lanes):
            lanes = pl.ds(lane, step_lanes)
            u = [phys_ref[pl.ds(k * rows + row, step_rows), lanes] for k in range(3)]
            b = [phys_ref[pl.ds((3 + k) * rows + row, step_rows), lanes] for k in range(3)]
            turn = [rotation_ref[k : k + 1, lanes] for k in range(3)]
            induction = cross(u, b)
            twisted = cross(turn, u)
            lorentz = cross(b, induction)
            force = [twisted[k] - lorentz_factor * lorentz[k] for k in range(3)]
            for k, item in enumerate(force + induction):
                item_high, item_low = halves(item)
                at = pl.ds(k * rows + row, step_rows)
                high_ref[at, lanes] = item_high
                low_ref[at, lanes] = item_low
    return to_coefs(high_ref[...], low_ref[...], coefs_ref)


def triple(pair):
    return jnp.concatenate([pair[0], pair[1], pair[0]], axis=1)


def build_kernel(
    info, pick_ref, mass_ref, stiff_ref, twist_ref, rates_ref, conn_ref, lists_ref,
    dense_ref, mass_own_ref, rest_own_ref, mass_ghost_ref, rest_ghost_ref, z_ref,
):
    nodes = pick_ref.shape[1]
    elements = conn_ref.shape[1]
    ghosts = lists_ref.shape[1]
    count = 2 * ghosts
    conn = conn_ref[...]
    pick = pick_ref[...]
    remap = slot_matrix(conn, lists_ref[...], info, nodes, ghosts)
    rates = rates_ref[0:1, :]
    step = 16
    for row in range(0, nodes, step):
        number = iota((step, elements), 0) + row
        hits = [(number == conn[a : a + 1, :]).astype(f32) for a in range(6)]
        for g, block in enumerate((mass_ref, stiff_ref, twist_ref)):
            for b in range(6):
                total = hits[0] * block[0, b : b + 1, :]
                for a in range(1, 6):
                    total = total + hits[a] * block[a, b : b + 1, :]
                lanes = pl.ds(b * elements, elements)
                z_ref[pl.ds(g * nodes + row, step), lanes] = total
                if g > 0:
                    z_ref[pl.ds((g + 2) * nodes + row, step), lanes] = total * rates
    arrives = lax.dot_general(
        remap, one_hot(conn, nodes, count), (((0,), (0,)), ((), ())), preferred_element_type=f32
    )
    column = jnp.concatenate([one_hot(conn, 0, nodes), arrives.astype(bf16)], axis=0)
    z = z_ref[...]
    first, second = halves(z)
    third = (z - first.astype(f32) - second.astype(f32)).astype(bf16)
    dense = dot_nt(first, column) + dot_nt(second, column) + dot_nt(third, column)
    dense_ref[...] = dense
    high, low = halves(dense)
    pairs = []
    for g in range(5):
        rows = slice(g * nodes, (g + 1) * nodes)
        factor = viscosity if g in (1, 2) else 1.0
        pairs.append([(factor * dot(pick, item[rows])).astype(bf16) for item in (high, low)])

    def own_part(pair):
        return triple([item[:, :nodes] for item in pair])

    def ghost_part(pair):
        return triple([item[:, nodes:] for item in pair])

    mass_own_ref[...] = own_part(pairs[0])
    mass_ghost_ref[...] = ghost_part(pairs[0])
    for f in range(2):
        used = (pairs[1], pairs[2]) if f == 0 else (pairs[3], pairs[4])
        rest_own_ref[f] = jnp.concatenate([own_part(pair) for pair in used], axis=0)
        rest_ghost_ref[f] = jnp.concatenate([ghost_part(pair) for pair in used], axis=0)


def force_kernel(
    state, planes_ref, coefs_ref, rotation_ref, squares_ref, mass_own, rest_own,
    force_ref, packed_ref, phys_ref, high_ref, low_ref,
):
    nodes = state.shape[1]
    count = packed_ref.shape[1]
    value = state[...].reshape(6 * nodes, state.shape[2])
    force_ref[...] = forcing(
        value, nodes, planes_ref, coefs_ref, rotation_ref, phys_ref, high_ref, low_ref
    ).reshape(force_ref.shape)
    square = squares_ref[0:1, :]
    for k in range(6):
        from_force = dot(mass_own[...], stacked_rows(force_ref[k]))
        from_state = dot(rest_own[k // 3], stacked_rows(state[k]))
        packed_ref[k] = from_force - (from_state[:count] + square * from_state[count:])


def ghost_block(info, near, far, k):
    distant = jnp.where(info[3:4, :] > 0.0, far[k], 0.0)
    return jnp.concatenate([near[k], distant], axis=0)


def start_kernel(
    info, near, far, packed, planes_ref, coefs_ref, rotation_ref, squares_ref, mass_ghost, rest_ghost,
    near_out, far_out, force_out, phys_ref, high_ref, low_ref,
):
    ghosts = near.shape[1]
    count = 2 * ghosts
    blocks = [ghost_block(info, near, far, k) for k in range(6)]
    value = jnp.concatenate(blocks, axis=0)
    force = forcing(value, count, planes_ref, coefs_ref, rotation_ref, phys_ref, high_ref, low_ref)
    square = squares_ref[0:1, :]
    for k in range(6):
        item = force[k * count : (k + 1) * count]
        force_out[k] = item
        from_force = dot(mass_ghost[...], stacked_rows(item))
        from_state = dot(rest_ghost[k // 3], stacked_rows(blocks[k]))
        total = packed[k] + from_force - (from_state[:count] + square * from_state[count:])
        near_out[k] = total[:ghosts]
        far_out[k] = total[ghosts:]


def apply_own(own, value, k, square, nodes, count):
    image = dot(own[k // 3], stacked_rows(value))
    full = image[:nodes] + square * image[nodes : 2 * nodes]
    packed = image[2 * nodes : 2 * nodes + count] + square * image[2 * nodes + count :]
    return full, packed


def first_kernel(
    info, near, far, force_ghost, force, state, dense_ref, pick_ref, squares_ref,
    own_ref, ghost_ref, back_ref, vector_out, image_out, packed_out, moments_out,
):
    nodes = state.shape[1]
    count = force_ghost.shape[1]
    square = squares_ref[0:1, :]
    pick = pick_ref[...]
    mass, stiff, twist, rate_stiff, rate_twist = [
        dense_ref[pl.ds(g * nodes, nodes), :] for g in range(5)
    ]
    mass_op = stacked_columns(mass)
    rest_ops = []
    for f in range(2):
        still = viscosity * stiff if f == 0 else rate_stiff
        turn = viscosity * twist if f == 0 else rate_twist
        rest_ops.append(jnp.concatenate([stacked_columns(still), stacked_columns(turn)], axis=0))
        image = (inverse_step * mass + still) * (1.0 / basis_scale)
        turn = turn * (1.0 / basis_scale)
        pairs = [halves(image), halves(turn)]
        pairs = pairs + [[dot(pick, item).astype(bf16) for item in pair] for pair in pairs]
        own_ref[f] = jnp.concatenate(
            [triple([item[:, :nodes] for item in pair]) for pair in pairs], axis=0
        )
        ghost_ref[f] = jnp.concatenate(
            [triple([item[:, nodes:] for item in pair]) for pair in pairs], axis=0
        )
        back = [jnp.transpose(item[:, nodes:]) for item in (image, turn)]
        back_ref[f] = jnp.concatenate([stacked_columns(item) for item in back], axis=0)
    for k in range(6):
        wide_force = jnp.concatenate([force[k], force_ghost[k]], axis=0)
        wide_state = jnp.concatenate([state[k], ghost_block(info, near, far, k)], axis=0)
        from_force = dot(mass_op, stacked_rows(wide_force))
        from_state = dot(rest_ops[k // 3], stacked_rows(wide_state))
        total = from_force - (from_state[:nodes] + square * from_state[nodes:])
        vector_out[k] = total
        full, packed = apply_own(own_ref, total, k, square, nodes, count)
        image_out[k] = full
        packed_out[k] = packed
        moments_out[k : k + 1, :] = jnp.sum(total * total, axis=0, keepdims=True)
    moments_out[6:8, :] = jnp.zeros((2, moments_out.shape[1]), f32)


def send_kernel(info, near, far, packed, ghost_ops, squares_ref, near_out, far_out):
    ghosts = near.shape[1]
    count = 2 * ghosts
    top = ghost_ops.shape[1] - 2 * count
    square = squares_ref[0:1, :]
    for k in range(6):
        image = dot(ghost_ops[k // 3, top:], stacked_rows(ghost_block(info, near, far, k)))
        total = packed[k] + image[:count] + square * image[count:]
        near_out[k] = total[:ghosts]
        far_out[k] = total[ghosts:]


def next_kernel(
    info, near, far, image, before, own, ghost_ops, squares_ref,
    vector_out, image_out, packed_out, moments_out,
):
    nodes = image.shape[1]
    count = 2 * near.shape[1]
    square = squares_ref[0:1, :]
    for k in range(6):
        part = dot(ghost_ops[k // 3, : 2 * nodes], stacked_rows(ghost_block(info, near, far, k)))
        total = image[k] + part[:nodes] + square * part[nodes:]
        vector_out[k] = total
        full, packed = apply_own(own, total, k, square, nodes, count)
        image_out[k] = full
        packed_out[k] = packed
        moments_out[k : k + 1, :] = jnp.sum(before[k] * total, axis=0, keepdims=True)
        moments_out[6 + k : 7 + k, :] = jnp.sum(total * total, axis=0, keepdims=True)
    moments_out[12:16, :] = jnp.zeros((4, moments_out.shape[1]), f32)


def last_kernel(
    info, near, far, near_last, image, before, own, ghost_ops, back_ops, squares_ref, first, second,
    vector_out, back_out, moments_out,
):
    nodes = image.shape[1]
    ghosts = near.shape[1]
    count = 2 * ghosts
    square = squares_ref[0:1, :]
    moments_out[0:6] = first[0:6]
    moments_out[6:18] = second[0:12]
    for k in range(6):
        part = dot(ghost_ops[k // 3, : 2 * nodes], stacked_rows(ghost_block(info, near, far, k)))
        total = image[k] + part[:nodes] + square * part[nodes:]
        vector_out[k] = total
        rows = stacked_rows(total)
        after = dot(own[k // 3, : 2 * nodes], rows)
        after = after[:nodes] + square * after[nodes:]
        back = dot(back_ops[k // 3], rows)
        back = back[:count] + square * back[count:]
        back_out[k] = back[ghosts:]
        moments_out[18 + k : 19 + k, :] = jnp.sum(before[k] * total, axis=0, keepdims=True)
        moments_out[24 + k : 25 + k, :] = jnp.sum(total * total, axis=0, keepdims=True)
        moments_out[30 + k : 31 + k, :] = jnp.sum(after * total, axis=0, keepdims=True) + jnp.sum(
            near_last[k] * back[:ghosts], axis=0, keepdims=True
        )
    moments_out[36:40, :] = jnp.zeros((4, moments_out.shape[1]), f32)


def join_kernel(weight, info, far, back, moments, *rest):
    out = rest[-1]
    total = moments[...]
    for other in rest[:-1]:
        total = total + other[...]
    out[...] = total
    for k in range(6):
        distant = jnp.where(info[3:4, :] > 0.0, far[k], 0.0)
        out[30 + k : 31 + k, :] += weight * jnp.sum(distant * back[k], axis=0, keepdims=True)


def finish_kernel(moments, other, velocity, magnetic, first, second, third, velocity_out, magnetic_out):
    total = moments[...] + other[...]
    m0, m1, m2, m3, m4, m5 = [total[6 * j : 6 * j + 6, :] for j in range(6)]
    scale = basis_scale
    alpha0 = m0 / (scale * m1 + epsilon)
    q1 = -alpha0 * scale
    rr1 = m0 + 2.0 * q1 * m1 + q1 * q1 * m2
    beta0 = rr1 / (m0 + epsilon)
    p0 = 1.0 + beta0
    p1 = q1
    alpha1 = rr1 / (scale * (p0 * p0 * m1 + 2.0 * p0 * p1 * m2 + p1 * p1 * m3) + epsilon)
    step1 = alpha1 * scale
    r1 = q1 - step1 * p0
    r2 = -step1 * p1
    rr2 = m0 + r1 * r1 * m2 + r2 * r2 * m4 + 2.0 * (r1 * m1 + r2 * m2 + r1 * r2 * m3)
    beta1 = rr2 / (rr1 + epsilon)
    d0 = 1.0 + beta1 * p0
    d1 = r1 + beta1 * p1
    d2 = r2
    curve = d0 * d0 * m1 + d1 * d1 * m3 + d2 * d2 * m5
    curve = curve + 2.0 * (d0 * d1 * m2 + d0 * d2 * m3 + d1 * d2 * m4)
    alpha2 = rr2 / (scale * curve + epsilon)
    c0 = alpha0 + alpha1 * p0 + alpha2 * d0
    c1 = alpha1 * p1 + alpha2 * d1
    c2 = alpha2 * d2
    for k in range(6):
        source, out = (velocity, velocity_out) if k < 3 else (magnetic, magnetic_out)
        change = (
            c0[k : k + 1, :] * first[k] + c1[k : k + 1, :] * second[k] + c2[k : k + 1, :] * third[k]
        )
        out[k % 3] = source[k % 3] + jnp.transpose(change)


def call(kernel, outs, operands, scratch=(), flops=0, limit=24, aliases=None):
    single = not isinstance(outs, list)
    shapes = [outs] if single else outs
    moved = sum(math.prod(o.shape) * o.dtype.itemsize for o in list(operands) + shapes)
    return pl.pallas_call(
        kernel,
        out_shape=outs,
        in_specs=[VMEM] * len(operands),
        out_specs=VMEM if single else [VMEM] * len(outs),
        scratch_shapes=list(scratch),
        input_output_aliases=aliases or {},
        compiler_params=pltpu.CompilerParams(vmem_limit_bytes=limit * 1024 * 1024),
        cost_estimate=pl.CostEstimate(flops=flops, bytes_accessed=moved, transcendentals=0),
    )(*operands)


def shape(*sizes, dtype=f32):
    return jax.ShapeDtypeStruct(sizes, dtype)


def involution(pairs):
    return [edge for a, b in pairs for edge in ((a, b), (b, a))]


def local(runs, count, velocity, magnetic, mass_blocks, stiff_blocks, twist_blocks, diffusivity, conn, lists):
    coefs, nodes = velocity.shape[1:]
    ghosts = lists.shape[1]
    elements = conn.shape[1]
    both = 2 * ghosts
    planes = 2 * coefs
    index = lax.axis_index("mesh")
    odd = index % 2
    low_valid = (index > 0).astype(jnp.int32)
    high_valid = (index < count - 1).astype(jnp.int32)
    far_valid = jnp.where(odd == 1, high_valid, low_valid)
    zero = jnp.zeros_like(odd)
    info = jnp.stack([odd, low_valid, high_valid, far_valid, zero, zero, zero, zero]).astype(f32)
    info = jnp.broadcast_to(info[:, None], (8, coefs))

    near_pairs = [(i, i ^ 1) for i in range(count)]
    far_pairs = []
    for run in range(runs):
        base = run * count
        far_pairs += involution([(base + i, base + i + 1) for i in range(1, count - 1, 2)])
    if runs % 2 == 0:
        for run in range(0, runs, 2):
            for end in (0, count - 1):
                far_pairs += involution([(run * count + end, (run + 1) * count + end)])

    def swap_near(value):
        return lax.ppermute(value, "mesh", near_pairs)

    def swap_far(value):
        return lax.ppermute(value, ("runs", "mesh"), far_pairs)

    plane_table, coef_table, rotation, squares = transform_tables(coefs)
    plane_table, coef_table = jnp.asarray(plane_table), jnp.asarray(coef_table)
    rotation, squares = jnp.asarray(rotation), jnp.asarray(squares)
    ends = shape(6, ghosts, coefs)
    whole = shape(6, nodes, coefs)
    packs = shape(6, both, coefs)

    def exchange(near, far):
        far = swap_far(far)
        return swap_near(near), far

    near, far, state, pick = call(
        pack_velocity_kernel,
        [ends, ends, whole, shape(both, nodes, dtype=bf16)],
        [info, velocity, conn],
    )
    near, far, state = call(
        pack_magnetic_kernel,
        [ends, ends, whole],
        [magnetic, pick, near, far, state],
        aliases={2: 0, 3: 1, 4: 2},
    )
    near_state, far_state = exchange(near, far)
    dense, mass_own, rest_own, mass_ghost, rest_ghost = call(
        build_kernel,
        [
            shape(5 * nodes, nodes + both),
            shape(both, 3 * nodes, dtype=bf16),
            shape(2, 2 * both, 3 * nodes, dtype=bf16),
            shape(both, 3 * both, dtype=bf16),
            shape(2, 2 * both, 3 * both, dtype=bf16),
        ],
        [info, pick, mass_blocks, stiff_blocks, twist_blocks, diffusivity.reshape(1, elements), conn, lists],
        scratch=[pltpu.VMEM((5 * nodes, 6 * elements), f32)],
        flops=1_000_000_000,
    )
    force, packed = call(
        force_kernel,
        [whole, packs],
        [state, plane_table, coef_table, rotation, squares, mass_own, rest_own],
        scratch=[
            pltpu.VMEM((6 * nodes, planes), f32),
            pltpu.VMEM((6 * nodes, planes), bf16),
            pltpu.VMEM((6 * nodes, planes), bf16),
        ],
        flops=2_000_000_000,
    )
    near, far, force_ghost = call(
        start_kernel,
        [ends, ends, packs],
        [info, near_state, far_state, packed, plane_table, coef_table, rotation, squares]
        + [mass_ghost, rest_ghost],
        scratch=[
            pltpu.VMEM((6 * both, planes), f32),
            pltpu.VMEM((6 * both, planes), bf16),
            pltpu.VMEM((6 * both, planes), bf16),
        ],
        flops=1_000_000_000,
    )
    near_now, far_now = exchange(near, far)
    own, ghost_ops, back_ops, vector0, image, packed, moments0 = call(
        first_kernel,
        [
            shape(2, 2 * nodes + 2 * both, 3 * nodes, dtype=bf16),
            shape(2, 2 * nodes + 2 * both, 3 * both, dtype=bf16),
            shape(2, 2 * both, 3 * nodes, dtype=bf16),
            whole,
            whole,
            packs,
            shape(8, coefs),
        ],
        [info, near_state, far_state, force_ghost, force, state, dense, pick, squares],
        flops=2_000_000_000,
    )
    near, far = call(
        send_kernel, [ends, ends], [info, near_now, far_now, packed, ghost_ops, squares], flops=100_000_000
    )
    near_next, far_next = exchange(near, far)
    vector1, image, packed, moments1 = call(
        next_kernel,
        [whole, whole, packs, shape(16, coefs)],
        [info, near_now, far_now, image, vector0, own, ghost_ops, squares],
        flops=2_000_000_000,
    )
    near, far = call(
        send_kernel, [ends, ends], [info, near_next, far_next, packed, ghost_ops, squares], flops=100_000_000
    )
    near_last, far_last = exchange(near, far)
    vector2, back, moments = call(
        last_kernel,
        [whole, ends, shape(40, coefs)],
        [info, near_next, far_next, near_last, image, vector1, own, ghost_ops, back_ops, squares]
        + [moments0, moments1],
        flops=2_000_000_000,
    )
    if count % 8 == 0 and count <= 16:
        joined = call(
            functools.partial(join_kernel, 2.0),
            shape(40, coefs),
            [info, far_last, back, moments, swap_near(moments)],
        )
        target = (2, 0, 3, 1)
        lines = count // 4
        half = None
        for step in range(lines):
            pairs = [(i, ((i // 4) ^ step) * 4 + target[i % 4]) for i in range(count)]
            term = lax.ppermute(joined, "mesh", pairs)
            half = term if half is None else half + term
        other = swap_near(half)
    else:
        joined = call(
            functools.partial(join_kernel, 1.0), shape(40, coefs), [info, far_last, back, moments]
        )
        half = lax.psum(joined, "mesh")
        other = jnp.zeros_like(half)
    new_velocity, new_magnetic = call(
        finish_kernel,
        [shape(3, coefs, nodes), shape(3, coefs, nodes)],
        [half, other, velocity, magnetic, vector0, vector1, vector2],
        flops=10_000_000,
    )
    return new_velocity, new_magnetic


def solution(mesh):
    in_specs = (
        P("runs", None, "mesh"),
        P("runs", None, "mesh"),
        P(None, None, "mesh"),
        P(None, None, "mesh"),
        P(None, None, "mesh"),
        P(("runs", "mesh")),
        P(None, "mesh"),
        P(None, "mesh"),
    )
    out_specs = (P("runs", None, "mesh"), P("runs", None, "mesh"))
    sizes = dict(mesh.shape)
    step = functools.partial(local, sizes["runs"], sizes["mesh"])
    return jax.shard_map(step, mesh=mesh, in_specs=in_specs, out_specs=out_specs, check_vma=False)
```

```python
import functools
import math

import jax
import jax.numpy as jnp
import ml_dtypes
import numpy as np
from jax import lax
from jax.experimental import pallas as pl
from jax.experimental.pallas import tpu as pltpu
from jax.sharding import PartitionSpec as P

viscosity = 2.0
inverse_step = 10.0
tilt_factor = 0.5
axial_factor = 1.0
lorentz_factor = 0.005
epsilon = 1e-06
basis_scale = 512.0

f32 = jnp.float32
bf16 = jnp.bfloat16
VMEM = pl.BlockSpec(memory_space=pltpu.VMEM)


def split_table(table):
    high = table.astype(np.float32).astype(ml_dtypes.bfloat16)
    low = (table - high.astype(np.float64)).astype(np.float32).astype(ml_dtypes.bfloat16)
    return high, low


def transform_tables(coefs):
    planes = 2 * coefs
    mode = np.arange(coefs) // 2
    turns = (np.arange(planes)[:, None] * mode[None, :]) % planes
    angles = 2.0 * math.pi / planes * turns
    inverse = np.where(np.arange(coefs)[None, :] % 2 == 0, np.cos(angles), np.sin(angles))
    weight = np.where(mode == 0, 1.0, 2.0) / planes
    to_planes = np.concatenate(split_table(inverse.T.copy()), axis=0)
    to_coefs = np.concatenate(split_table(inverse * weight[None, :]), axis=0)
    phi = 2.0 * math.pi / planes * np.arange(planes)
    rows = np.zeros((8, planes), np.float32)
    rows[0] = -2.0 * tilt_factor * np.cos(phi)
    rows[1] = 2.0 * tilt_factor * np.sin(phi)
    rows[2] = -2.0 * axial_factor
    squares = np.zeros((8, coefs), np.float32)
    squares[:] = (mode * mode).astype(np.float32)[None, :]
    return to_planes, to_coefs, rows, squares


def halves(value):
    high = value.astype(bf16)
    return high, (value - high.astype(f32)).astype(bf16)


def dot(first, second):
    return lax.dot_general(first, second, (((1,), (0,)), ((), ())), preferred_element_type=f32)


def dot_nt(first, second):
    return lax.dot_general(first, second, (((1,), (1,)), ((), ())), preferred_element_type=f32)


def stacked_columns(value):
    high, low = halves(value)
    return jnp.concatenate([high, low, high], axis=1)


def stacked_rows(value):
    high, low = halves(value)
    return jnp.concatenate([high, high, low], axis=0)


def iota(shape, dim):
    return lax.broadcasted_iota(jnp.int32, shape, dim)


def one_hot(conn, first, count):
    row = iota((count, conn.shape[1]), 0) + first
    return jnp.concatenate([(row == conn[a : a + 1, :]).astype(bf16) for a in range(6)], axis=1)


def element_sides(conn, nodes, ghosts):
    own = jnp.max((conn < nodes).astype(f32), axis=0, keepdims=True)
    low = jnp.max(((conn >= nodes) & (conn < nodes + ghosts)).astype(f32), axis=0, keepdims=True)
    high = jnp.max((conn >= nodes + ghosts).astype(f32), axis=0, keepdims=True)
    return own, low, high


def eight_rows(items):
    row = iota((8, items[0].shape[1]), 0)
    total = jnp.zeros(row.shape, f32)
    for i, item in enumerate(items):
        total = jnp.where(row == i, item, total)
    return total


def pack_matrix(conn, odd, nodes, ghosts):
    _, low, high = element_sides(conn, nodes, ghosts)
    sides = eight_rows([low, high]).astype(bf16)
    sides = jnp.concatenate([sides] * 6, axis=1)
    named = dot_nt(sides, one_hot(conn, 0, nodes))
    flags = jnp.where(named > 0.0, 1.0, 0.0)
    before = (iota((nodes, nodes), 0) < iota((nodes, nodes), 1)).astype(bf16)
    ranks = dot(flags.astype(bf16), before).astype(jnp.int32)
    rows = iota((2 * ghosts, nodes), 0)
    picks = []
    odd = odd[:, :nodes].astype(jnp.int32)
    for side in range(2):
        offset = (1 - odd) * ghosts if side == 0 else odd * ghosts
        rank = ranks[side : side + 1, :]
        rank = jnp.where((flags[side : side + 1, :] > 0.0) & (rank < ghosts), rank + offset, -1)
        picks.append(rows == rank)
    return jnp.where(picks[0] | picks[1], 1.0, 0.0).astype(bf16)


def to_row(column, size):
    eye = iota((size, size), 0) == iota((size, size), 1)
    return jnp.sum(jnp.where(eye, column, 0.0), axis=0, keepdims=True)


def to_column(row, size):
    eye = iota((size, size), 0) == iota((size, size), 1)
    return jnp.sum(jnp.where(eye, row, 0.0), axis=1, keepdims=True)


def slot_matrix(conn, lists, info, nodes, ghosts):
    own, _, _ = element_sides(conn, nodes, ghosts)
    slot = iota((2 * ghosts, conn.shape[1]), 0) + nodes
    active = jnp.zeros((2 * ghosts, conn.shape[1]), f32)
    for a in range(conn.shape[0]):
        active = jnp.maximum(active, jnp.where(slot == conn[a : a + 1, :], own, 0.0))
    active = jnp.max(active, axis=1, keepdims=True)
    parts = []
    for side in range(2):
        flag = active[side * ghosts : (side + 1) * ghosts]
        node_row = lists[side : side + 1, :].astype(f32)
        node_column = to_column(node_row, ghosts)
        smaller = (node_row < node_column).astype(f32) * to_row(flag, ghosts)
        rank = jnp.sum(smaller, axis=1, keepdims=True).astype(jnp.int32)
        odd = info[0:1, : 2 * ghosts].astype(jnp.int32)
        offset = (1 - odd) * ghosts if side == 0 else odd * ghosts
        live = (flag > 0.0) & (info[1 + side : 2 + side, : 2 * ghosts] > 0.0)
        rows = iota((ghosts, 2 * ghosts), 1)
        parts.append(jnp.where(live & (rows == rank + offset), 1.0, 0.0))
    return jnp.concatenate(parts, axis=0).astype(bf16)


def pack_field(field, at, pick, near_ref, far_ref, state_ref):
    ghosts = near_ref.shape[1]
    for k in range(3):
        block = jnp.transpose(field[k])
        state_ref[at + k] = block
        first, rest = halves(block)
        second = (block - first.astype(f32) - rest.astype(f32)).astype(bf16)
        packed = dot(pick, first) + dot(pick, rest) + dot(pick, second)
        near_ref[at + k] = packed[:ghosts]
        far_ref[at + k] = packed[ghosts:]


def pack_velocity_kernel(info, velocity, conn_ref, near_ref, far_ref, state_ref, pick_ref):
    pick = pack_matrix(conn_ref[...], info[0:1, :], velocity.shape[2], near_ref.shape[1])
    pick_ref[...] = pick
    pack_field(velocity, 0, pick, near_ref, far_ref, state_ref)


def pack_magnetic_kernel(
    magnetic, pick_ref, near_in, far_in, state_in, near_ref, far_ref, state_ref
):
    pack_field(magnetic, 3, pick_ref[...], near_ref, far_ref, state_ref)


def to_planes(high, low, table):
    coefs = high.shape[1]
    return dot(high, table[:coefs]) + dot(low, table[:coefs]) + dot(high, table[coefs:])


def to_coefs(high, low, table):
    planes = high.shape[1]
    return dot(high, table[:planes]) + dot(low, table[:planes]) + dot(high, table[planes:])


def cross(a, b):
    return [
        a[1] * b[2] - a[2] * b[1],
        a[2] * b[0] - a[0] * b[2],
        a[0] * b[1] - a[1] * b[0],
    ]


def forcing(value, rows, planes_ref, coefs_ref, rotation_ref, phys_ref, high_ref, low_ref):
    planes = planes_ref.shape[1]
    high, low = halves(value)
    phys_ref[...] = to_planes(high, low, planes_ref)
    step_rows, step_lanes = 16, 256
    for row in range(0, rows, step_rows):
        for lane in range(0, planes, step_lanes):
            lanes = pl.ds(lane, step_lanes)
            u = [phys_ref[pl.ds(k * rows + row, step_rows), lanes] for k in range(3)]
            b = [phys_ref[pl.ds((3 + k) * rows + row, step_rows), lanes] for k in range(3)]
            turn = [rotation_ref[k : k + 1, lanes] for k in range(3)]
            induction = cross(u, b)
            twisted = cross(turn, u)
            lorentz = cross(b, induction)
            force = [twisted[k] - lorentz_factor * lorentz[k] for k in range(3)]
            for k, item in enumerate(force + induction):
                item_high, item_low = halves(item)
                at = pl.ds(k * rows + row, step_rows)
                high_ref[at, lanes] = item_high
                low_ref[at, lanes] = item_low
    return to_coefs(high_ref[...], low_ref[...], coefs_ref)


def triple(pair):
    return jnp.concatenate([pair[0], pair[1], pair[0]], axis=1)


def build_kernel(
    info, pick_ref, mass_ref, stiff_ref, twist_ref, rates_ref, conn_ref, lists_ref,
    dense_ref, mass_own_ref, rest_own_ref, mass_ghost_ref, rest_ghost_ref, z_ref,
):
    nodes = pick_ref.shape[1]
    elements = conn_ref.shape[1]
    ghosts = lists_ref.shape[1]
    count = 2 * ghosts
    conn = conn_ref[...]
    pick = pick_ref[...]
    remap = slot_matrix(conn, lists_ref[...], info, nodes, ghosts)
    rates = rates_ref[0:1, :]
    step = 16
    for row in range(0, nodes, step):
        number = iota((step, elements), 0) + row
        hits = [(number == conn[a : a + 1, :]).astype(f32) for a in range(6)]
        for g, block in enumerate((mass_ref, stiff_ref, twist_ref)):
            for b in range(6):
                total = hits[0] * block[0, b : b + 1, :]
                for a in range(1, 6):
                    total = total + hits[a] * block[a, b : b + 1, :]
                lanes = pl.ds(b * elements, elements)
                z_ref[pl.ds(g * nodes + row, step), lanes] = total
                if g > 0:
                    z_ref[pl.ds((g + 2) * nodes + row, step), lanes] = total * rates
    arrives = lax.dot_general(
        remap, one_hot(conn, nodes, count), (((0,), (0,)), ((), ())), preferred_element_type=f32
    )
    column = jnp.concatenate([one_hot(conn, 0, nodes), arrives.astype(bf16)], axis=0)
    z = z_ref[...]
    first, second = halves(z)
    third = (z - first.astype(f32) - second.astype(f32)).astype(bf16)
    dense = dot_nt(first, column) + dot_nt(second, column) + dot_nt(third, column)
    dense_ref[...] = dense
    high, low = halves(dense)
    pairs = []
    for g in range(5):
        rows = slice(g * nodes, (g + 1) * nodes)
        factor = viscosity if g in (1, 2) else 1.0
        pairs.append([(factor * dot(pick, item[rows])).astype(bf16) for item in (high, low)])

    def own_part(pair):
        return triple([item[:, :nodes] for item in pair])

    def ghost_part(pair):
        return triple([item[:, nodes:] for item in pair])

    mass_own_ref[...] = own_part(pairs[0])
    mass_ghost_ref[...] = ghost_part(pairs[0])
    for f in range(2):
        used = (pairs[1], pairs[2]) if f == 0 else (pairs[3], pairs[4])
        rest_own_ref[f] = jnp.concatenate([own_part(pair) for pair in used], axis=0)
        rest_ghost_ref[f] = jnp.concatenate([ghost_part(pair) for pair in used], axis=0)


def force_kernel(
    state, planes_ref, coefs_ref, rotation_ref, squares_ref, mass_own, rest_own,
    force_ref, packed_ref, phys_ref, high_ref, low_ref,
):
    nodes = state.shape[1]
    count = packed_ref.shape[1]
    value = state[...].reshape(6 * nodes, state.shape[2])
    force_ref[...] = forcing(
        value, nodes, planes_ref, coefs_ref, rotation_ref, phys_ref, high_ref, low_ref
    ).reshape(force_ref.shape)
    square = squares_ref[0:1, :]
    for k in range(6):
        from_force = dot(mass_own[...], stacked_rows(force_ref[k]))
        from_state = dot(rest_own[k // 3], stacked_rows(state[k]))
        packed_ref[k] = from_force - (from_state[:count] + square * from_state[count:])


def ghost_block(info, near, far, k):
    distant = jnp.where(info[3:4, :] > 0.0, far[k], 0.0)
    return jnp.concatenate([near[k], distant], axis=0)


def start_kernel(
    info, far, near, packed, planes_ref, coefs_ref, rotation_ref, squares_ref, mass_ghost, rest_ghost,
    near_out, far_out, force_out, phys_ref, high_ref, low_ref,
):
    ghosts = near.shape[1]
    count = 2 * ghosts
    blocks = [ghost_block(info, near, far, k) for k in range(6)]
    value = jnp.concatenate(blocks, axis=0)
    force = forcing(value, count, planes_ref, coefs_ref, rotation_ref, phys_ref, high_ref, low_ref)
    square = squares_ref[0:1, :]
    for k in range(6):
        item = force[k * count : (k + 1) * count]
        force_out[k] = item
        from_force = dot(mass_ghost[...], stacked_rows(item))
        from_state = dot(rest_ghost[k // 3], stacked_rows(blocks[k]))
        total = packed[k] + from_force - (from_state[:count] + square * from_state[count:])
        near_out[k] = total[:ghosts]
        far_out[k] = total[ghosts:]


def apply_own(own, value, k, square, nodes, count):
    image = dot(own[k // 3], stacked_rows(value))
    full = image[:nodes] + square * image[nodes : 2 * nodes]
    packed = image[2 * nodes : 2 * nodes + count] + square * image[2 * nodes + count :]
    return full, packed


def first_kernel(
    info, far, near, force_ghost, force, state, dense_ref, pick_ref, squares_ref,
    own_ref, ghost_ref, back_ref, vector_out, image_out, packed_out, moments_out,
):
    nodes = state.shape[1]
    count = force_ghost.shape[1]
    square = squares_ref[0:1, :]
    pick = pick_ref[...]
    mass, stiff, twist, rate_stiff, rate_twist = [
        dense_ref[pl.ds(g * nodes, nodes), :] for g in range(5)
    ]
    mass_op = stacked_columns(mass)
    rest_ops = []
    for f in range(2):
        still = viscosity * stiff if f == 0 else rate_stiff
        turn = viscosity * twist if f == 0 else rate_twist
        rest_ops.append(jnp.concatenate([stacked_columns(still), stacked_columns(turn)], axis=0))
        image = (inverse_step * mass + still) * (1.0 / basis_scale)
        turn = turn * (1.0 / basis_scale)
        pairs = [halves(image), halves(turn)]
        pairs = pairs + [[dot(pick, item).astype(bf16) for item in pair] for pair in pairs]
        own_ref[f] = jnp.concatenate(
            [triple([item[:, :nodes] for item in pair]) for pair in pairs], axis=0
        )
        ghost_ref[f] = jnp.concatenate(
            [triple([item[:, nodes:] for item in pair]) for pair in pairs], axis=0
        )
        back = [jnp.transpose(item[:, nodes:]) for item in (image, turn)]
        back_ref[f] = jnp.concatenate([stacked_columns(item) for item in back], axis=0)
    for k in range(6):
        wide_force = jnp.concatenate([force[k], force_ghost[k]], axis=0)
        wide_state = jnp.concatenate([state[k], ghost_block(info, near, far, k)], axis=0)
        from_force = dot(mass_op, stacked_rows(wide_force))
        from_state = dot(rest_ops[k // 3], stacked_rows(wide_state))
        total = from_force - (from_state[:nodes] + square * from_state[nodes:])
        vector_out[k] = total
        full, packed = apply_own(own_ref, total, k, square, nodes, count)
        image_out[k] = full
        packed_out[k] = packed
        moments_out[k : k + 1, :] = jnp.sum(total * total, axis=0, keepdims=True)
    moments_out[6:8, :] = jnp.zeros((2, moments_out.shape[1]), f32)


def send_kernel(info, far, near, packed, ghost_ops, squares_ref, near_out, far_out):
    ghosts = near.shape[1]
    count = 2 * ghosts
    top = ghost_ops.shape[1] - 2 * count
    square = squares_ref[0:1, :]
    for k in range(6):
        image = dot(ghost_ops[k // 3, top:], stacked_rows(ghost_block(info, near, far, k)))
        total = packed[k] + image[:count] + square * image[count:]
        near_out[k] = total[:ghosts]
        far_out[k] = total[ghosts:]


def next_kernel(
    info, far, near, image, before, own, ghost_ops, squares_ref,
    vector_out, image_out, packed_out, moments_out,
):
    nodes = image.shape[1]
    count = 2 * near.shape[1]
    square = squares_ref[0:1, :]
    for k in range(6):
        part = dot(ghost_ops[k // 3, : 2 * nodes], stacked_rows(ghost_block(info, near, far, k)))
        total = image[k] + part[:nodes] + square * part[nodes:]
        vector_out[k] = total
        full, packed = apply_own(own, total, k, square, nodes, count)
        image_out[k] = full
        packed_out[k] = packed
        moments_out[k : k + 1, :] = jnp.sum(before[k] * total, axis=0, keepdims=True)
        moments_out[6 + k : 7 + k, :] = jnp.sum(total * total, axis=0, keepdims=True)
    moments_out[12:16, :] = jnp.zeros((4, moments_out.shape[1]), f32)


def last_kernel(
    info, far, near, image, before, own, ghost_ops, back_ops, squares_ref, first, second,
    vector_out, back_out, moments_out,
):
    nodes = image.shape[1]
    ghosts = near.shape[1]
    count = 2 * ghosts
    square = squares_ref[0:1, :]
    moments_out[0:6] = first[0:6]
    moments_out[6:18] = second[0:12]
    for k in range(6):
        part = dot(ghost_ops[k // 3, : 2 * nodes], stacked_rows(ghost_block(info, near, far, k)))
        total = image[k] + part[:nodes] + square * part[nodes:]
        vector_out[k] = total
        rows = stacked_rows(total)
        after = dot(own[k // 3, : 2 * nodes], rows)
        after = after[:nodes] + square * after[nodes:]
        back = dot(back_ops[k // 3], rows)
        back = back[:count] + square * back[count:]
        back_out[k] = back
        moments_out[18 + k : 19 + k, :] = jnp.sum(before[k] * total, axis=0, keepdims=True)
        moments_out[24 + k : 25 + k, :] = jnp.sum(total * total, axis=0, keepdims=True)
        moments_out[30 + k : 31 + k, :] = jnp.sum(after * total, axis=0, keepdims=True)
    moments_out[36:40, :] = jnp.zeros((4, moments_out.shape[1]), f32)


def join_kernel(far_weight, near_weight, info, far, near, back, moments, *rest):
    ghosts = near.shape[1]
    out = rest[-1]
    total = moments[...]
    for other in rest[:-1]:
        total = total + other[...]
    out[...] = total
    for k in range(6):
        distant = jnp.where(info[3:4, :] > 0.0, far[k], 0.0)
        crossing = far_weight * jnp.sum(distant * back[k, ghosts:], axis=0, keepdims=True)
        crossing += near_weight * jnp.sum(near[k] * back[k, :ghosts], axis=0, keepdims=True)
        out[30 + k : 31 + k, :] += crossing


def finish_kernel(moments, other, velocity, magnetic, first, second, third, velocity_out, magnetic_out):
    total = moments[...] + other[...]
    m0, m1, m2, m3, m4, m5 = [total[6 * j : 6 * j + 6, :] for j in range(6)]
    scale = basis_scale
    alpha0 = m0 / (scale * m1 + epsilon)
    q1 = -alpha0 * scale
    rr1 = m0 + 2.0 * q1 * m1 + q1 * q1 * m2
    beta0 = rr1 / (m0 + epsilon)
    p0 = 1.0 + beta0
    p1 = q1
    alpha1 = rr1 / (scale * (p0 * p0 * m1 + 2.0 * p0 * p1 * m2 + p1 * p1 * m3) + epsilon)
    step1 = alpha1 * scale
    r1 = q1 - step1 * p0
    r2 = -step1 * p1
    rr2 = m0 + r1 * r1 * m2 + r2 * r2 * m4 + 2.0 * (r1 * m1 + r2 * m2 + r1 * r2 * m3)
    beta1 = rr2 / (rr1 + epsilon)
    d0 = 1.0 + beta1 * p0
    d1 = r1 + beta1 * p1
    d2 = r2
    curve = d0 * d0 * m1 + d1 * d1 * m3 + d2 * d2 * m5
    curve = curve + 2.0 * (d0 * d1 * m2 + d0 * d2 * m3 + d1 * d2 * m4)
    alpha2 = rr2 / (scale * curve + epsilon)
    c0 = alpha0 + alpha1 * p0 + alpha2 * d0
    c1 = alpha1 * p1 + alpha2 * d1
    c2 = alpha2 * d2
    for k in range(6):
        source, out = (velocity, velocity_out) if k < 3 else (magnetic, magnetic_out)
        change = (
            c0[k : k + 1, :] * first[k] + c1[k : k + 1, :] * second[k] + c2[k : k + 1, :] * third[k]
        )
        out[k % 3] = source[k % 3] + jnp.transpose(change)


def call(kernel, outs, operands, scratch=(), flops=0, limit=24, aliases=None):
    single = not isinstance(outs, list)
    shapes = [outs] if single else outs
    moved = sum(math.prod(o.shape) * o.dtype.itemsize for o in list(operands) + shapes)
    return pl.pallas_call(
        kernel,
        out_shape=outs,
        in_specs=[VMEM] * len(operands),
        out_specs=VMEM if single else [VMEM] * len(outs),
        scratch_shapes=list(scratch),
        input_output_aliases=aliases or {},
        compiler_params=pltpu.CompilerParams(vmem_limit_bytes=limit * 1024 * 1024),
        cost_estimate=pl.CostEstimate(flops=flops, bytes_accessed=moved, transcendentals=0),
    )(*operands)


def shape(*sizes, dtype=f32):
    return jax.ShapeDtypeStruct(sizes, dtype)


def involution(pairs):
    return [edge for a, b in pairs for edge in ((a, b), (b, a))]


def local(runs, count, velocity, magnetic, mass_blocks, stiff_blocks, twist_blocks, diffusivity, conn, lists):
    coefs, nodes = velocity.shape[1:]
    ghosts = lists.shape[1]
    elements = conn.shape[1]
    both = 2 * ghosts
    planes = 2 * coefs
    index = lax.axis_index("mesh")
    odd = index % 2
    low_valid = (index > 0).astype(jnp.int32)
    high_valid = (index < count - 1).astype(jnp.int32)
    far_valid = jnp.where(odd == 1, high_valid, low_valid)
    row = lax.broadcasted_iota(jnp.int32, (8, coefs), 0)
    flags = jnp.where(row == 0, odd, jnp.where(row == 1, low_valid, jnp.where(row == 2, high_valid, far_valid)))
    info = flags.astype(f32)

    near_pairs = [(i, i ^ 1) for i in range(count)]
    far_pairs = []
    for run in range(runs):
        base = run * count
        far_pairs += involution([(base + i, base + i + 1) for i in range(1, count - 1, 2)])
    if runs % 2 == 0:
        for run in range(0, runs, 2):
            for end in (0, count - 1):
                far_pairs += involution([(run * count + end, (run + 1) * count + end)])

    def swap_near(value):
        return lax.ppermute(value, "mesh", near_pairs)

    def swap_far(value):
        return lax.ppermute(value, ("runs", "mesh"), far_pairs)

    plane_table, coef_table, rotation, squares = transform_tables(coefs)
    plane_table, coef_table = jnp.asarray(plane_table), jnp.asarray(coef_table)
    rotation, squares = jnp.asarray(rotation), jnp.asarray(squares)
    ends = shape(6, ghosts, coefs)
    whole = shape(6, nodes, coefs)
    packs = shape(6, both, coefs)

    def exchange(near, far):
        far = swap_far(far)
        return swap_near(near), far

    near, far, state, pick = call(
        pack_velocity_kernel,
        [ends, ends, whole, shape(both, nodes, dtype=bf16)],
        [info, velocity, conn],
    )
    near, far, state = call(
        pack_magnetic_kernel,
        [ends, ends, whole],
        [magnetic, pick, near, far, state],
        aliases={2: 0, 3: 1, 4: 2},
    )
    near_state, far_state = exchange(near, far)
    dense, mass_own, rest_own, mass_ghost, rest_ghost = call(
        build_kernel,
        [
            shape(5 * nodes, nodes + both),
            shape(both, 3 * nodes, dtype=bf16),
            shape(2, 2 * both, 3 * nodes, dtype=bf16),
            shape(both, 3 * both, dtype=bf16),
            shape(2, 2 * both, 3 * both, dtype=bf16),
        ],
        [info, pick, mass_blocks, stiff_blocks, twist_blocks, diffusivity.reshape(1, elements), conn, lists],
        scratch=[pltpu.VMEM((5 * nodes, 6 * elements), f32)],
        flops=1_000_000_000,
    )
    force, packed = call(
        force_kernel,
        [whole, packs],
        [state, plane_table, coef_table, rotation, squares, mass_own, rest_own],
        scratch=[
            pltpu.VMEM((6 * nodes, planes), f32),
            pltpu.VMEM((6 * nodes, planes), bf16),
            pltpu.VMEM((6 * nodes, planes), bf16),
        ],
        flops=2_000_000_000,
    )
    near, far, force_ghost = call(
        start_kernel,
        [ends, ends, packs],
        [info, far_state, near_state, packed, plane_table, coef_table, rotation, squares]
        + [mass_ghost, rest_ghost],
        scratch=[
            pltpu.VMEM((6 * both, planes), f32),
            pltpu.VMEM((6 * both, planes), bf16),
            pltpu.VMEM((6 * both, planes), bf16),
        ],
        flops=1_000_000_000,
    )
    near_now, far_now = exchange(near, far)
    own, ghost_ops, back_ops, vector0, image, packed, moments0 = call(
        first_kernel,
        [
            shape(2, 2 * nodes + 2 * both, 3 * nodes, dtype=bf16),
            shape(2, 2 * nodes + 2 * both, 3 * both, dtype=bf16),
            shape(2, 2 * both, 3 * nodes, dtype=bf16),
            whole,
            whole,
            packs,
            shape(8, coefs),
        ],
        [info, far_state, near_state, force_ghost, force, state, dense, pick, squares],
        flops=2_000_000_000,
    )
    near, far = call(
        send_kernel, [ends, ends], [info, far_now, near_now, packed, ghost_ops, squares], flops=100_000_000
    )
    near_next, far_next = exchange(near, far)
    vector1, image, packed, moments1 = call(
        next_kernel,
        [whole, whole, packs, shape(16, coefs)],
        [info, far_now, near_now, image, vector0, own, ghost_ops, squares],
        flops=2_000_000_000,
    )
    near, far = call(
        send_kernel, [ends, ends], [info, far_next, near_next, packed, ghost_ops, squares], flops=100_000_000
    )
    near_last, far_last = exchange(near, far)
    vector2, back, moments = call(
        last_kernel,
        [whole, packs, shape(40, coefs)],
        [info, far_next, near_next, image, vector1, own, ghost_ops, back_ops, squares]
        + [moments0, moments1],
        flops=2_000_000_000,
    )
    if count % 8 == 0 and count <= 16:
        joined = call(
            functools.partial(join_kernel, 2.0, 2.0),
            shape(40, coefs),
            [info, far_last, near_last, back, moments, swap_near(moments)],
        )
        target = (2, 0, 3, 1)
        lines = count // 4
        half = None
        for step in range(lines):
            pairs = [(i, ((i // 4) ^ step) * 4 + target[i % 4]) for i in range(count)]
            term = lax.ppermute(joined, "mesh", pairs)
            half = term if half is None else half + term
        other = swap_near(half)
    else:
        joined = call(
            functools.partial(join_kernel, 1.0, 1.0), shape(40, coefs), [info, far_last, near_last, back, moments]
        )
        half = lax.psum(joined, "mesh")
        other = jnp.zeros_like(half)
    new_velocity, new_magnetic = call(
        finish_kernel,
        [shape(3, coefs, nodes), shape(3, coefs, nodes)],
        [half, other, velocity, magnetic, vector0, vector1, vector2],
        flops=10_000_000,
    )
    return new_velocity, new_magnetic


def solution(mesh):
    in_specs = (
        P("runs", None, "mesh"),
        P("runs", None, "mesh"),
        P(None, None, "mesh"),
        P(None, None, "mesh"),
        P(None, None, "mesh"),
        P(("runs", "mesh")),
        P(None, "mesh"),
        P(None, "mesh"),
    )
    out_specs = (P("runs", None, "mesh"), P("runs", None, "mesh"))
    sizes = dict(mesh.shape)
    step = functools.partial(local, sizes["runs"], sizes["mesh"])
    return jax.shard_map(step, mesh=mesh, in_specs=in_specs, out_specs=out_specs, check_vma=False)
```

```python
import functools
import math

import jax
import jax.numpy as jnp
import ml_dtypes
import numpy as np
from jax import lax
from jax.experimental import pallas as pl
from jax.experimental.pallas import tpu as pltpu
from jax.sharding import PartitionSpec as P

viscosity = 2.0
inverse_step = 10.0
tilt_factor = 0.5
axial_factor = 1.0
lorentz_factor = 0.005
epsilon = 1e-06
basis_scale = 512.0

f32 = jnp.float32
bf16 = jnp.bfloat16
VMEM = pl.BlockSpec(memory_space=pltpu.VMEM)


def split_table(table):
    high = table.astype(np.float32).astype(ml_dtypes.bfloat16)
    low = (table - high.astype(np.float64)).astype(np.float32).astype(ml_dtypes.bfloat16)
    return high, low


def transform_tables(coefs):
    planes = 2 * coefs
    mode = np.arange(coefs) // 2
    turns = (np.arange(planes)[:, None] * mode[None, :]) % planes
    angles = 2.0 * math.pi / planes * turns
    inverse = np.where(np.arange(coefs)[None, :] % 2 == 0, np.cos(angles), np.sin(angles))
    weight = np.where(mode == 0, 1.0, 2.0) / planes
    to_planes = np.concatenate(split_table(inverse.T.copy()), axis=0)
    to_coefs = np.concatenate(split_table(inverse * weight[None, :]), axis=0)
    phi = 2.0 * math.pi / planes * np.arange(planes)
    rows = np.zeros((8, planes), np.float32)
    rows[0] = -2.0 * tilt_factor * np.cos(phi)
    rows[1] = 2.0 * tilt_factor * np.sin(phi)
    rows[2] = -2.0 * axial_factor
    squares = np.zeros((8, coefs), np.float32)
    squares[:] = (mode * mode).astype(np.float32)[None, :]
    return to_planes, to_coefs, rows, squares


def halves(value):
    high = value.astype(bf16)
    return high, (value - high.astype(f32)).astype(bf16)


def dot(first, second):
    return lax.dot_general(first, second, (((1,), (0,)), ((), ())), preferred_element_type=f32)


def dot_nt(first, second):
    return lax.dot_general(first, second, (((1,), (1,)), ((), ())), preferred_element_type=f32)


def stacked_columns(value):
    high, low = halves(value)
    return jnp.concatenate([high, low, high], axis=1)


def stacked_rows(value):
    high, low = halves(value)
    return jnp.concatenate([high, high, low], axis=0)


def iota(shape, dim):
    return lax.broadcasted_iota(jnp.int32, shape, dim)


def one_hot(conn, first, count):
    row = iota((count, conn.shape[1]), 0) + first
    return jnp.concatenate([(row == conn[a : a + 1, :]).astype(bf16) for a in range(6)], axis=1)


def element_sides(conn, nodes, ghosts):
    own = jnp.max((conn < nodes).astype(f32), axis=0, keepdims=True)
    low = jnp.max(((conn >= nodes) & (conn < nodes + ghosts)).astype(f32), axis=0, keepdims=True)
    high = jnp.max((conn >= nodes + ghosts).astype(f32), axis=0, keepdims=True)
    return own, low, high


def eight_rows(items):
    row = iota((8, items[0].shape[1]), 0)
    total = jnp.zeros(row.shape, f32)
    for i, item in enumerate(items):
        total = jnp.where(row == i, item, total)
    return total


def pack_matrix(conn, odd, nodes, ghosts):
    _, low, high = element_sides(conn, nodes, ghosts)
    sides = eight_rows([low, high]).astype(bf16)
    sides = jnp.concatenate([sides] * 6, axis=1)
    named = dot_nt(sides, one_hot(conn, 0, nodes))
    flags = jnp.where(named > 0.0, 1.0, 0.0)
    before = (iota((nodes, nodes), 0) < iota((nodes, nodes), 1)).astype(bf16)
    ranks = dot(flags.astype(bf16), before).astype(jnp.int32)
    rows = iota((2 * ghosts, nodes), 0)
    picks = []
    odd = odd[:, :nodes].astype(jnp.int32)
    for side in range(2):
        offset = (1 - odd) * ghosts if side == 0 else odd * ghosts
        rank = ranks[side : side + 1, :]
        rank = jnp.where((flags[side : side + 1, :] > 0.0) & (rank < ghosts), rank + offset, -1)
        picks.append(rows == rank)
    return jnp.where(picks[0] | picks[1], 1.0, 0.0).astype(bf16)


def to_row(column, size):
    eye = iota((size, size), 0) == iota((size, size), 1)
    return jnp.sum(jnp.where(eye, column, 0.0), axis=0, keepdims=True)


def to_column(row, size):
    eye = iota((size, size), 0) == iota((size, size), 1)
    return jnp.sum(jnp.where(eye, row, 0.0), axis=1, keepdims=True)


def slot_matrix(conn, lists, info, nodes, ghosts):
    own, _, _ = element_sides(conn, nodes, ghosts)
    slot = iota((2 * ghosts, conn.shape[1]), 0) + nodes
    active = jnp.zeros((2 * ghosts, conn.shape[1]), f32)
    for a in range(conn.shape[0]):
        active = jnp.maximum(active, jnp.where(slot == conn[a : a + 1, :], own, 0.0))
    active = jnp.max(active, axis=1, keepdims=True)
    parts = []
    for side in range(2):
        flag = active[side * ghosts : (side + 1) * ghosts]
        node_row = lists[side : side + 1, :].astype(f32)
        node_column = to_column(node_row, ghosts)
        smaller = (node_row < node_column).astype(f32) * to_row(flag, ghosts)
        rank = jnp.sum(smaller, axis=1, keepdims=True).astype(jnp.int32)
        odd = info[0:1, : 2 * ghosts].astype(jnp.int32)
        offset = (1 - odd) * ghosts if side == 0 else odd * ghosts
        live = (flag > 0.0) & (info[1 + side : 2 + side, : 2 * ghosts] > 0.0)
        rows = iota((ghosts, 2 * ghosts), 1)
        parts.append(jnp.where(live & (rows == rank + offset), 1.0, 0.0))
    return jnp.concatenate(parts, axis=0).astype(bf16)


def pack_field(field, at, pick, near_ref, far_ref, state_ref):
    ghosts = near_ref.shape[1]
    for k in range(3):
        block = jnp.transpose(field[k])
        state_ref[at + k] = block
        first, rest = halves(block)
        second = (block - first.astype(f32) - rest.astype(f32)).astype(bf16)
        packed = dot(pick, first) + dot(pick, rest) + dot(pick, second)
        near_ref[at + k] = packed[:ghosts]
        far_ref[at + k] = packed[ghosts:]


def pick_kernel(info, conn_ref, pick_ref):
    rows, nodes = pick_ref.shape
    pick_ref[...] = pack_matrix(conn_ref[...], info[0:1, :], nodes, rows // 2)


def pack_velocity_kernel(velocity, pick_ref, near_ref, far_ref, state_ref):
    pack_field(velocity, 0, pick_ref[...], near_ref, far_ref, state_ref)


def pack_magnetic_kernel(
    magnetic, pick_ref, near_in, far_in, state_in, near_ref, far_ref, state_ref
):
    pack_field(magnetic, 3, pick_ref[...], near_ref, far_ref, state_ref)


def to_planes(high, low, table):
    coefs = high.shape[1]
    return dot(high, table[:coefs]) + dot(low, table[:coefs]) + dot(high, table[coefs:])


def to_coefs(high, low, table):
    planes = high.shape[1]
    return dot(high, table[:planes]) + dot(low, table[:planes]) + dot(high, table[planes:])


def cross(a, b):
    return [
        a[1] * b[2] - a[2] * b[1],
        a[2] * b[0] - a[0] * b[2],
        a[0] * b[1] - a[1] * b[0],
    ]


def forcing(value, rows, planes_ref, coefs_ref, rotation_ref, phys_ref, high_ref, low_ref):
    planes = planes_ref.shape[1]
    high, low = halves(value)
    phys_ref[...] = to_planes(high, low, planes_ref)
    step_rows, step_lanes = 16, 256
    for row in range(0, rows, step_rows):
        for lane in range(0, planes, step_lanes):
            lanes = pl.ds(lane, step_lanes)
            u = [phys_ref[pl.ds(k * rows + row, step_rows), lanes] for k in range(3)]
            b = [phys_ref[pl.ds((3 + k) * rows + row, step_rows), lanes] for k in range(3)]
            turn = [rotation_ref[k : k + 1, lanes] for k in range(3)]
            induction = cross(u, b)
            twisted = cross(turn, u)
            lorentz = cross(b, induction)
            force = [twisted[k] - lorentz_factor * lorentz[k] for k in range(3)]
            for k, item in enumerate(force + induction):
                item_high, item_low = halves(item)
                at = pl.ds(k * rows + row, step_rows)
                high_ref[at, lanes] = item_high
                low_ref[at, lanes] = item_low
    return to_coefs(high_ref[...], low_ref[...], coefs_ref)


def triple(pair):
    return jnp.concatenate([pair[0], pair[1], pair[0]], axis=1)


def build_kernel(
    info, pick_ref, mass_ref, stiff_ref, twist_ref, rates_ref, conn_ref, lists_ref,
    dense_ref, mass_own_ref, rest_own_ref, mass_ghost_ref, rest_ghost_ref, z_ref,
):
    nodes = pick_ref.shape[1]
    elements = conn_ref.shape[1]
    ghosts = lists_ref.shape[1]
    count = 2 * ghosts
    conn = conn_ref[...]
    pick = pick_ref[...]
    remap = slot_matrix(conn, lists_ref[...], info, nodes, ghosts)
    rates = rates_ref[0:1, :]
    step = 16
    for row in range(0, nodes, step):
        number = iota((step, elements), 0) + row
        hits = [(number == conn[a : a + 1, :]).astype(f32) for a in range(6)]
        for g, block in enumerate((mass_ref, stiff_ref, twist_ref)):
            for b in range(6):
                total = hits[0] * block[0, b : b + 1, :]
                for a in range(1, 6):
                    total = total + hits[a] * block[a, b : b + 1, :]
                lanes = pl.ds(b * elements, elements)
                z_ref[pl.ds(g * nodes + row, step), lanes] = total
                if g > 0:
                    z_ref[pl.ds((g + 2) * nodes + row, step), lanes] = total * rates
    arrives = lax.dot_general(
        remap, one_hot(conn, nodes, count), (((0,), (0,)), ((), ())), preferred_element_type=f32
    )
    column = jnp.concatenate([one_hot(conn, 0, nodes), arrives.astype(bf16)], axis=0)
    z = z_ref[...]
    first, second = halves(z)
    third = (z - first.astype(f32) - second.astype(f32)).astype(bf16)
    dense = dot_nt(first, column) + dot_nt(second, column) + dot_nt(third, column)
    dense_ref[...] = dense
    high, low = halves(dense)
    pairs = []
    for g in range(5):
        rows = slice(g * nodes, (g + 1) * nodes)
        factor = viscosity if g in (1, 2) else 1.0
        pairs.append([(factor * dot(pick, item[rows])).astype(bf16) for item in (high, low)])

    def own_part(pair):
        return triple([item[:, :nodes] for item in pair])

    def ghost_part(pair):
        return triple([item[:, nodes:] for item in pair])

    mass_own_ref[...] = own_part(pairs[0])
    mass_ghost_ref[...] = ghost_part(pairs[0])
    for f in range(2):
        used = (pairs[1], pairs[2]) if f == 0 else (pairs[3], pairs[4])
        rest_own_ref[f] = jnp.concatenate([own_part(pair) for pair in used], axis=0)
        rest_ghost_ref[f] = jnp.concatenate([ghost_part(pair) for pair in used], axis=0)


def force_kernel(
    state, planes_ref, coefs_ref, rotation_ref, squares_ref, mass_own, rest_own,
    force_ref, packed_ref, phys_ref, high_ref, low_ref,
):
    nodes = state.shape[1]
    count = packed_ref.shape[1]
    value = state[...].reshape(6 * nodes, state.shape[2])
    force_ref[...] = forcing(
        value, nodes, planes_ref, coefs_ref, rotation_ref, phys_ref, high_ref, low_ref
    ).reshape(force_ref.shape)
    square = squares_ref[0:1, :]
    for k in range(6):
        from_force = dot(mass_own[...], stacked_rows(force_ref[k]))
        from_state = dot(rest_own[k // 3], stacked_rows(state[k]))
        packed_ref[k] = from_force - (from_state[:count] + square * from_state[count:])


def ghost_block(info, near, far, k):
    distant = jnp.where(info[3:4, :] > 0.0, far[k], 0.0)
    return jnp.concatenate([near[k], distant], axis=0)


def start_kernel(
    info, far, near, packed, planes_ref, coefs_ref, rotation_ref, squares_ref, mass_ghost, rest_ghost,
    near_out, far_out, force_out, phys_ref, high_ref, low_ref,
):
    ghosts = near.shape[1]
    count = 2 * ghosts
    blocks = [ghost_block(info, near, far, k) for k in range(6)]
    value = jnp.concatenate(blocks, axis=0)
    force = forcing(value, count, planes_ref, coefs_ref, rotation_ref, phys_ref, high_ref, low_ref)
    square = squares_ref[0:1, :]
    for k in range(6):
        item = force[k * count : (k + 1) * count]
        force_out[k] = item
        from_force = dot(mass_ghost[...], stacked_rows(item))
        from_state = dot(rest_ghost[k // 3], stacked_rows(blocks[k]))
        total = packed[k] + from_force - (from_state[:count] + square * from_state[count:])
        near_out[k] = total[:ghosts]
        far_out[k] = total[ghosts:]


def apply_own(own, value, k, square, nodes, count):
    image = dot(own[k // 3], stacked_rows(value))
    full = image[:nodes] + square * image[nodes : 2 * nodes]
    packed = image[2 * nodes : 2 * nodes + count] + square * image[2 * nodes + count :]
    return full, packed


def first_kernel(
    info, far, near, force_ghost, force, state, dense_ref, pick_ref, squares_ref,
    own_ref, ghost_ref, back_ref, vector_out, image_out, packed_out, moments_out,
):
    nodes = state.shape[1]
    count = force_ghost.shape[1]
    square = squares_ref[0:1, :]
    pick = pick_ref[...]
    mass, stiff, twist, rate_stiff, rate_twist = [
        dense_ref[pl.ds(g * nodes, nodes), :] for g in range(5)
    ]
    mass_op = stacked_columns(mass)
    rest_ops = []
    for f in range(2):
        still = viscosity * stiff if f == 0 else rate_stiff
        turn = viscosity * twist if f == 0 else rate_twist
        rest_ops.append(jnp.concatenate([stacked_columns(still), stacked_columns(turn)], axis=0))
        image = (inverse_step * mass + still) * (1.0 / basis_scale)
        turn = turn * (1.0 / basis_scale)
        pairs = [halves(image), halves(turn)]
        pairs = pairs + [[dot(pick, item).astype(bf16) for item in pair] for pair in pairs]
        own_ref[f] = jnp.concatenate(
            [triple([item[:, :nodes] for item in pair]) for pair in pairs], axis=0
        )
        ghost_ref[f] = jnp.concatenate(
            [triple([item[:, nodes:] for item in pair]) for pair in pairs], axis=0
        )
        back = [jnp.transpose(item[:, nodes:]) for item in (image, turn)]
        back_ref[f] = jnp.concatenate([stacked_columns(item) for item in back], axis=0)
    for k in range(6):
        wide_force = jnp.concatenate([force[k], force_ghost[k]], axis=0)
        wide_state = jnp.concatenate([state[k], ghost_block(info, near, far, k)], axis=0)
        from_force = dot(mass_op, stacked_rows(wide_force))
        from_state = dot(rest_ops[k // 3], stacked_rows(wide_state))
        total = from_force - (from_state[:nodes] + square * from_state[nodes:])
        vector_out[k] = total
        full, packed = apply_own(own_ref, total, k, square, nodes, count)
        image_out[k] = full
        packed_out[k] = packed
        moments_out[k : k + 1, :] = jnp.sum(total * total, axis=0, keepdims=True)
    moments_out[6:8, :] = jnp.zeros((2, moments_out.shape[1]), f32)


def send_kernel(info, far, near, packed, ghost_ops, squares_ref, near_out, far_out):
    ghosts = near.shape[1]
    count = 2 * ghosts
    top = ghost_ops.shape[1] - 2 * count
    square = squares_ref[0:1, :]
    for k in range(6):
        image = dot(ghost_ops[k // 3, top:], stacked_rows(ghost_block(info, near, far, k)))
        total = packed[k] + image[:count] + square * image[count:]
        near_out[k] = total[:ghosts]
        far_out[k] = total[ghosts:]


def combine(image, square):
    half = image.shape[0] // 2
    return image[:half] + square * image[half:]


def near_only(near):
    return stacked_rows(jnp.concatenate([near, jnp.zeros_like(near)], axis=0))


def far_only(info, far):
    distant = jnp.where(info[3:4, :] > 0.0, far, 0.0)
    return stacked_rows(jnp.concatenate([jnp.zeros_like(far), distant], axis=0))


def second_kernel(
    info, far, near, near_next, image, own, ghost_ops, squares_ref, vector_out, far_out, packed_near
):
    nodes = image.shape[1]
    ghosts = near.shape[1]
    square = squares_ref[0:1, :]
    for k in range(6):
        ops = ghost_ops[k // 3, : 2 * nodes]
        total = image[k] + combine(dot(ops, stacked_rows(ghost_block(info, near, far, k))), square)
        vector_out[k] = total
        packed = dot(own[k // 3, 2 * nodes :], stacked_rows(total))
        packed = combine(packed + dot(ghost_ops[k // 3, 2 * nodes :], near_only(near_next[k])), square)
        packed_near[k] = packed[:ghosts]
        far_out[k] = packed[ghosts:]


def spread_kernel(
    vector, before, near, own, ghost_ops, back_ops, squares_ref, image_out, back_out, moments_out
):
    nodes = vector.shape[1]
    ghosts = near.shape[1]
    square = squares_ref[0:1, :]
    for k in range(6):
        value = vector[k]
        rows = stacked_rows(value)
        image = dot(own[k // 3, : 2 * nodes], rows)
        image_out[k] = combine(image + dot(ghost_ops[k // 3, : 2 * nodes], near_only(near[k])), square)
        back_out[k] = combine(dot(back_ops[k // 3], rows), square)[ghosts:]
        moments_out[k : k + 1, :] = jnp.sum(before[k] * value, axis=0, keepdims=True)
        moments_out[6 + k : 7 + k, :] = jnp.sum(value * value, axis=0, keepdims=True)
    moments_out[12:16, :] = jnp.zeros((4, moments_out.shape[1]), f32)


def third_kernel(info, far, image, packed_near, ghost_ops, squares_ref, vector_out, near_out):
    nodes = image.shape[1]
    ghosts = far.shape[1]
    square = squares_ref[0:1, :]
    for k in range(6):
        part = dot(ghost_ops[k // 3], far_only(info, far[k]))
        vector_out[k] = image[k] + combine(part[: 2 * nodes], square)
        near_out[k] = packed_near[k] + combine(part[2 * nodes :], square)[:ghosts]


def last_kernel(
    vector, before, own, back_ops, squares_ref, first, second, back_out, moments_out
):
    nodes = vector.shape[1]
    square = squares_ref[0:1, :]
    moments_out[0:6] = first[0:6]
    moments_out[6:18] = second[0:12]
    for k in range(6):
        value = vector[k]
        rows = stacked_rows(value)
        after = combine(dot(own[k // 3, : 2 * nodes], rows), square)
        back_out[k] = combine(dot(back_ops[k // 3], rows), square)
        moments_out[18 + k : 19 + k, :] = jnp.sum(before[k] * value, axis=0, keepdims=True)
        moments_out[24 + k : 25 + k, :] = jnp.sum(value * value, axis=0, keepdims=True)
        moments_out[30 + k : 31 + k, :] = jnp.sum(after * value, axis=0, keepdims=True)
    moments_out[36:40, :] = jnp.zeros((4, moments_out.shape[1]), f32)


def join_kernel(far_weight, near_weight, info, far, sent, near, back, moments, *rest):
    ghosts = near.shape[1]
    out = rest[-1]
    total = moments[...]
    for other in rest[:-1]:
        total = total + other[...]
    out[...] = total
    for k in range(6):
        distant = jnp.where(info[3:4, :] > 0.0, far[k] + sent[k], 0.0)
        crossing = far_weight * jnp.sum(distant * back[k, ghosts:], axis=0, keepdims=True)
        crossing += near_weight * jnp.sum(near[k] * back[k, :ghosts], axis=0, keepdims=True)
        out[30 + k : 31 + k, :] += crossing


def finish_kernel(moments, other, velocity, magnetic, first, second, third, velocity_out, magnetic_out):
    total = moments[...] + other[...]
    m0, m1, m2, m3, m4, m5 = [total[6 * j : 6 * j + 6, :] for j in range(6)]
    scale = basis_scale
    alpha0 = m0 / (scale * m1 + epsilon)
    q1 = -alpha0 * scale
    rr1 = m0 + 2.0 * q1 * m1 + q1 * q1 * m2
    beta0 = rr1 / (m0 + epsilon)
    p0 = 1.0 + beta0
    p1 = q1
    alpha1 = rr1 / (scale * (p0 * p0 * m1 + 2.0 * p0 * p1 * m2 + p1 * p1 * m3) + epsilon)
    step1 = alpha1 * scale
    r1 = q1 - step1 * p0
    r2 = -step1 * p1
    rr2 = m0 + r1 * r1 * m2 + r2 * r2 * m4 + 2.0 * (r1 * m1 + r2 * m2 + r1 * r2 * m3)
    beta1 = rr2 / (rr1 + epsilon)
    d0 = 1.0 + beta1 * p0
    d1 = r1 + beta1 * p1
    d2 = r2
    curve = d0 * d0 * m1 + d1 * d1 * m3 + d2 * d2 * m5
    curve = curve + 2.0 * (d0 * d1 * m2 + d0 * d2 * m3 + d1 * d2 * m4)
    alpha2 = rr2 / (scale * curve + epsilon)
    c0 = alpha0 + alpha1 * p0 + alpha2 * d0
    c1 = alpha1 * p1 + alpha2 * d1
    c2 = alpha2 * d2
    for k in range(6):
        source, out = (velocity, velocity_out) if k < 3 else (magnetic, magnetic_out)
        change = (
            c0[k : k + 1, :] * first[k] + c1[k : k + 1, :] * second[k] + c2[k : k + 1, :] * third[k]
        )
        out[k % 3] = source[k % 3] + jnp.transpose(change)


def call(kernel, outs, operands, scratch=(), flops=0, limit=24, aliases=None, moved=None):
    single = not isinstance(outs, list)
    shapes = [outs] if single else outs
    moved = moved or sum(math.prod(o.shape) * o.dtype.itemsize for o in list(operands) + shapes)
    return pl.pallas_call(
        kernel,
        out_shape=outs,
        in_specs=[VMEM] * len(operands),
        out_specs=VMEM if single else [VMEM] * len(outs),
        scratch_shapes=list(scratch),
        input_output_aliases=aliases or {},
        compiler_params=pltpu.CompilerParams(vmem_limit_bytes=limit * 1024 * 1024),
        cost_estimate=pl.CostEstimate(flops=flops, bytes_accessed=moved, transcendentals=0),
    )(*operands)


def shape(*sizes, dtype=f32):
    return jax.ShapeDtypeStruct(sizes, dtype)


def involution(pairs):
    return [edge for a, b in pairs for edge in ((a, b), (b, a))]


def local(runs, count, velocity, magnetic, mass_blocks, stiff_blocks, twist_blocks, diffusivity, conn, lists):
    coefs, nodes = velocity.shape[1:]
    ghosts = lists.shape[1]
    elements = conn.shape[1]
    both = 2 * ghosts
    planes = 2 * coefs
    index = lax.axis_index("mesh")
    odd = index % 2
    low_valid = (index > 0).astype(jnp.int32)
    high_valid = (index < count - 1).astype(jnp.int32)
    far_valid = jnp.where(odd == 1, high_valid, low_valid)
    row = lax.broadcasted_iota(jnp.int32, (8, coefs), 0)
    flags = jnp.where(row == 0, odd, jnp.where(row == 1, low_valid, jnp.where(row == 2, high_valid, far_valid)))
    info = flags.astype(f32)

    near_pairs = [(i, i ^ 1) for i in range(count)]
    far_pairs = []
    for run in range(runs):
        base = run * count
        far_pairs += involution([(base + i, base + i + 1) for i in range(1, count - 1, 2)])
    if runs % 2 == 0:
        for run in range(0, runs, 2):
            for end in (0, count - 1):
                far_pairs += involution([(run * count + end, (run + 1) * count + end)])

    def swap_near(value):
        return lax.ppermute(value, "mesh", near_pairs)

    def swap_far(value):
        return lax.ppermute(value, ("runs", "mesh"), far_pairs)

    plane_table, coef_table, rotation, squares = transform_tables(coefs)
    plane_table, coef_table = jnp.asarray(plane_table), jnp.asarray(coef_table)
    rotation, squares = jnp.asarray(rotation), jnp.asarray(squares)
    ends = shape(6, ghosts, coefs)
    whole = shape(6, nodes, coefs)
    packs = shape(6, both, coefs)

    def swap_far_beside(value):
        return lax.ppermute(value, ("runs", "mesh"), far_pairs[::-1])

    def exchange(near, far):
        far = swap_far(far)
        return swap_near(near), far

    pick = call(pick_kernel, shape(both, nodes, dtype=bf16), [info, conn], flops=100_000_000, moved=1000)
    near, far, state = call(
        pack_velocity_kernel, [ends, ends, whole], [velocity, pick], flops=100_000_000, moved=1000
    )
    near, far, state = call(
        pack_magnetic_kernel,
        [ends, ends, whole],
        [magnetic, pick, near, far, state],
        aliases={2: 0, 3: 1, 4: 2},
        flops=100_000_000,
        moved=1000,
    )
    near_state, far_state = exchange(near, far)
    dense, mass_own, rest_own, mass_ghost, rest_ghost = call(
        build_kernel,
        [
            shape(5 * nodes, nodes + both),
            shape(both, 3 * nodes, dtype=bf16),
            shape(2, 2 * both, 3 * nodes, dtype=bf16),
            shape(both, 3 * both, dtype=bf16),
            shape(2, 2 * both, 3 * both, dtype=bf16),
        ],
        [info, pick, mass_blocks, stiff_blocks, twist_blocks, diffusivity.reshape(1, elements), conn, lists],
        scratch=[pltpu.VMEM((5 * nodes, 6 * elements), f32)],
        flops=1_000_000_000,
    )
    force, packed = call(
        force_kernel,
        [whole, packs],
        [state, plane_table, coef_table, rotation, squares, mass_own, rest_own],
        scratch=[
            pltpu.VMEM((6 * nodes, planes), f32),
            pltpu.VMEM((6 * nodes, planes), bf16),
            pltpu.VMEM((6 * nodes, planes), bf16),
        ],
        flops=2_000_000_000,
    )
    near, far, force_ghost = call(
        start_kernel,
        [ends, ends, packs],
        [info, far_state, near_state, packed, plane_table, coef_table, rotation, squares]
        + [mass_ghost, rest_ghost],
        scratch=[
            pltpu.VMEM((6 * both, planes), f32),
            pltpu.VMEM((6 * both, planes), bf16),
            pltpu.VMEM((6 * both, planes), bf16),
        ],
        flops=1_000_000_000,
    )
    near_now, far_now = exchange(near, far)
    own, ghost_ops, back_ops, vector0, image, packed, moments0 = call(
        first_kernel,
        [
            shape(2, 2 * nodes + 2 * both, 3 * nodes, dtype=bf16),
            shape(2, 2 * nodes + 2 * both, 3 * both, dtype=bf16),
            shape(2, 2 * both, 3 * nodes, dtype=bf16),
            whole,
            whole,
            packs,
            shape(8, coefs),
        ],
        [info, far_state, near_state, force_ghost, force, state, dense, pick, squares],
        flops=2_000_000_000,
    )
    near, far = call(
        send_kernel, [ends, ends], [info, far_now, near_now, packed, ghost_ops, squares], flops=100_000_000
    )
    near_next, far_next = exchange(near, far)
    vector1, far, packed_near = call(
        second_kernel,
        [whole, ends, ends],
        [info, far_now, near_now, near_next, image, own, ghost_ops, squares],
        flops=1_000_000_000,
    )
    far_last = swap_far_beside(far)
    image, back1, moments1 = call(
        spread_kernel,
        [whole, ends, shape(16, coefs)],
        [vector1, vector0, near_next, own, ghost_ops, back_ops, squares],
        flops=1_000_000_000,
    )
    vector2, near = call(
        third_kernel, [whole, ends], [info, far_next, image, packed_near, ghost_ops, squares], flops=500_000_000
    )
    near_last = swap_near(near)
    back, moments = call(
        last_kernel,
        [packs, shape(40, coefs)],
        [vector2, vector1, own, back_ops, squares, moments0, moments1],
        flops=1_000_000_000,
    )
    if count % 8 == 0 and count <= 16:
        joined = call(
            functools.partial(join_kernel, 2.0, 2.0),
            shape(40, coefs),
            [info, far_last, back1, near_last, back, moments, swap_near(moments)],
        )
        target = (2, 0, 3, 1)
        lines = count // 4
        half = None
        for step in range(lines):
            pairs = [(i, ((i // 4) ^ step) * 4 + target[i % 4]) for i in range(count)]
            term = lax.ppermute(joined, "mesh", pairs)
            half = term if half is None else half + term
        other = swap_near(half)
    else:
        joined = call(
            functools.partial(join_kernel, 1.0, 1.0), shape(40, coefs), [info, far_last, back1, near_last, back, moments]
        )
        half = lax.psum(joined, "mesh")
        other = jnp.zeros_like(half)
    new_velocity, new_magnetic = call(
        finish_kernel,
        [shape(3, coefs, nodes), shape(3, coefs, nodes)],
        [half, other, velocity, magnetic, vector0, vector1, vector2],
        flops=10_000_000,
    )
    return new_velocity, new_magnetic


def solution(mesh):
    in_specs = (
        P("runs", None, "mesh"),
        P("runs", None, "mesh"),
        P(None, None, "mesh"),
        P(None, None, "mesh"),
        P(None, None, "mesh"),
        P(("runs", "mesh")),
        P(None, "mesh"),
        P(None, "mesh"),
    )
    out_specs = (P("runs", None, "mesh"), P("runs", None, "mesh"))
    sizes = dict(mesh.shape)
    step = functools.partial(local, sizes["runs"], sizes["mesh"])
    return jax.shard_map(step, mesh=mesh, in_specs=in_specs, out_specs=out_specs, check_vma=False)
```

```python
import functools
import math

import jax
import jax.numpy as jnp
import ml_dtypes
import numpy as np
from jax import lax
from jax.experimental import pallas as pl
from jax.experimental.pallas import tpu as pltpu
from jax.sharding import PartitionSpec as P

viscosity = 2.0
inverse_step = 10.0
tilt_factor = 0.5
axial_factor = 1.0
lorentz_factor = 0.005
epsilon = 1e-06
basis_scale = 512.0

f32 = jnp.float32
bf16 = jnp.bfloat16
VMEM = pl.BlockSpec(memory_space=pltpu.VMEM)


def split_table(table):
    high = table.astype(np.float32).astype(ml_dtypes.bfloat16)
    low = (table - high.astype(np.float64)).astype(np.float32).astype(ml_dtypes.bfloat16)
    return high, low


def transform_tables(coefs):
    planes = 2 * coefs
    mode = np.arange(coefs) // 2
    turns = (np.arange(planes)[:, None] * mode[None, :]) % planes
    angles = 2.0 * math.pi / planes * turns
    inverse = np.where(np.arange(coefs)[None, :] % 2 == 0, np.cos(angles), np.sin(angles))
    weight = np.where(mode == 0, 1.0, 2.0) / planes
    to_planes = np.concatenate(split_table(inverse.T.copy()), axis=0)
    to_coefs = np.concatenate(split_table(inverse * weight[None, :]), axis=0)
    phi = 2.0 * math.pi / planes * np.arange(planes)
    rows = np.zeros((8, planes), np.float32)
    rows[0] = -2.0 * tilt_factor * np.cos(phi)
    rows[1] = 2.0 * tilt_factor * np.sin(phi)
    rows[2] = -2.0 * axial_factor
    squares = np.zeros((8, coefs), np.float32)
    squares[:] = (mode * mode).astype(np.float32)[None, :]
    return to_planes, to_coefs, rows, squares


def halves(value):
    high = value.astype(bf16)
    return high, (value - high.astype(f32)).astype(bf16)


def dot(first, second):
    return lax.dot_general(first, second, (((1,), (0,)), ((), ())), preferred_element_type=f32)


def dot_nt(first, second):
    return lax.dot_general(first, second, (((1,), (1,)), ((), ())), preferred_element_type=f32)


def stacked_columns(value):
    high, low = halves(value)
    return jnp.concatenate([high, low, high], axis=1)


def stacked_rows(value):
    high, low = halves(value)
    return jnp.concatenate([high, high, low], axis=0)


def iota(shape, dim):
    return lax.broadcasted_iota(jnp.int32, shape, dim)


def one_hot(conn, first, count):
    row = iota((count, conn.shape[1]), 0) + first
    return jnp.concatenate([(row == conn[a : a + 1, :]).astype(bf16) for a in range(6)], axis=1)


def element_sides(conn, nodes, ghosts):
    own = jnp.max((conn < nodes).astype(f32), axis=0, keepdims=True)
    low = jnp.max(((conn >= nodes) & (conn < nodes + ghosts)).astype(f32), axis=0, keepdims=True)
    high = jnp.max((conn >= nodes + ghosts).astype(f32), axis=0, keepdims=True)
    return own, low, high


def eight_rows(items):
    row = iota((8, items[0].shape[1]), 0)
    total = jnp.zeros(row.shape, f32)
    for i, item in enumerate(items):
        total = jnp.where(row == i, item, total)
    return total


def pack_matrix(conn, odd, nodes, ghosts):
    _, low, high = element_sides(conn, nodes, ghosts)
    sides = eight_rows([low, high]).astype(bf16)
    sides = jnp.concatenate([sides] * 6, axis=1)
    named = dot_nt(sides, one_hot(conn, 0, nodes))
    flags = jnp.where(named > 0.0, 1.0, 0.0)
    before = (iota((nodes, nodes), 0) < iota((nodes, nodes), 1)).astype(bf16)
    ranks = dot(flags.astype(bf16), before).astype(jnp.int32)
    rows = iota((2 * ghosts, nodes), 0)
    picks = []
    odd = odd[:, :nodes].astype(jnp.int32)
    for side in range(2):
        offset = (1 - odd) * ghosts if side == 0 else odd * ghosts
        rank = ranks[side : side + 1, :]
        rank = jnp.where((flags[side : side + 1, :] > 0.0) & (rank < ghosts), rank + offset, -1)
        picks.append(rows == rank)
    return jnp.where(picks[0] | picks[1], 1.0, 0.0).astype(bf16)


def to_row(column, size):
    eye = iota((size, size), 0) == iota((size, size), 1)
    return jnp.sum(jnp.where(eye, column, 0.0), axis=0, keepdims=True)


def to_column(row, size):
    eye = iota((size, size), 0) == iota((size, size), 1)
    return jnp.sum(jnp.where(eye, row, 0.0), axis=1, keepdims=True)


def slot_matrix(conn, lists, info, nodes, ghosts):
    own, _, _ = element_sides(conn, nodes, ghosts)
    slot = iota((2 * ghosts, conn.shape[1]), 0) + nodes
    active = jnp.zeros((2 * ghosts, conn.shape[1]), f32)
    for a in range(conn.shape[0]):
        active = jnp.maximum(active, jnp.where(slot == conn[a : a + 1, :], own, 0.0))
    active = jnp.max(active, axis=1, keepdims=True)
    parts = []
    for side in range(2):
        flag = active[side * ghosts : (side + 1) * ghosts]
        node_row = lists[side : side + 1, :].astype(f32)
        node_column = to_column(node_row, ghosts)
        smaller = (node_row < node_column).astype(f32) * to_row(flag, ghosts)
        rank = jnp.sum(smaller, axis=1, keepdims=True).astype(jnp.int32)
        odd = info[0:1, : 2 * ghosts].astype(jnp.int32)
        offset = (1 - odd) * ghosts if side == 0 else odd * ghosts
        live = (flag > 0.0) & (info[1 + side : 2 + side, : 2 * ghosts] > 0.0)
        rows = iota((ghosts, 2 * ghosts), 1)
        parts.append(jnp.where(live & (rows == rank + offset), 1.0, 0.0))
    return jnp.concatenate(parts, axis=0).astype(bf16)


def pack_field(field, at, pick, near_ref, far_ref, state_ref):
    ghosts = near_ref.shape[1]
    for k in range(3):
        block = jnp.transpose(field[k])
        state_ref[at + k] = block
        first, rest = halves(block)
        second = (block - first.astype(f32) - rest.astype(f32)).astype(bf16)
        packed = dot(pick, first) + dot(pick, rest) + dot(pick, second)
        near_ref[at + k] = packed[:ghosts]
        far_ref[at + k] = packed[ghosts:]


def pick_kernel(info, conn_ref, pick_ref):
    rows, nodes = pick_ref.shape
    pick_ref[...] = pack_matrix(conn_ref[...], info[0:1, :], nodes, rows // 2)


def pack_velocity_kernel(velocity, pick_ref, near_ref, far_ref, state_ref):
    pack_field(velocity, 0, pick_ref[...], near_ref, far_ref, state_ref)


def pack_magnetic_kernel(
    magnetic, pick_ref, near_in, far_in, state_in, near_ref, far_ref, state_ref
):
    pack_field(magnetic, 3, pick_ref[...], near_ref, far_ref, state_ref)


def cross(a, b):
    return [
        a[1] * b[2] - a[2] * b[1],
        a[2] * b[0] - a[0] * b[2],
        a[0] * b[1] - a[1] * b[0],
    ]


def forcing(value, rows, planes_ref, coefs_ref, rotation_ref):
    coefs = value.shape[1]
    planes = planes_ref.shape[1]
    high, low = halves(value)
    part = planes // 2
    total = None
    for first in range(0, planes, part):
        lanes = slice(first, first + part)
        table = planes_ref[:coefs, lanes]
        phys = dot(high, table) + dot(low, table) + dot(high, planes_ref[coefs:, lanes])
        u = [phys[k * rows : (k + 1) * rows] for k in range(3)]
        b = [phys[(3 + k) * rows : (4 + k) * rows] for k in range(3)]
        turn = [rotation_ref[k : k + 1, lanes] for k in range(3)]
        induction = cross(u, b)
        twisted = cross(turn, u)
        lorentz = cross(b, induction)
        force = [twisted[k] - lorentz_factor * lorentz[k] for k in range(3)]
        item_high, item_low = halves(jnp.concatenate(force + induction, axis=0))
        table = coefs_ref[lanes]
        term = dot(item_high, table) + dot(item_low, table)
        term = term + dot(item_high, coefs_ref[planes + first : planes + first + part])
        total = term if total is None else total + term
    return total


def triple(pair):
    return jnp.concatenate([pair[0], pair[1], pair[0]], axis=1)


def build_kernel(
    info, pick_ref, mass_ref, stiff_ref, twist_ref, rates_ref, conn_ref, lists_ref,
    dense_ref, mass_own_ref, rest_own_ref, mass_ghost_ref, rest_ghost_ref, z_ref,
):
    nodes = pick_ref.shape[1]
    elements = conn_ref.shape[1]
    ghosts = lists_ref.shape[1]
    count = 2 * ghosts
    conn = conn_ref[...]
    pick = pick_ref[...]
    remap = slot_matrix(conn, lists_ref[...], info, nodes, ghosts)
    rates = rates_ref[0:1, :]
    step = 16
    for row in range(0, nodes, step):
        number = iota((step, elements), 0) + row
        hits = [(number == conn[a : a + 1, :]).astype(f32) for a in range(6)]
        for g, block in enumerate((mass_ref, stiff_ref, twist_ref)):
            for b in range(6):
                total = hits[0] * block[0, b : b + 1, :]
                for a in range(1, 6):
                    total = total + hits[a] * block[a, b : b + 1, :]
                lanes = pl.ds(b * elements, elements)
                z_ref[pl.ds(g * nodes + row, step), lanes] = total
                if g > 0:
                    z_ref[pl.ds((g + 2) * nodes + row, step), lanes] = total * rates
    arrives = lax.dot_general(
        remap, one_hot(conn, nodes, count), (((0,), (0,)), ((), ())), preferred_element_type=f32
    )
    column = jnp.concatenate([one_hot(conn, 0, nodes), arrives.astype(bf16)], axis=0)
    z = z_ref[...]
    first, second = halves(z)
    third = (z - first.astype(f32) - second.astype(f32)).astype(bf16)
    dense = dot_nt(first, column) + dot_nt(second, column) + dot_nt(third, column)
    dense_ref[...] = dense
    high, low = halves(dense)
    pairs = []
    for g in range(5):
        rows = slice(g * nodes, (g + 1) * nodes)
        factor = viscosity if g in (1, 2) else 1.0
        pairs.append([(factor * dot(pick, item[rows])).astype(bf16) for item in (high, low)])

    def own_part(pair):
        return triple([item[:, :nodes] for item in pair])

    def ghost_part(pair):
        return triple([item[:, nodes:] for item in pair])

    mass_own_ref[...] = own_part(pairs[0])
    mass_ghost_ref[...] = ghost_part(pairs[0])
    for f in range(2):
        used = (pairs[1], pairs[2]) if f == 0 else (pairs[3], pairs[4])
        rest_own_ref[f] = jnp.concatenate([own_part(pair) for pair in used], axis=0)
        rest_ghost_ref[f] = jnp.concatenate([ghost_part(pair) for pair in used], axis=0)


def force_kernel(
    state, planes_ref, coefs_ref, rotation_ref, squares_ref, mass_own, rest_own,
    force_ref, packed_ref,
):
    nodes = state.shape[1]
    count = packed_ref.shape[1]
    value = state[...].reshape(6 * nodes, state.shape[2])
    force_ref[...] = forcing(
        value, nodes, planes_ref, coefs_ref, rotation_ref
    ).reshape(force_ref.shape)
    square = squares_ref[0:1, :]
    for k in range(6):
        from_force = dot(mass_own[...], stacked_rows(force_ref[k]))
        from_state = dot(rest_own[k // 3], stacked_rows(state[k]))
        packed_ref[k] = from_force - (from_state[:count] + square * from_state[count:])


def ghost_block(info, near, far, k):
    distant = jnp.where(info[3:4, :] > 0.0, far[k], 0.0)
    return jnp.concatenate([near[k], distant], axis=0)


def start_kernel(
    info, far, near, packed, planes_ref, coefs_ref, rotation_ref, squares_ref, mass_ghost, rest_ghost,
    near_out, far_out, force_out,
):
    ghosts = near.shape[1]
    count = 2 * ghosts
    blocks = [ghost_block(info, near, far, k) for k in range(6)]
    value = jnp.concatenate(blocks, axis=0)
    force = forcing(value, count, planes_ref, coefs_ref, rotation_ref)
    square = squares_ref[0:1, :]
    for k in range(6):
        item = force[k * count : (k + 1) * count]
        force_out[k] = item
        from_force = dot(mass_ghost[...], stacked_rows(item))
        from_state = dot(rest_ghost[k // 3], stacked_rows(blocks[k]))
        total = packed[k] + from_force - (from_state[:count] + square * from_state[count:])
        near_out[k] = total[:ghosts]
        far_out[k] = total[ghosts:]


def apply_own(own, value, k, square, nodes, count):
    image = dot(own[k // 3], stacked_rows(value))
    full = image[:nodes] + square * image[nodes : 2 * nodes]
    packed = image[2 * nodes : 2 * nodes + count] + square * image[2 * nodes + count :]
    return full, packed


def first_kernel(
    info, far, near, force_ghost, force, state, dense_ref, pick_ref, squares_ref,
    own_ref, ghost_ref, back_ref, vector_out, image_out, packed_out, moments_out,
):
    nodes = state.shape[1]
    count = force_ghost.shape[1]
    square = squares_ref[0:1, :]
    pick = pick_ref[...]
    mass, stiff, twist, rate_stiff, rate_twist = [
        dense_ref[pl.ds(g * nodes, nodes), :] for g in range(5)
    ]
    mass_op = stacked_columns(mass)
    rest_ops = []
    for f in range(2):
        still = viscosity * stiff if f == 0 else rate_stiff
        turn = viscosity * twist if f == 0 else rate_twist
        rest_ops.append(jnp.concatenate([stacked_columns(still), stacked_columns(turn)], axis=0))
        image = (inverse_step * mass + still) * (1.0 / basis_scale)
        turn = turn * (1.0 / basis_scale)
        pairs = [halves(image), halves(turn)]
        pairs = pairs + [[dot(pick, item).astype(bf16) for item in pair] for pair in pairs]
        own_ref[f] = jnp.concatenate(
            [triple([item[:, :nodes] for item in pair]) for pair in pairs], axis=0
        )
        ghost_ref[f] = jnp.concatenate(
            [triple([item[:, nodes:] for item in pair]) for pair in pairs], axis=0
        )
        back = [jnp.transpose(item[:, nodes:]) for item in (image, turn)]
        back_ref[f] = jnp.concatenate([stacked_columns(item) for item in back], axis=0)
    for k in range(6):
        wide_force = jnp.concatenate([force[k], force_ghost[k]], axis=0)
        wide_state = jnp.concatenate([state[k], ghost_block(info, near, far, k)], axis=0)
        from_force = dot(mass_op, stacked_rows(wide_force))
        from_state = dot(rest_ops[k // 3], stacked_rows(wide_state))
        total = from_force - (from_state[:nodes] + square * from_state[nodes:])
        vector_out[k] = total
        full, packed = apply_own(own_ref, total, k, square, nodes, count)
        image_out[k] = full
        packed_out[k] = packed
        moments_out[k : k + 1, :] = jnp.sum(total * total, axis=0, keepdims=True)
    moments_out[6:8, :] = jnp.zeros((2, moments_out.shape[1]), f32)


def send_kernel(info, far, near, packed, ghost_ops, squares_ref, near_out, far_out):
    ghosts = near.shape[1]
    count = 2 * ghosts
    top = ghost_ops.shape[1] - 2 * count
    square = squares_ref[0:1, :]
    for k in range(6):
        image = dot(ghost_ops[k // 3, top:], stacked_rows(ghost_block(info, near, far, k)))
        total = packed[k] + image[:count] + square * image[count:]
        near_out[k] = total[:ghosts]
        far_out[k] = total[ghosts:]


def combine(image, square):
    half = image.shape[0] // 2
    return image[:half] + square * image[half:]


def near_only(near):
    return stacked_rows(jnp.concatenate([near, jnp.zeros_like(near)], axis=0))


def far_only(info, far):
    distant = jnp.where(info[3:4, :] > 0.0, far, 0.0)
    return stacked_rows(jnp.concatenate([jnp.zeros_like(far), distant], axis=0))


def second_kernel(
    info, far, near, near_next, image, before, own, ghost_ops, back_ops, squares_ref,
    vector_out, far_out, packed_near, image_out, back_out, moments_out,
):
    nodes = image.shape[1]
    ghosts = near.shape[1]
    square = squares_ref[0:1, :]
    for k in range(6):
        ops = ghost_ops[k // 3, : 2 * nodes]
        total = image[k] + combine(dot(ops, stacked_rows(ghost_block(info, near, far, k))), square)
        vector_out[k] = total
        rows = stacked_rows(total)
        after = dot(own[k // 3], rows) + dot(ghost_ops[k // 3], near_only(near_next[k]))
        image_out[k] = combine(after[: 2 * nodes], square)
        packed = combine(after[2 * nodes :], square)
        packed_near[k] = packed[:ghosts]
        far_out[k] = packed[ghosts:]
        back_out[k] = combine(dot(back_ops[k // 3], rows), square)[ghosts:]
        moments_out[k : k + 1, :] = jnp.sum(before[k] * total, axis=0, keepdims=True)
        moments_out[6 + k : 7 + k, :] = jnp.sum(total * total, axis=0, keepdims=True)
    moments_out[12:16, :] = jnp.zeros((4, moments_out.shape[1]), f32)


def third_kernel(info, far, image, packed_near, ghost_ops, squares_ref, vector_out, near_out):
    nodes = image.shape[1]
    ghosts = far.shape[1]
    square = squares_ref[0:1, :]
    for k in range(6):
        part = dot(ghost_ops[k // 3], far_only(info, far[k]))
        vector_out[k] = image[k] + combine(part[: 2 * nodes], square)
        near_out[k] = packed_near[k] + combine(part[2 * nodes :], square)[:ghosts]


def last_kernel(
    vector, before, own, back_ops, squares_ref, first, second, back_out, moments_out
):
    nodes = vector.shape[1]
    square = squares_ref[0:1, :]
    moments_out[0:6] = first[0:6]
    moments_out[6:18] = second[0:12]
    for k in range(6):
        value = vector[k]
        rows = stacked_rows(value)
        after = combine(dot(own[k // 3, : 2 * nodes], rows), square)
        back_out[k] = combine(dot(back_ops[k // 3], rows), square)
        moments_out[18 + k : 19 + k, :] = jnp.sum(before[k] * value, axis=0, keepdims=True)
        moments_out[24 + k : 25 + k, :] = jnp.sum(value * value, axis=0, keepdims=True)
        moments_out[30 + k : 31 + k, :] = jnp.sum(after * value, axis=0, keepdims=True)
    moments_out[36:40, :] = jnp.zeros((4, moments_out.shape[1]), f32)


def join_kernel(far_weight, near_weight, info, far, sent, near, back, moments, *rest):
    ghosts = near.shape[1]
    out = rest[-1]
    total = moments[...]
    for other in rest[:-1]:
        total = total + other[...]
    out[...] = total
    for k in range(6):
        distant = jnp.where(info[3:4, :] > 0.0, far[k] + sent[k], 0.0)
        crossing = far_weight * jnp.sum(distant * back[k, ghosts:], axis=0, keepdims=True)
        crossing += near_weight * jnp.sum(near[k] * back[k, :ghosts], axis=0, keepdims=True)
        out[30 + k : 31 + k, :] += crossing


def finish_kernel(moments, other, velocity, magnetic, first, second, third, velocity_out, magnetic_out):
    total = moments[...] + other[...]
    m0, m1, m2, m3, m4, m5 = [total[6 * j : 6 * j + 6, :] for j in range(6)]
    scale = basis_scale
    alpha0 = m0 / (scale * m1 + epsilon)
    q1 = -alpha0 * scale
    rr1 = m0 + 2.0 * q1 * m1 + q1 * q1 * m2
    beta0 = rr1 / (m0 + epsilon)
    p0 = 1.0 + beta0
    p1 = q1
    alpha1 = rr1 / (scale * (p0 * p0 * m1 + 2.0 * p0 * p1 * m2 + p1 * p1 * m3) + epsilon)
    step1 = alpha1 * scale
    r1 = q1 - step1 * p0
    r2 = -step1 * p1
    rr2 = m0 + r1 * r1 * m2 + r2 * r2 * m4 + 2.0 * (r1 * m1 + r2 * m2 + r1 * r2 * m3)
    beta1 = rr2 / (rr1 + epsilon)
    d0 = 1.0 + beta1 * p0
    d1 = r1 + beta1 * p1
    d2 = r2
    curve = d0 * d0 * m1 + d1 * d1 * m3 + d2 * d2 * m5
    curve = curve + 2.0 * (d0 * d1 * m2 + d0 * d2 * m3 + d1 * d2 * m4)
    alpha2 = rr2 / (scale * curve + epsilon)
    c0 = alpha0 + alpha1 * p0 + alpha2 * d0
    c1 = alpha1 * p1 + alpha2 * d1
    c2 = alpha2 * d2
    for k in range(6):
        source, out = (velocity, velocity_out) if k < 3 else (magnetic, magnetic_out)
        change = (
            c0[k : k + 1, :] * first[k] + c1[k : k + 1, :] * second[k] + c2[k : k + 1, :] * third[k]
        )
        out[k % 3] = source[k % 3] + jnp.transpose(change)


def call(kernel, outs, operands, scratch=(), flops=0, limit=24, aliases=None, moved=None):
    single = not isinstance(outs, list)
    shapes = [outs] if single else outs
    moved = moved or sum(math.prod(o.shape) * o.dtype.itemsize for o in list(operands) + shapes)
    return pl.pallas_call(
        kernel,
        out_shape=outs,
        in_specs=[VMEM] * len(operands),
        out_specs=VMEM if single else [VMEM] * len(outs),
        scratch_shapes=list(scratch),
        input_output_aliases=aliases or {},
        compiler_params=pltpu.CompilerParams(vmem_limit_bytes=limit * 1024 * 1024),
        cost_estimate=pl.CostEstimate(flops=flops, bytes_accessed=moved, transcendentals=0),
    )(*operands)


def shape(*sizes, dtype=f32):
    return jax.ShapeDtypeStruct(sizes, dtype)


def involution(pairs):
    return [edge for a, b in pairs for edge in ((a, b), (b, a))]


def local(runs, count, velocity, magnetic, mass_blocks, stiff_blocks, twist_blocks, diffusivity, conn, lists):
    coefs, nodes = velocity.shape[1:]
    ghosts = lists.shape[1]
    elements = conn.shape[1]
    both = 2 * ghosts
    index = lax.axis_index("mesh")
    odd = index % 2
    low_valid = (index > 0).astype(jnp.int32)
    high_valid = (index < count - 1).astype(jnp.int32)
    far_valid = jnp.where(odd == 1, high_valid, low_valid)
    row = lax.broadcasted_iota(jnp.int32, (8, coefs), 0)
    flags = jnp.where(row == 0, odd, jnp.where(row == 1, low_valid, jnp.where(row == 2, high_valid, far_valid)))
    info = flags.astype(f32)

    near_pairs = [(i, i ^ 1) for i in range(count)]
    far_pairs = []
    for run in range(runs):
        base = run * count
        far_pairs += involution([(base + i, base + i + 1) for i in range(1, count - 1, 2)])
    if runs % 2 == 0:
        for run in range(0, runs, 2):
            for end in (0, count - 1):
                far_pairs += involution([(run * count + end, (run + 1) * count + end)])

    def swap_near(value):
        return lax.ppermute(value, "mesh", near_pairs)

    def swap_far(value):
        return lax.ppermute(value, ("runs", "mesh"), far_pairs)

    plane_table, coef_table, rotation, squares = transform_tables(coefs)
    plane_table, coef_table = jnp.asarray(plane_table), jnp.asarray(coef_table)
    rotation, squares = jnp.asarray(rotation), jnp.asarray(squares)
    ends = shape(6, ghosts, coefs)
    whole = shape(6, nodes, coefs)
    packs = shape(6, both, coefs)

    def swap_far_beside(value):
        return lax.ppermute(value, ("runs", "mesh"), far_pairs[::-1])

    def exchange(near, far):
        far = swap_far(far)
        return swap_near(near), far

    pick = call(pick_kernel, shape(both, nodes, dtype=bf16), [info, conn], flops=100_000_000, moved=1000)
    near, far, state = call(
        pack_velocity_kernel, [ends, ends, whole], [velocity, pick], flops=100_000_000, moved=1000
    )
    near, far, state = call(
        pack_magnetic_kernel,
        [ends, ends, whole],
        [magnetic, pick, near, far, state],
        aliases={2: 0, 3: 1, 4: 2},
        flops=100_000_000,
        moved=1000,
    )
    near_state, far_state = exchange(near, far)
    dense, mass_own, rest_own, mass_ghost, rest_ghost = call(
        build_kernel,
        [
            shape(5 * nodes, nodes + both),
            shape(both, 3 * nodes, dtype=bf16),
            shape(2, 2 * both, 3 * nodes, dtype=bf16),
            shape(both, 3 * both, dtype=bf16),
            shape(2, 2 * both, 3 * both, dtype=bf16),
        ],
        [info, pick, mass_blocks, stiff_blocks, twist_blocks, diffusivity.reshape(1, elements), conn, lists],
        scratch=[pltpu.VMEM((5 * nodes, 6 * elements), f32)],
        flops=1_000_000_000,
    )
    force, packed = call(
        force_kernel,
        [whole, packs],
        [state, plane_table, coef_table, rotation, squares, mass_own, rest_own],
        flops=2_000_000_000,
    )
    near, far, force_ghost = call(
        start_kernel,
        [ends, ends, packs],
        [info, far_state, near_state, packed, plane_table, coef_table, rotation, squares]
        + [mass_ghost, rest_ghost],
        flops=1_000_000_000,
    )
    near_now, far_now = exchange(near, far)
    own, ghost_ops, back_ops, vector0, image, packed, moments0 = call(
        first_kernel,
        [
            shape(2, 2 * nodes + 2 * both, 3 * nodes, dtype=bf16),
            shape(2, 2 * nodes + 2 * both, 3 * both, dtype=bf16),
            shape(2, 2 * both, 3 * nodes, dtype=bf16),
            whole,
            whole,
            packs,
            shape(8, coefs),
        ],
        [info, far_state, near_state, force_ghost, force, state, dense, pick, squares],
        flops=2_000_000_000,
    )
    near, far = call(
        send_kernel, [ends, ends], [info, far_now, near_now, packed, ghost_ops, squares], flops=100_000_000
    )
    near_next, far_next = exchange(near, far)
    vector1, far, packed_near, image, back1, moments1 = call(
        second_kernel,
        [whole, ends, ends, whole, ends, shape(16, coefs)],
        [info, far_now, near_now, near_next, image, vector0, own, ghost_ops, back_ops, squares],
        flops=1_000_000_000,
    )
    far_last = swap_far_beside(far)
    vector2, near = call(
        third_kernel, [whole, ends], [info, far_next, image, packed_near, ghost_ops, squares], flops=500_000_000
    )
    near_last = swap_near(near)
    back, moments = call(
        last_kernel,
        [packs, shape(40, coefs)],
        [vector2, vector1, own, back_ops, squares, moments0, moments1],
        flops=1_000_000_000,
    )
    if count % 8 == 0 and count <= 16:
        joined = call(
            functools.partial(join_kernel, 2.0, 2.0),
            shape(40, coefs),
            [info, far_last, back1, near_last, back, moments, swap_near(moments)],
        )
        target = (2, 0, 3, 1)
        lines = count // 4
        half = None
        for step in range(lines):
            pairs = [(i, ((i // 4) ^ step) * 4 + target[i % 4]) for i in range(count)]
            term = lax.ppermute(joined, "mesh", pairs)
            half = term if half is None else half + term
        other = swap_near(half)
    else:
        joined = call(
            functools.partial(join_kernel, 1.0, 1.0), shape(40, coefs), [info, far_last, back1, near_last, back, moments]
        )
        half = lax.psum(joined, "mesh")
        other = jnp.zeros_like(half)
    new_velocity, new_magnetic = call(
        finish_kernel,
        [shape(3, coefs, nodes), shape(3, coefs, nodes)],
        [half, other, velocity, magnetic, vector0, vector1, vector2],
        flops=10_000_000,
    )
    return new_velocity, new_magnetic


def solution(mesh):
    in_specs = (
        P("runs", None, "mesh"),
        P("runs", None, "mesh"),
        P(None, None, "mesh"),
        P(None, None, "mesh"),
        P(None, None, "mesh"),
        P(("runs", "mesh")),
        P(None, "mesh"),
        P(None, "mesh"),
    )
    out_specs = (P("runs", None, "mesh"), P("runs", None, "mesh"))
    sizes = dict(mesh.shape)
    step = functools.partial(local, sizes["runs"], sizes["mesh"])
    return jax.shard_map(step, mesh=mesh, in_specs=in_specs, out_specs=out_specs, check_vma=False)
```

```python
import functools
import math

import jax
import jax.numpy as jnp
import ml_dtypes
import numpy as np
from jax import lax
from jax.experimental import pallas as pl
from jax.experimental.pallas import tpu as pltpu
from jax.sharding import PartitionSpec as P

viscosity = 2.0
inverse_step = 10.0
tilt_factor = 0.5
axial_factor = 1.0
lorentz_factor = 0.005
epsilon = 1e-06
basis_scale = 512.0

f32 = jnp.float32
bf16 = jnp.bfloat16
VMEM = pl.BlockSpec(memory_space=pltpu.VMEM)


def split_table(table):
    high = table.astype(np.float32).astype(ml_dtypes.bfloat16)
    low = (table - high.astype(np.float64)).astype(np.float32).astype(ml_dtypes.bfloat16)
    return high, low


def transform_tables(coefs):
    planes = 2 * coefs
    mode = np.arange(coefs) // 2
    turns = (np.arange(planes)[:, None] * mode[None, :]) % planes
    angles = 2.0 * math.pi / planes * turns
    inverse = np.where(np.arange(coefs)[None, :] % 2 == 0, np.cos(angles), np.sin(angles))
    weight = np.where(mode == 0, 1.0, 2.0) / planes
    to_planes = np.concatenate(split_table(inverse.T.copy()), axis=0)
    to_coefs = np.concatenate(split_table(inverse * weight[None, :]), axis=0)
    phi = 2.0 * math.pi / planes * np.arange(planes)
    rows = np.zeros((8, planes), np.float32)
    rows[0] = -2.0 * tilt_factor * np.cos(phi)
    rows[1] = 2.0 * tilt_factor * np.sin(phi)
    rows[2] = -2.0 * axial_factor
    squares = np.zeros((8, coefs), np.float32)
    squares[:] = (mode * mode).astype(np.float32)[None, :]
    return to_planes, to_coefs, rows, squares


def halves(value):
    high = value.astype(bf16)
    return high, (value - high.astype(f32)).astype(bf16)


def dot(first, second):
    return lax.dot_general(first, second, (((1,), (0,)), ((), ())), preferred_element_type=f32)


def dot_nt(first, second):
    return lax.dot_general(first, second, (((1,), (1,)), ((), ())), preferred_element_type=f32)


def stacked_columns(value):
    high, low = halves(value)
    return jnp.concatenate([high, low, high], axis=1)


def stacked_rows(value):
    high, low = halves(value)
    return jnp.concatenate([high, high, low], axis=0)


def iota(shape, dim):
    return lax.broadcasted_iota(jnp.int32, shape, dim)


def one_hot(conn, first, count):
    row = iota((count, conn.shape[1]), 0) + first
    return jnp.concatenate([(row == conn[a : a + 1, :]).astype(bf16) for a in range(6)], axis=1)


def element_sides(conn, nodes, ghosts):
    own = jnp.max((conn < nodes).astype(f32), axis=0, keepdims=True)
    low = jnp.max(((conn >= nodes) & (conn < nodes + ghosts)).astype(f32), axis=0, keepdims=True)
    high = jnp.max((conn >= nodes + ghosts).astype(f32), axis=0, keepdims=True)
    return own, low, high


def eight_rows(items):
    row = iota((8, items[0].shape[1]), 0)
    total = jnp.zeros(row.shape, f32)
    for i, item in enumerate(items):
        total = jnp.where(row == i, item, total)
    return total


def pack_matrix(conn, odd, nodes, ghosts):
    _, low, high = element_sides(conn, nodes, ghosts)
    sides = eight_rows([low, high]).astype(bf16)
    sides = jnp.concatenate([sides] * 6, axis=1)
    named = dot_nt(sides, one_hot(conn, 0, nodes))
    flags = jnp.where(named > 0.0, 1.0, 0.0)
    before = (iota((nodes, nodes), 0) < iota((nodes, nodes), 1)).astype(bf16)
    ranks = dot(flags.astype(bf16), before).astype(jnp.int32)
    rows = iota((2 * ghosts, nodes), 0)
    picks = []
    odd = odd[:, :nodes].astype(jnp.int32)
    for side in range(2):
        offset = (1 - odd) * ghosts if side == 0 else odd * ghosts
        rank = ranks[side : side + 1, :]
        rank = jnp.where((flags[side : side + 1, :] > 0.0) & (rank < ghosts), rank + offset, -1)
        picks.append(rows == rank)
    return jnp.where(picks[0] | picks[1], 1.0, 0.0).astype(bf16)


def to_row(column, size):
    eye = iota((size, size), 0) == iota((size, size), 1)
    return jnp.sum(jnp.where(eye, column, 0.0), axis=0, keepdims=True)


def to_column(row, size):
    eye = iota((size, size), 0) == iota((size, size), 1)
    return jnp.sum(jnp.where(eye, row, 0.0), axis=1, keepdims=True)


def slot_matrix(conn, lists, info, nodes, ghosts):
    own, _, _ = element_sides(conn, nodes, ghosts)
    slot = iota((2 * ghosts, conn.shape[1]), 0) + nodes
    active = jnp.zeros((2 * ghosts, conn.shape[1]), f32)
    for a in range(conn.shape[0]):
        active = jnp.maximum(active, jnp.where(slot == conn[a : a + 1, :], own, 0.0))
    active = jnp.max(active, axis=1, keepdims=True)
    parts = []
    for side in range(2):
        flag = active[side * ghosts : (side + 1) * ghosts]
        node_row = lists[side : side + 1, :].astype(f32)
        node_column = to_column(node_row, ghosts)
        smaller = (node_row < node_column).astype(f32) * to_row(flag, ghosts)
        rank = jnp.sum(smaller, axis=1, keepdims=True).astype(jnp.int32)
        odd = info[0:1, : 2 * ghosts].astype(jnp.int32)
        offset = (1 - odd) * ghosts if side == 0 else odd * ghosts
        live = (flag > 0.0) & (info[1 + side : 2 + side, : 2 * ghosts] > 0.0)
        rows = iota((ghosts, 2 * ghosts), 1)
        parts.append(jnp.where(live & (rows == rank + offset), 1.0, 0.0))
    return jnp.concatenate(parts, axis=0).astype(bf16)


def pack_field(field, at, pick, near_ref, far_ref, state_ref):
    ghosts = near_ref.shape[1]
    for k in range(3):
        block = jnp.transpose(field[k])
        state_ref[at + k] = block
        first, rest = halves(block)
        second = (block - first.astype(f32) - rest.astype(f32)).astype(bf16)
        packed = dot(pick, first) + dot(pick, rest) + dot(pick, second)
        near_ref[at + k] = packed[:ghosts]
        far_ref[at + k] = packed[ghosts:]


def pick_kernel(info, conn_ref, pick_ref):
    rows, nodes = pick_ref.shape
    pick_ref[...] = pack_matrix(conn_ref[...], info[0:1, :], nodes, rows // 2)


def pack_velocity_kernel(velocity, pick_ref, near_ref, far_ref, state_ref):
    pack_field(velocity, 0, pick_ref[...], near_ref, far_ref, state_ref)


def pack_magnetic_kernel(
    magnetic, pick_ref, near_in, far_in, state_in, near_ref, far_ref, state_ref
):
    pack_field(magnetic, 3, pick_ref[...], near_ref, far_ref, state_ref)


def cross(a, b):
    return [
        a[1] * b[2] - a[2] * b[1],
        a[2] * b[0] - a[0] * b[2],
        a[0] * b[1] - a[1] * b[0],
    ]


def forcing(value, rows, planes_ref, coefs_ref, rotation_ref):
    coefs = value.shape[1]
    planes = planes_ref.shape[1]
    high, low = halves(value)
    part = planes // 2
    total = None
    for first in range(0, planes, part):
        lanes = slice(first, first + part)
        table = planes_ref[:coefs, lanes]
        phys = dot(high, table) + dot(low, table) + dot(high, planes_ref[coefs:, lanes])
        u = [phys[k * rows : (k + 1) * rows] for k in range(3)]
        b = [phys[(3 + k) * rows : (4 + k) * rows] for k in range(3)]
        turn = [rotation_ref[k : k + 1, lanes] for k in range(3)]
        induction = cross(u, b)
        twisted = cross(turn, u)
        lorentz = cross(b, induction)
        force = [twisted[k] - lorentz_factor * lorentz[k] for k in range(3)]
        item_high, item_low = halves(jnp.concatenate(force + induction, axis=0))
        table = coefs_ref[lanes]
        term = dot(item_high, table) + dot(item_low, table)
        term = term + dot(item_high, coefs_ref[planes + first : planes + first + part])
        total = term if total is None else total + term
    return total


def triple(pair):
    return jnp.concatenate([pair[0], pair[1], pair[0]], axis=1)


def build_kernel(
    info, pick_ref, mass_ref, stiff_ref, twist_ref, rates_ref, conn_ref, lists_ref,
    dense_ref, mass_own_ref, rest_own_ref, mass_ghost_ref, rest_ghost_ref, z_ref,
):
    nodes = pick_ref.shape[1]
    elements = conn_ref.shape[1]
    ghosts = lists_ref.shape[1]
    count = 2 * ghosts
    conn = conn_ref[...]
    pick = pick_ref[...]
    remap = slot_matrix(conn, lists_ref[...], info, nodes, ghosts)
    rates = rates_ref[0:1, :]
    step = 16
    for row in range(0, nodes, step):
        number = iota((step, elements), 0) + row
        hits = [(number == conn[a : a + 1, :]).astype(f32) for a in range(6)]
        for g, block in enumerate((mass_ref, stiff_ref, twist_ref)):
            for b in range(6):
                total = hits[0] * block[0, b : b + 1, :]
                for a in range(1, 6):
                    total = total + hits[a] * block[a, b : b + 1, :]
                lanes = pl.ds(b * elements, elements)
                z_ref[pl.ds(g * nodes + row, step), lanes] = total
                if g > 0:
                    z_ref[pl.ds((g + 2) * nodes + row, step), lanes] = total * rates
    arrives = lax.dot_general(
        remap, one_hot(conn, nodes, count), (((0,), (0,)), ((), ())), preferred_element_type=f32
    )
    column = jnp.concatenate([one_hot(conn, 0, nodes), arrives.astype(bf16)], axis=0)
    z = z_ref[...]
    first, second = halves(z)
    dense = dot_nt(first, column) + dot_nt(second, column)
    dense_ref[...] = dense
    high, low = halves(dense)
    pairs = []
    for g in range(5):
        rows = slice(g * nodes, (g + 1) * nodes)
        factor = viscosity if g in (1, 2) else 1.0
        pairs.append([(factor * dot(pick, item[rows])).astype(bf16) for item in (high, low)])

    def own_part(pair):
        return triple([item[:, :nodes] for item in pair])

    def ghost_part(pair):
        return triple([item[:, nodes:] for item in pair])

    mass_own_ref[...] = own_part(pairs[0])
    mass_ghost_ref[...] = ghost_part(pairs[0])
    for f in range(2):
        used = (pairs[1], pairs[2]) if f == 0 else (pairs[3], pairs[4])
        rest_own_ref[f] = jnp.concatenate([own_part(pair) for pair in used], axis=0)
        rest_ghost_ref[f] = jnp.concatenate([ghost_part(pair) for pair in used], axis=0)


def force_kernel(
    state, planes_ref, coefs_ref, rotation_ref, squares_ref, mass_own, rest_own,
    force_ref, packed_ref,
):
    nodes = state.shape[1]
    count = packed_ref.shape[1]
    value = state[...].reshape(6 * nodes, state.shape[2])
    force_ref[...] = forcing(
        value, nodes, planes_ref, coefs_ref, rotation_ref
    ).reshape(force_ref.shape)
    square = squares_ref[0:1, :]
    for k in range(6):
        from_force = dot(mass_own[...], stacked_rows(force_ref[k]))
        from_state = dot(rest_own[k // 3], stacked_rows(state[k]))
        packed_ref[k] = from_force - (from_state[:count] + square * from_state[count:])


def ghost_block(info, near, far, k):
    distant = jnp.where(info[3:4, :] > 0.0, far[k], 0.0)
    return jnp.concatenate([near[k], distant], axis=0)


def start_kernel(
    info, far, near, packed, planes_ref, coefs_ref, rotation_ref, squares_ref, mass_ghost, rest_ghost,
    near_out, far_out, force_out,
):
    ghosts = near.shape[1]
    count = 2 * ghosts
    blocks = [ghost_block(info, near, far, k) for k in range(6)]
    value = jnp.concatenate(blocks, axis=0)
    force = forcing(value, count, planes_ref, coefs_ref, rotation_ref)
    square = squares_ref[0:1, :]
    for k in range(6):
        item = force[k * count : (k + 1) * count]
        force_out[k] = item
        from_force = dot(mass_ghost[...], stacked_rows(item))
        from_state = dot(rest_ghost[k // 3], stacked_rows(blocks[k]))
        total = packed[k] + from_force - (from_state[:count] + square * from_state[count:])
        near_out[k] = total[:ghosts]
        far_out[k] = total[ghosts:]


def apply_own(own, value, k, square, nodes, count):
    image = dot(own[k // 3], stacked_rows(value))
    full = image[:nodes] + square * image[nodes : 2 * nodes]
    packed = image[2 * nodes : 2 * nodes + count] + square * image[2 * nodes + count :]
    return full, packed


def first_kernel(
    info, far, near, force_ghost, force, state, dense_ref, pick_ref, squares_ref,
    own_ref, ghost_ref, back_ref, vector_out, image_out, packed_out, moments_out,
):
    nodes = state.shape[1]
    count = force_ghost.shape[1]
    square = squares_ref[0:1, :]
    pick = pick_ref[...]
    mass, stiff, twist, rate_stiff, rate_twist = [
        dense_ref[pl.ds(g * nodes, nodes), :] for g in range(5)
    ]
    mass_op = stacked_columns(mass)
    rest_ops = []
    for f in range(2):
        still = viscosity * stiff if f == 0 else rate_stiff
        turn = viscosity * twist if f == 0 else rate_twist
        rest_ops.append(jnp.concatenate([stacked_columns(still), stacked_columns(turn)], axis=0))
        image = (inverse_step * mass + still) * (1.0 / basis_scale)
        turn = turn * (1.0 / basis_scale)
        pairs = [halves(image), halves(turn)]
        pairs = pairs + [[dot(pick, item).astype(bf16) for item in pair] for pair in pairs]
        own_ref[f] = jnp.concatenate(
            [triple([item[:, :nodes] for item in pair]) for pair in pairs], axis=0
        )
        ghost_ref[f] = jnp.concatenate(
            [triple([item[:, nodes:] for item in pair]) for pair in pairs], axis=0
        )
        back = [jnp.transpose(item[:, nodes:]) for item in (image, turn)]
        back_ref[f] = jnp.concatenate([stacked_columns(item) for item in back], axis=0)
    for k in range(6):
        wide_force = jnp.concatenate([force[k], force_ghost[k]], axis=0)
        wide_state = jnp.concatenate([state[k], ghost_block(info, near, far, k)], axis=0)
        from_force = dot(mass_op, stacked_rows(wide_force))
        from_state = dot(rest_ops[k // 3], stacked_rows(wide_state))
        total = from_force - (from_state[:nodes] + square * from_state[nodes:])
        vector_out[k] = total
        full, packed = apply_own(own_ref, total, k, square, nodes, count)
        image_out[k] = full
        packed_out[k] = packed
        moments_out[k : k + 1, :] = jnp.sum(total * total, axis=0, keepdims=True)
    moments_out[6:8, :] = jnp.zeros((2, moments_out.shape[1]), f32)


def send_kernel(info, far, near, packed, ghost_ops, squares_ref, near_out, far_out):
    ghosts = near.shape[1]
    count = 2 * ghosts
    top = ghost_ops.shape[1] - 2 * count
    square = squares_ref[0:1, :]
    for k in range(6):
        image = dot(ghost_ops[k // 3, top:], stacked_rows(ghost_block(info, near, far, k)))
        total = packed[k] + image[:count] + square * image[count:]
        near_out[k] = total[:ghosts]
        far_out[k] = total[ghosts:]


def combine(image, square):
    half = image.shape[0] // 2
    return image[:half] + square * image[half:]


def near_only(near):
    return stacked_rows(jnp.concatenate([near, jnp.zeros_like(near)], axis=0))


def far_only(info, far):
    distant = jnp.where(info[3:4, :] > 0.0, far, 0.0)
    return stacked_rows(jnp.concatenate([jnp.zeros_like(far), distant], axis=0))


def second_kernel(
    info, far, near, near_next, image, before, own, ghost_ops, back_ops, squares_ref,
    vector_out, far_out, packed_near, image_out, back_out, moments_out,
):
    nodes = image.shape[1]
    ghosts = near.shape[1]
    square = squares_ref[0:1, :]
    for k in range(6):
        ops = ghost_ops[k // 3, : 2 * nodes]
        total = image[k] + combine(dot(ops, stacked_rows(ghost_block(info, near, far, k))), square)
        vector_out[k] = total
        rows = stacked_rows(total)
        after = dot(own[k // 3], rows) + dot(ghost_ops[k // 3], near_only(near_next[k]))
        image_out[k] = combine(after[: 2 * nodes], square)
        packed = combine(after[2 * nodes :], square)
        packed_near[k] = packed[:ghosts]
        far_out[k] = packed[ghosts:]
        back_out[k] = combine(dot(back_ops[k // 3], rows), square)[ghosts:]
        moments_out[k : k + 1, :] = jnp.sum(before[k] * total, axis=0, keepdims=True)
        moments_out[6 + k : 7 + k, :] = jnp.sum(total * total, axis=0, keepdims=True)
    moments_out[12:16, :] = jnp.zeros((4, moments_out.shape[1]), f32)


def third_kernel(info, far, image, packed_near, ghost_ops, squares_ref, vector_out, near_out):
    nodes = image.shape[1]
    ghosts = far.shape[1]
    square = squares_ref[0:1, :]
    for k in range(6):
        part = dot(ghost_ops[k // 3], far_only(info, far[k]))
        vector_out[k] = image[k] + combine(part[: 2 * nodes], square)
        near_out[k] = packed_near[k] + combine(part[2 * nodes :], square)[:ghosts]


def last_kernel(
    vector, before, own, back_ops, squares_ref, first, second, back_out, moments_out
):
    nodes = vector.shape[1]
    square = squares_ref[0:1, :]
    moments_out[0:6] = first[0:6]
    moments_out[6:18] = second[0:12]
    for k in range(6):
        value = vector[k]
        rows = stacked_rows(value)
        after = combine(dot(own[k // 3, : 2 * nodes], rows), square)
        back_out[k] = combine(dot(back_ops[k // 3], rows), square)
        moments_out[18 + k : 19 + k, :] = jnp.sum(before[k] * value, axis=0, keepdims=True)
        moments_out[24 + k : 25 + k, :] = jnp.sum(value * value, axis=0, keepdims=True)
        moments_out[30 + k : 31 + k, :] = jnp.sum(after * value, axis=0, keepdims=True)
    moments_out[36:40, :] = jnp.zeros((4, moments_out.shape[1]), f32)


def join_kernel(far_weight, near_weight, info, far, sent, near, back, moments, *rest):
    ghosts = near.shape[1]
    out = rest[-1]
    half = out.shape[1]
    total = moments[...]
    for other in rest[:-1]:
        total = total + other[...]
    out[0:36] = total[:36, :half]
    out[36:72] = total[:36, half:]
    for k in range(6):
        distant = jnp.where(info[3:4, :] > 0.0, far[k] + sent[k], 0.0)
        crossing = far_weight * jnp.sum(distant * back[k, ghosts:], axis=0, keepdims=True)
        crossing += near_weight * jnp.sum(near[k] * back[k, :ghosts], axis=0, keepdims=True)
        out[30 + k : 31 + k, :] += crossing[:, :half]
        out[66 + k : 67 + k, :] += crossing[:, half:]


def finish_kernel(moments, other, velocity, magnetic, first, second, third, velocity_out, magnetic_out):
    total = moments[...] + other[...]
    total = jnp.concatenate([total[:36], total[36:]], axis=1)
    m0, m1, m2, m3, m4, m5 = [total[6 * j : 6 * j + 6, :] for j in range(6)]
    scale = basis_scale
    alpha0 = m0 / (scale * m1 + epsilon)
    q1 = -alpha0 * scale
    rr1 = m0 + 2.0 * q1 * m1 + q1 * q1 * m2
    beta0 = rr1 / (m0 + epsilon)
    p0 = 1.0 + beta0
    p1 = q1
    alpha1 = rr1 / (scale * (p0 * p0 * m1 + 2.0 * p0 * p1 * m2 + p1 * p1 * m3) + epsilon)
    step1 = alpha1 * scale
    r1 = q1 - step1 * p0
    r2 = -step1 * p1
    rr2 = m0 + r1 * r1 * m2 + r2 * r2 * m4 + 2.0 * (r1 * m1 + r2 * m2 + r1 * r2 * m3)
    beta1 = rr2 / (rr1 + epsilon)
    d0 = 1.0 + beta1 * p0
    d1 = r1 + beta1 * p1
    d2 = r2
    curve = d0 * d0 * m1 + d1 * d1 * m3 + d2 * d2 * m5
    curve = curve + 2.0 * (d0 * d1 * m2 + d0 * d2 * m3 + d1 * d2 * m4)
    alpha2 = rr2 / (scale * curve + epsilon)
    c0 = alpha0 + alpha1 * p0 + alpha2 * d0
    c1 = alpha1 * p1 + alpha2 * d1
    c2 = alpha2 * d2
    for k in range(6):
        source, out = (velocity, velocity_out) if k < 3 else (magnetic, magnetic_out)
        change = (
            c0[k : k + 1, :] * first[k] + c1[k : k + 1, :] * second[k] + c2[k : k + 1, :] * third[k]
        )
        out[k % 3] = source[k % 3] + jnp.transpose(change)


def call(kernel, outs, operands, scratch=(), flops=0, limit=24, aliases=None, moved=None):
    single = not isinstance(outs, list)
    shapes = [outs] if single else outs
    moved = moved or sum(math.prod(o.shape) * o.dtype.itemsize for o in list(operands) + shapes)
    return pl.pallas_call(
        kernel,
        out_shape=outs,
        in_specs=[VMEM] * len(operands),
        out_specs=VMEM if single else [VMEM] * len(outs),
        scratch_shapes=list(scratch),
        input_output_aliases=aliases or {},
        compiler_params=pltpu.CompilerParams(vmem_limit_bytes=limit * 1024 * 1024),
        cost_estimate=pl.CostEstimate(flops=flops, bytes_accessed=moved, transcendentals=0),
    )(*operands)


def shape(*sizes, dtype=f32):
    return jax.ShapeDtypeStruct(sizes, dtype)


def involution(pairs):
    return [edge for a, b in pairs for edge in ((a, b), (b, a))]


def local(runs, count, velocity, magnetic, mass_blocks, stiff_blocks, twist_blocks, diffusivity, conn, lists):
    coefs, nodes = velocity.shape[1:]
    ghosts = lists.shape[1]
    elements = conn.shape[1]
    both = 2 * ghosts
    index = lax.axis_index("mesh")
    odd = index % 2
    low_valid = (index > 0).astype(jnp.int32)
    high_valid = (index < count - 1).astype(jnp.int32)
    far_valid = jnp.where(odd == 1, high_valid, low_valid)
    row = lax.broadcasted_iota(jnp.int32, (8, coefs), 0)
    flags = jnp.where(row == 0, odd, jnp.where(row == 1, low_valid, jnp.where(row == 2, high_valid, far_valid)))
    info = flags.astype(f32)

    near_pairs = [(i, i ^ 1) for i in range(count)]
    far_pairs = []
    for run in range(runs):
        base = run * count
        far_pairs += involution([(base + i, base + i + 1) for i in range(1, count - 1, 2)])
    if runs % 2 == 0:
        for run in range(0, runs, 2):
            for end in (0, count - 1):
                far_pairs += involution([(run * count + end, (run + 1) * count + end)])

    def swap_near(value):
        return lax.ppermute(value, "mesh", near_pairs)

    def swap_far(value):
        return lax.ppermute(value, ("runs", "mesh"), far_pairs)

    plane_table, coef_table, rotation, squares = transform_tables(coefs)
    plane_table, coef_table = jnp.asarray(plane_table), jnp.asarray(coef_table)
    rotation, squares = jnp.asarray(rotation), jnp.asarray(squares)
    ends = shape(6, ghosts, coefs)
    whole = shape(6, nodes, coefs)
    packs = shape(6, both, coefs)

    def swap_far_beside(value):
        return lax.ppermute(value, ("runs", "mesh"), far_pairs[::-1])

    def exchange(near, far):
        far = swap_far(far)
        return swap_near(near), far

    pick = call(pick_kernel, shape(both, nodes, dtype=bf16), [info, conn], flops=100_000_000, moved=1000)
    near, far, state = call(
        pack_velocity_kernel, [ends, ends, whole], [velocity, pick], flops=100_000_000, moved=1000
    )
    near, far, state = call(
        pack_magnetic_kernel,
        [ends, ends, whole],
        [magnetic, pick, near, far, state],
        aliases={2: 0, 3: 1, 4: 2},
        flops=100_000_000,
        moved=1000,
    )
    near_state, far_state = exchange(near, far)
    dense, mass_own, rest_own, mass_ghost, rest_ghost = call(
        build_kernel,
        [
            shape(5 * nodes, nodes + both),
            shape(both, 3 * nodes, dtype=bf16),
            shape(2, 2 * both, 3 * nodes, dtype=bf16),
            shape(both, 3 * both, dtype=bf16),
            shape(2, 2 * both, 3 * both, dtype=bf16),
        ],
        [info, pick, mass_blocks, stiff_blocks, twist_blocks, diffusivity.reshape(1, elements), conn, lists],
        scratch=[pltpu.VMEM((5 * nodes, 6 * elements), f32)],
        flops=1_000_000_000,
    )
    force, packed = call(
        force_kernel,
        [whole, packs],
        [state, plane_table, coef_table, rotation, squares, mass_own, rest_own],
        flops=2_000_000_000,
    )
    near, far, force_ghost = call(
        start_kernel,
        [ends, ends, packs],
        [info, far_state, near_state, packed, plane_table, coef_table, rotation, squares]
        + [mass_ghost, rest_ghost],
        flops=1_000_000_000,
    )
    near_now, far_now = exchange(near, far)
    own, ghost_ops, back_ops, vector0, image, packed, moments0 = call(
        first_kernel,
        [
            shape(2, 2 * nodes + 2 * both, 3 * nodes, dtype=bf16),
            shape(2, 2 * nodes + 2 * both, 3 * both, dtype=bf16),
            shape(2, 2 * both, 3 * nodes, dtype=bf16),
            whole,
            whole,
            packs,
            shape(8, coefs),
        ],
        [info, far_state, near_state, force_ghost, force, state, dense, pick, squares],
        flops=2_000_000_000,
    )
    near, far = call(
        send_kernel, [ends, ends], [info, far_now, near_now, packed, ghost_ops, squares], flops=100_000_000
    )
    near_next, far_next = exchange(near, far)
    vector1, far, packed_near, image, back1, moments1 = call(
        second_kernel,
        [whole, ends, ends, whole, ends, shape(16, coefs)],
        [info, far_now, near_now, near_next, image, vector0, own, ghost_ops, back_ops, squares],
        flops=1_000_000_000,
    )
    far_last = swap_far_beside(far)
    vector2, near = call(
        third_kernel, [whole, ends], [info, far_next, image, packed_near, ghost_ops, squares], flops=500_000_000
    )
    near_last = swap_near(near)
    back, moments = call(
        last_kernel,
        [packs, shape(40, coefs)],
        [vector2, vector1, own, back_ops, squares, moments0, moments1],
        flops=1_000_000_000,
    )
    if count % 8 == 0 and count <= 16:
        joined = call(
            functools.partial(join_kernel, 2.0, 2.0),
            shape(72, coefs // 2),
            [info, far_last, back1, near_last, back, moments, swap_near(moments)],
        )
        target = (2, 0, 3, 1)
        lines = count // 4
        half = None
        for step in range(lines):
            pairs = [(i, ((i // 4) ^ step) * 4 + target[i % 4]) for i in range(count)]
            term = lax.ppermute(joined, "mesh", pairs)
            half = term if half is None else half + term
        other = swap_near(half)
    else:
        joined = call(
            functools.partial(join_kernel, 1.0, 1.0), shape(72, coefs // 2), [info, far_last, back1, near_last, back, moments]
        )
        half = lax.psum(joined, "mesh")
        other = jnp.zeros_like(half)
    new_velocity, new_magnetic = call(
        finish_kernel,
        [shape(3, coefs, nodes), shape(3, coefs, nodes)],
        [half, other, velocity, magnetic, vector0, vector1, vector2],
        flops=10_000_000,
    )
    return new_velocity, new_magnetic


def solution(mesh):
    in_specs = (
        P("runs", None, "mesh"),
        P("runs", None, "mesh"),
        P(None, None, "mesh"),
        P(None, None, "mesh"),
        P(None, None, "mesh"),
        P(("runs", "mesh")),
        P(None, "mesh"),
        P(None, "mesh"),
    )
    out_specs = (P("runs", None, "mesh"), P("runs", None, "mesh"))
    sizes = dict(mesh.shape)
    step = functools.partial(local, sizes["runs"], sizes["mesh"])
    return jax.shard_map(step, mesh=mesh, in_specs=in_specs, out_specs=out_specs, check_vma=False)
```

```python
import functools
import math

import jax
import jax.numpy as jnp
import ml_dtypes
import numpy as np
from jax import lax
from jax.experimental import pallas as pl
from jax.experimental.pallas import tpu as pltpu
from jax.sharding import PartitionSpec as P

viscosity = 2.0
inverse_step = 10.0
tilt_factor = 0.5
axial_factor = 1.0
lorentz_factor = 0.005
epsilon = 1e-06
basis_scale = 512.0
residual_scale = 2.0**-8

f32 = jnp.float32
bf16 = jnp.bfloat16
VMEM = pl.BlockSpec(memory_space=pltpu.VMEM)


def split_table(table):
    high = table.astype(np.float32).astype(ml_dtypes.bfloat16)
    low = (table - high.astype(np.float64)).astype(np.float32).astype(ml_dtypes.bfloat16)
    return high, low


def transform_tables(coefs):
    planes = 2 * coefs
    mode = np.arange(coefs) // 2
    turns = (np.arange(planes)[:, None] * mode[None, :]) % planes
    angles = 2.0 * math.pi / planes * turns
    inverse = np.where(np.arange(coefs)[None, :] % 2 == 0, np.cos(angles), np.sin(angles))
    weight = np.where(mode == 0, 1.0, 2.0) / planes
    to_planes = np.concatenate(split_table(inverse.T.copy()), axis=0)
    to_coefs = np.concatenate(split_table(inverse * weight[None, :]), axis=0)
    phi = 2.0 * math.pi / planes * np.arange(planes)
    rows = np.zeros((8, planes), np.float32)
    rows[0] = -2.0 * tilt_factor * np.cos(phi)
    rows[1] = 2.0 * tilt_factor * np.sin(phi)
    rows[2] = -2.0 * axial_factor
    squares = np.zeros((8, coefs), np.float32)
    squares[:] = (mode * mode).astype(np.float32)[None, :]
    return to_planes, to_coefs, rows, squares


def halves(value):
    high = value.astype(bf16)
    return high, (value - high.astype(f32)).astype(bf16)


def dot(first, second):
    return lax.dot_general(first, second, (((1,), (0,)), ((), ())), preferred_element_type=f32)


def dot_nt(first, second):
    return lax.dot_general(first, second, (((1,), (1,)), ((), ())), preferred_element_type=f32)


def stacked_columns(value):
    high, low = halves(value)
    return jnp.concatenate([high, low, high], axis=1)


def stacked_rows(value):
    high, low = halves(value)
    return jnp.concatenate([high, high, low], axis=0)


def iota(shape, dim):
    return lax.broadcasted_iota(jnp.int32, shape, dim)


def one_hot(conn, first, count):
    row = iota((count, conn.shape[1]), 0) + first
    return jnp.concatenate([(row == conn[a : a + 1, :]).astype(bf16) for a in range(6)], axis=1)


def element_sides(conn, nodes, ghosts):
    own = jnp.max((conn < nodes).astype(f32), axis=0, keepdims=True)
    low = jnp.max(((conn >= nodes) & (conn < nodes + ghosts)).astype(f32), axis=0, keepdims=True)
    high = jnp.max((conn >= nodes + ghosts).astype(f32), axis=0, keepdims=True)
    return own, low, high


def eight_rows(items):
    row = iota((8, items[0].shape[1]), 0)
    total = jnp.zeros(row.shape, f32)
    for i, item in enumerate(items):
        total = jnp.where(row == i, item, total)
    return total


def pack_matrix(conn, odd, nodes, ghosts):
    _, low, high = element_sides(conn, nodes, ghosts)
    sides = eight_rows([low, high]).astype(bf16)
    sides = jnp.concatenate([sides] * 6, axis=1)
    named = dot_nt(sides, one_hot(conn, 0, nodes))
    flags = jnp.where(named > 0.0, 1.0, 0.0)
    before = (iota((nodes, nodes), 0) < iota((nodes, nodes), 1)).astype(bf16)
    ranks = dot(flags.astype(bf16), before).astype(jnp.int32)
    rows = iota((2 * ghosts, nodes), 0)
    picks = []
    odd = odd[:, :nodes].astype(jnp.int32)
    for side in range(2):
        offset = (1 - odd) * ghosts if side == 0 else odd * ghosts
        rank = ranks[side : side + 1, :]
        rank = jnp.where((flags[side : side + 1, :] > 0.0) & (rank < ghosts), rank + offset, -1)
        picks.append(rows == rank)
    return jnp.where(picks[0] | picks[1], 1.0, 0.0).astype(bf16)


def to_row(column, size):
    eye = iota((size, size), 0) == iota((size, size), 1)
    return jnp.sum(jnp.where(eye, column, 0.0), axis=0, keepdims=True)


def to_column(row, size):
    eye = iota((size, size), 0) == iota((size, size), 1)
    return jnp.sum(jnp.where(eye, row, 0.0), axis=1, keepdims=True)


def slot_matrix(conn, lists, info, nodes, ghosts):
    own, _, _ = element_sides(conn, nodes, ghosts)
    slot = iota((2 * ghosts, conn.shape[1]), 0) + nodes
    active = jnp.zeros((2 * ghosts, conn.shape[1]), f32)
    for a in range(conn.shape[0]):
        active = jnp.maximum(active, jnp.where(slot == conn[a : a + 1, :], own, 0.0))
    active = jnp.max(active, axis=1, keepdims=True)
    parts = []
    for side in range(2):
        flag = active[side * ghosts : (side + 1) * ghosts]
        node_row = lists[side : side + 1, :].astype(f32)
        node_column = to_column(node_row, ghosts)
        smaller = (node_row < node_column).astype(f32) * to_row(flag, ghosts)
        rank = jnp.sum(smaller, axis=1, keepdims=True).astype(jnp.int32)
        odd = info[0:1, : 2 * ghosts].astype(jnp.int32)
        offset = (1 - odd) * ghosts if side == 0 else odd * ghosts
        live = (flag > 0.0) & (info[1 + side : 2 + side, : 2 * ghosts] > 0.0)
        rows = iota((ghosts, 2 * ghosts), 1)
        parts.append(jnp.where(live & (rows == rank + offset), 1.0, 0.0))
    return jnp.concatenate(parts, axis=0).astype(bf16)


def pack_field(field, at, pick, near_ref, far_ref, state_ref):
    ghosts = near_ref.shape[1]
    for k in range(3):
        block = jnp.transpose(field[k])
        state_ref[at + k] = block
        first, rest = halves(block)
        second = (block - first.astype(f32) - rest.astype(f32)).astype(bf16)
        packed = dot(pick, first) + dot(pick, rest) + dot(pick, second)
        near_ref[at + k] = packed[:ghosts]
        far_ref[at + k] = packed[ghosts:]


def pick_kernel(info, conn_ref, pick_ref):
    rows, nodes = pick_ref.shape
    pick_ref[...] = pack_matrix(conn_ref[...], info[0:1, :], nodes, rows // 2)


def pack_velocity_kernel(velocity, pick_ref, near_ref, far_ref, state_ref):
    pack_field(velocity, 0, pick_ref[...], near_ref, far_ref, state_ref)


def pack_magnetic_kernel(
    magnetic, pick_ref, near_in, far_in, state_in, near_ref, far_ref, state_ref
):
    pack_field(magnetic, 3, pick_ref[...], near_ref, far_ref, state_ref)


def cross(a, b):
    return [
        a[1] * b[2] - a[2] * b[1],
        a[2] * b[0] - a[0] * b[2],
        a[0] * b[1] - a[1] * b[0],
    ]


def forcing(value, rows, planes_ref, coefs_ref, rotation_ref):
    coefs = value.shape[1]
    planes = planes_ref.shape[1]
    high, low = halves(value)
    part = planes // 2
    total = None
    for first in range(0, planes, part):
        lanes = slice(first, first + part)
        table = planes_ref[:coefs, lanes]
        phys = dot(high, table) + dot(low, table) + dot(high, planes_ref[coefs:, lanes])
        u = [phys[k * rows : (k + 1) * rows] for k in range(3)]
        b = [phys[(3 + k) * rows : (4 + k) * rows] for k in range(3)]
        turn = [rotation_ref[k : k + 1, lanes] for k in range(3)]
        induction = cross(u, b)
        twisted = cross(turn, u)
        lorentz = cross(b, induction)
        force = [twisted[k] - lorentz_factor * lorentz[k] for k in range(3)]
        item_high, item_low = halves(jnp.concatenate(force + induction, axis=0))
        table = coefs_ref[lanes]
        term = dot(item_high, table) + dot(item_low, table)
        term = term + dot(item_high, coefs_ref[planes + first : planes + first + part])
        total = term if total is None else total + term
    return total


def triple(pair):
    return jnp.concatenate([pair[0], pair[1], pair[0]], axis=1)


def build_kernel(
    info, pick_ref, mass_ref, stiff_ref, twist_ref, rates_ref, conn_ref, lists_ref,
    dense_ref, mass_own_ref, rest_own_ref, mass_ghost_ref, rest_ghost_ref, z_ref,
):
    nodes = pick_ref.shape[1]
    elements = conn_ref.shape[1]
    ghosts = lists_ref.shape[1]
    count = 2 * ghosts
    conn = conn_ref[...]
    pick = pick_ref[...]
    remap = slot_matrix(conn, lists_ref[...], info, nodes, ghosts)
    rates = rates_ref[0:1, :]
    step = 16
    for row in range(0, nodes, step):
        number = iota((step, elements), 0) + row
        hits = [(number == conn[a : a + 1, :]).astype(f32) for a in range(6)]
        for g, block in enumerate((mass_ref, stiff_ref, twist_ref)):
            for b in range(6):
                total = hits[0] * block[0, b : b + 1, :]
                for a in range(1, 6):
                    total = total + hits[a] * block[a, b : b + 1, :]
                lanes = pl.ds(b * elements, elements)
                z_ref[pl.ds(g * nodes + row, step), lanes] = total
                if g > 0:
                    z_ref[pl.ds((g + 2) * nodes + row, step), lanes] = total * rates
    arrives = lax.dot_general(
        remap, one_hot(conn, nodes, count), (((0,), (0,)), ((), ())), preferred_element_type=f32
    )
    column = jnp.concatenate([one_hot(conn, 0, nodes), arrives.astype(bf16)], axis=0)
    z = z_ref[...]
    first, second = halves(z)
    dense = dot_nt(first, column) + dot_nt(second, column)
    dense_ref[...] = dense
    high, low = halves(dense)
    pairs = []
    for g in range(5):
        rows = slice(g * nodes, (g + 1) * nodes)
        factor = residual_scale * (viscosity if g in (1, 2) else 1.0)
        pairs.append([(factor * dot(pick, item[rows])).astype(bf16) for item in (high, low)])

    def own_part(pair):
        return triple([item[:, :nodes] for item in pair])

    def ghost_part(pair):
        return triple([item[:, nodes:] for item in pair])

    mass_own_ref[...] = own_part(pairs[0])
    mass_ghost_ref[...] = ghost_part(pairs[0])
    for f in range(2):
        used = (pairs[1], pairs[2]) if f == 0 else (pairs[3], pairs[4])
        rest_own_ref[f] = jnp.concatenate([own_part(pair) for pair in used], axis=0)
        rest_ghost_ref[f] = jnp.concatenate([ghost_part(pair) for pair in used], axis=0)


def force_kernel(
    state, planes_ref, coefs_ref, rotation_ref, squares_ref, mass_own, rest_own,
    force_ref, packed_ref,
):
    nodes = state.shape[1]
    count = packed_ref.shape[1]
    value = state[...].reshape(6 * nodes, state.shape[2])
    force_ref[...] = forcing(
        value, nodes, planes_ref, coefs_ref, rotation_ref
    ).reshape(force_ref.shape)
    square = squares_ref[0:1, :]
    for k in range(6):
        from_force = dot(mass_own[...], stacked_rows(force_ref[k]))
        from_state = dot(rest_own[k // 3], stacked_rows(state[k]))
        packed_ref[k] = from_force - (from_state[:count] + square * from_state[count:])


def ghost_block(info, near, far, k):
    distant = jnp.where(info[3:4, :] > 0.0, far[k], 0.0)
    return jnp.concatenate([near[k], distant], axis=0)


def start_kernel(
    info, far, near, packed, planes_ref, coefs_ref, rotation_ref, squares_ref, mass_ghost, rest_ghost,
    near_out, far_out, force_out,
):
    ghosts = near.shape[1]
    count = 2 * ghosts
    blocks = [ghost_block(info, near, far, k) for k in range(6)]
    value = jnp.concatenate(blocks, axis=0)
    force = forcing(value, count, planes_ref, coefs_ref, rotation_ref)
    square = squares_ref[0:1, :]
    for k in range(6):
        item = force[k * count : (k + 1) * count]
        force_out[k] = item
        from_force = dot(mass_ghost[...], stacked_rows(item))
        from_state = dot(rest_ghost[k // 3], stacked_rows(blocks[k]))
        total = packed[k] + from_force - (from_state[:count] + square * from_state[count:])
        near_out[k] = total[:ghosts]
        far_out[k] = total[ghosts:]


def apply_own(own, value, k, square, nodes, count):
    image = dot(own[k // 3], stacked_rows(value))
    full = image[:nodes] + square * image[nodes : 2 * nodes]
    packed = image[2 * nodes : 2 * nodes + count] + square * image[2 * nodes + count :]
    return full, packed


def first_kernel(
    info, far, near, force_ghost, force, state, dense_ref, pick_ref, squares_ref,
    own_ref, ghost_ref, back_ref, vector_out, image_out, packed_out, moments_out,
):
    nodes = state.shape[1]
    count = force_ghost.shape[1]
    square = squares_ref[0:1, :]
    pick = pick_ref[...]
    mass, stiff, twist, rate_stiff, rate_twist = [
        dense_ref[pl.ds(g * nodes, nodes), :] for g in range(5)
    ]
    mass_op = stacked_columns(residual_scale * mass)
    rest_ops = []
    for f in range(2):
        still = viscosity * stiff if f == 0 else rate_stiff
        turn = viscosity * twist if f == 0 else rate_twist
        rest = [stacked_columns(residual_scale * item) for item in (still, turn)]
        rest_ops.append(jnp.concatenate(rest, axis=0))
        image = (inverse_step * mass + still) * (1.0 / basis_scale)
        turn = turn * (1.0 / basis_scale)
        pairs = [halves(image), halves(turn)]
        pairs = pairs + [[dot(pick, item).astype(bf16) for item in pair] for pair in pairs]
        own_ref[f] = jnp.concatenate(
            [triple([item[:, :nodes] for item in pair]) for pair in pairs], axis=0
        )
        ghost_ref[f] = jnp.concatenate(
            [triple([item[:, nodes:] for item in pair]) for pair in pairs], axis=0
        )
        back = [jnp.transpose(item[:, nodes:]) for item in (image, turn)]
        back_ref[f] = jnp.concatenate([stacked_columns(item) for item in back], axis=0)
    for k in range(6):
        wide_force = jnp.concatenate([force[k], force_ghost[k]], axis=0)
        wide_state = jnp.concatenate([state[k], ghost_block(info, near, far, k)], axis=0)
        from_force = dot(mass_op, stacked_rows(wide_force))
        from_state = dot(rest_ops[k // 3], stacked_rows(wide_state))
        total = from_force - (from_state[:nodes] + square * from_state[nodes:])
        vector_out[k] = total
        full, packed = apply_own(own_ref, total, k, square, nodes, count)
        image_out[k] = full
        packed_out[k] = packed
        moments_out[k : k + 1, :] = jnp.sum(total * total, axis=0, keepdims=True)
    moments_out[6:8, :] = jnp.zeros((2, moments_out.shape[1]), f32)


def send_kernel(info, far, near, packed, ghost_ops, squares_ref, near_out, far_out):
    ghosts = near.shape[1]
    count = 2 * ghosts
    top = ghost_ops.shape[1] - 2 * count
    square = squares_ref[0:1, :]
    for k in range(6):
        image = dot(ghost_ops[k // 3, top:], stacked_rows(ghost_block(info, near, far, k)))
        total = packed[k] + image[:count] + square * image[count:]
        near_out[k] = total[:ghosts]
        far_out[k] = total[ghosts:]


def combine(image, square):
    half = image.shape[0] // 2
    return image[:half] + square * image[half:]


def near_only(near):
    return stacked_rows(jnp.concatenate([near, jnp.zeros_like(near)], axis=0))


def far_only(info, far):
    distant = jnp.where(info[3:4, :] > 0.0, far, 0.0)
    return stacked_rows(jnp.concatenate([jnp.zeros_like(far), distant], axis=0))


def second_kernel(
    info, far, near, near_next, image, before, own, ghost_ops, back_ops, squares_ref,
    vector_out, far_out, packed_near, image_out, back_out, moments_out,
):
    nodes = image.shape[1]
    ghosts = near.shape[1]
    square = squares_ref[0:1, :]
    for k in range(6):
        ops = ghost_ops[k // 3, : 2 * nodes]
        total = image[k] + combine(dot(ops, stacked_rows(ghost_block(info, near, far, k))), square)
        vector_out[k] = total
        rows = stacked_rows(total)
        after = dot(own[k // 3], rows) + dot(ghost_ops[k // 3], near_only(near_next[k]))
        image_out[k] = combine(after[: 2 * nodes], square)
        packed = combine(after[2 * nodes :], square)
        packed_near[k] = packed[:ghosts]
        far_out[k] = packed[ghosts:]
        back_out[k] = combine(dot(back_ops[k // 3], rows), square)[ghosts:]
        moments_out[k : k + 1, :] = jnp.sum(before[k] * total, axis=0, keepdims=True)
        moments_out[6 + k : 7 + k, :] = jnp.sum(total * total, axis=0, keepdims=True)
    moments_out[12:16, :] = jnp.zeros((4, moments_out.shape[1]), f32)


def third_kernel(info, far, image, packed_near, ghost_ops, squares_ref, vector_out, near_out):
    nodes = image.shape[1]
    ghosts = far.shape[1]
    square = squares_ref[0:1, :]
    for k in range(6):
        part = dot(ghost_ops[k // 3], far_only(info, far[k]))
        vector_out[k] = image[k] + combine(part[: 2 * nodes], square)
        near_out[k] = packed_near[k] + combine(part[2 * nodes :], square)[:ghosts]


def last_kernel(
    vector, before, own, back_ops, squares_ref, first, second, back_out, moments_out
):
    nodes = vector.shape[1]
    square = squares_ref[0:1, :]
    moments_out[0:6] = first[0:6]
    moments_out[6:18] = second[0:12]
    for k in range(6):
        value = vector[k]
        rows = stacked_rows(value)
        after = combine(dot(own[k // 3, : 2 * nodes], rows), square)
        back_out[k] = combine(dot(back_ops[k // 3], rows), square)
        moments_out[18 + k : 19 + k, :] = jnp.sum(before[k] * value, axis=0, keepdims=True)
        moments_out[24 + k : 25 + k, :] = jnp.sum(value * value, axis=0, keepdims=True)
        moments_out[30 + k : 31 + k, :] = jnp.sum(after * value, axis=0, keepdims=True)
    moments_out[36:40, :] = jnp.zeros((4, moments_out.shape[1]), f32)


def join_kernel(far_weight, near_weight, info, far, sent, near, back, moments, *rest):
    ghosts = near.shape[1]
    out = rest[-1]
    half = out.shape[1]
    total = moments[...]
    for other in rest[:-1]:
        total = total + other[...]
    out[0:36] = total[:36, :half]
    out[36:72] = total[:36, half:]
    for k in range(6):
        distant = jnp.where(info[3:4, :] > 0.0, far[k] + sent[k], 0.0)
        crossing = far_weight * jnp.sum(distant * back[k, ghosts:], axis=0, keepdims=True)
        crossing += near_weight * jnp.sum(near[k] * back[k, :ghosts], axis=0, keepdims=True)
        out[30 + k : 31 + k, :] += crossing[:, :half]
        out[66 + k : 67 + k, :] += crossing[:, half:]


def finish_kernel(moments, other, velocity, magnetic, first, second, third, velocity_out, magnetic_out):
    total = moments[...] + other[...]
    total = jnp.concatenate([total[:36], total[36:]], axis=1)
    m0, m1, m2, m3, m4, m5 = [total[6 * j : 6 * j + 6, :] for j in range(6)]
    scale = basis_scale
    small = epsilon * residual_scale * residual_scale
    alpha0 = m0 / (scale * m1 + small)
    q1 = -alpha0 * scale
    rr1 = jnp.maximum(m0 + 2.0 * q1 * m1 + q1 * q1 * m2, 0.0)
    beta0 = rr1 / (m0 + small)
    p0 = 1.0 + beta0
    p1 = q1
    alpha1 = rr1 / (scale * (p0 * p0 * m1 + 2.0 * p0 * p1 * m2 + p1 * p1 * m3) + small)
    step1 = alpha1 * scale
    r1 = q1 - step1 * p0
    r2 = -step1 * p1
    rr2 = m0 + r1 * r1 * m2 + r2 * r2 * m4 + 2.0 * (r1 * m1 + r2 * m2 + r1 * r2 * m3)
    rr2 = jnp.maximum(rr2, 0.0)
    beta1 = rr2 / (rr1 + small)
    d0 = 1.0 + beta1 * p0
    d1 = r1 + beta1 * p1
    d2 = r2
    curve = d0 * d0 * m1 + d1 * d1 * m3 + d2 * d2 * m5
    curve = curve + 2.0 * (d0 * d1 * m2 + d0 * d2 * m3 + d1 * d2 * m4)
    alpha2 = rr2 / (scale * curve + small)
    back = 1.0 / residual_scale
    c0 = back * (alpha0 + alpha1 * p0 + alpha2 * d0)
    c1 = back * (alpha1 * p1 + alpha2 * d1)
    c2 = back * (alpha2 * d2)
    for k in range(6):
        source, out = (velocity, velocity_out) if k < 3 else (magnetic, magnetic_out)
        change = (
            c0[k : k + 1, :] * first[k] + c1[k : k + 1, :] * second[k] + c2[k : k + 1, :] * third[k]
        )
        out[k % 3] = source[k % 3] + jnp.transpose(change)


def call(kernel, outs, operands, scratch=(), flops=0, limit=24, aliases=None, moved=None):
    single = not isinstance(outs, list)
    shapes = [outs] if single else outs
    moved = moved or sum(math.prod(o.shape) * o.dtype.itemsize for o in list(operands) + shapes)
    return pl.pallas_call(
        kernel,
        out_shape=outs,
        in_specs=[VMEM] * len(operands),
        out_specs=VMEM if single else [VMEM] * len(outs),
        scratch_shapes=list(scratch),
        input_output_aliases=aliases or {},
        compiler_params=pltpu.CompilerParams(vmem_limit_bytes=limit * 1024 * 1024),
        cost_estimate=pl.CostEstimate(flops=flops, bytes_accessed=moved, transcendentals=0),
    )(*operands)


def shape(*sizes, dtype=f32):
    return jax.ShapeDtypeStruct(sizes, dtype)


def involution(pairs):
    return [edge for a, b in pairs for edge in ((a, b), (b, a))]


def local(runs, count, velocity, magnetic, mass_blocks, stiff_blocks, twist_blocks, diffusivity, conn, lists):
    coefs, nodes = velocity.shape[1:]
    ghosts = lists.shape[1]
    elements = conn.shape[1]
    both = 2 * ghosts
    index = lax.axis_index("mesh")
    odd = index % 2
    low_valid = (index > 0).astype(jnp.int32)
    high_valid = (index < count - 1).astype(jnp.int32)
    far_valid = jnp.where(odd == 1, high_valid, low_valid)
    row = lax.broadcasted_iota(jnp.int32, (8, coefs), 0)
    flags = jnp.where(row == 0, odd, jnp.where(row == 1, low_valid, jnp.where(row == 2, high_valid, far_valid)))
    info = flags.astype(f32)

    near_pairs = [(i, i ^ 1) for i in range(count)]
    far_pairs = []
    for run in range(runs):
        base = run * count
        far_pairs += involution([(base + i, base + i + 1) for i in range(1, count - 1, 2)])
    if runs % 2 == 0:
        for run in range(0, runs, 2):
            for end in (0, count - 1):
                far_pairs += involution([(run * count + end, (run + 1) * count + end)])

    def swap_near(value):
        return lax.ppermute(value, "mesh", near_pairs)

    def swap_far(value):
        return lax.ppermute(value, ("runs", "mesh"), far_pairs)

    plane_table, coef_table, rotation, squares = transform_tables(coefs)
    plane_table, coef_table = jnp.asarray(plane_table), jnp.asarray(coef_table)
    rotation, squares = jnp.asarray(rotation), jnp.asarray(squares)
    ends = shape(6, ghosts, coefs)
    whole = shape(6, nodes, coefs)
    packs = shape(6, both, coefs)

    def swap_far_beside(value):
        return lax.ppermute(value, ("runs", "mesh"), far_pairs[::-1])

    def exchange(near, far):
        far = swap_far(far)
        return swap_near(near), far

    pick = call(pick_kernel, shape(both, nodes, dtype=bf16), [info, conn], flops=100_000_000, moved=1000)
    near, far, state = call(
        pack_velocity_kernel, [ends, ends, whole], [velocity, pick], flops=100_000_000, moved=1000
    )
    near, far, state = call(
        pack_magnetic_kernel,
        [ends, ends, whole],
        [magnetic, pick, near, far, state],
        aliases={2: 0, 3: 1, 4: 2},
        flops=100_000_000,
        moved=1000,
    )
    near_state, far_state = exchange(near, far)
    dense, mass_own, rest_own, mass_ghost, rest_ghost = call(
        build_kernel,
        [
            shape(5 * nodes, nodes + both),
            shape(both, 3 * nodes, dtype=bf16),
            shape(2, 2 * both, 3 * nodes, dtype=bf16),
            shape(both, 3 * both, dtype=bf16),
            shape(2, 2 * both, 3 * both, dtype=bf16),
        ],
        [info, pick, mass_blocks, stiff_blocks, twist_blocks, diffusivity.reshape(1, elements), conn, lists],
        scratch=[pltpu.VMEM((5 * nodes, 6 * elements), f32)],
        flops=1_000_000_000,
    )
    force, packed = call(
        force_kernel,
        [whole, packs],
        [state, plane_table, coef_table, rotation, squares, mass_own, rest_own],
        flops=2_000_000_000,
    )
    near, far, force_ghost = call(
        start_kernel,
        [ends, ends, packs],
        [info, far_state, near_state, packed, plane_table, coef_table, rotation, squares]
        + [mass_ghost, rest_ghost],
        flops=1_000_000_000,
    )
    near_now, far_now = exchange(near, far)
    own, ghost_ops, back_ops, vector0, image, packed, moments0 = call(
        first_kernel,
        [
            shape(2, 2 * nodes + 2 * both, 3 * nodes, dtype=bf16),
            shape(2, 2 * nodes + 2 * both, 3 * both, dtype=bf16),
            shape(2, 2 * both, 3 * nodes, dtype=bf16),
            whole,
            whole,
            packs,
            shape(8, coefs),
        ],
        [info, far_state, near_state, force_ghost, force, state, dense, pick, squares],
        flops=2_000_000_000,
    )
    near, far = call(
        send_kernel, [ends, ends], [info, far_now, near_now, packed, ghost_ops, squares], flops=100_000_000
    )
    near_next, far_next = exchange(near, far)
    vector1, far, packed_near, image, back1, moments1 = call(
        second_kernel,
        [whole, ends, ends, whole, ends, shape(16, coefs)],
        [info, far_now, near_now, near_next, image, vector0, own, ghost_ops, back_ops, squares],
        flops=1_000_000_000,
    )
    far_last = swap_far_beside(far)
    vector2, near = call(
        third_kernel, [whole, ends], [info, far_next, image, packed_near, ghost_ops, squares], flops=500_000_000
    )
    near_last = swap_near(near)
    back, moments = call(
        last_kernel,
        [packs, shape(40, coefs)],
        [vector2, vector1, own, back_ops, squares, moments0, moments1],
        flops=1_000_000_000,
    )
    if count % 8 == 0 and count <= 16:
        joined = call(
            functools.partial(join_kernel, 2.0, 2.0),
            shape(72, coefs // 2),
            [info, far_last, back1, near_last, back, moments, swap_near(moments)],
        )
        target = (2, 0, 3, 1)
        lines = count // 4
        half = None
        for step in range(lines):
            pairs = [(i, ((i // 4) ^ step) * 4 + target[i % 4]) for i in range(count)]
            term = lax.ppermute(joined, "mesh", pairs)
            half = term if half is None else half + term
        other = swap_near(half)
    else:
        joined = call(
            functools.partial(join_kernel, 1.0, 1.0), shape(72, coefs // 2), [info, far_last, back1, near_last, back, moments]
        )
        half = lax.psum(joined, "mesh")
        other = jnp.zeros_like(half)
    new_velocity, new_magnetic = call(
        finish_kernel,
        [shape(3, coefs, nodes), shape(3, coefs, nodes)],
        [half, other, velocity, magnetic, vector0, vector1, vector2],
        flops=10_000_000,
    )
    return new_velocity, new_magnetic


def solution(mesh):
    in_specs = (
        P("runs", None, "mesh"),
        P("runs", None, "mesh"),
        P(None, None, "mesh"),
        P(None, None, "mesh"),
        P(None, None, "mesh"),
        P(("runs", "mesh")),
        P(None, "mesh"),
        P(None, "mesh"),
    )
    out_specs = (P("runs", None, "mesh"), P("runs", None, "mesh"))
    sizes = dict(mesh.shape)
    step = functools.partial(local, sizes["runs"], sizes["mesh"])
    return jax.shard_map(step, mesh=mesh, in_specs=in_specs, out_specs=out_specs, check_vma=False)
```

```python
import functools
import math

import jax
import jax.numpy as jnp
import ml_dtypes
import numpy as np
from jax import lax
from jax.experimental import pallas as pl
from jax.experimental.pallas import tpu as pltpu
from jax.sharding import PartitionSpec as P

viscosity = 2.0
inverse_step = 10.0
tilt_factor = 0.5
axial_factor = 1.0
lorentz_factor = 0.005
epsilon = 1e-06
basis_scale = 512.0
residual_scale = 2.0**-8

f32 = jnp.float32
bf16 = jnp.bfloat16
VMEM = pl.BlockSpec(memory_space=pltpu.VMEM)


def split_table(table):
    high = table.astype(np.float32).astype(ml_dtypes.bfloat16)
    low = (table - high.astype(np.float64)).astype(np.float32).astype(ml_dtypes.bfloat16)
    return high, low


def transform_tables(coefs):
    planes = 2 * coefs
    mode = np.arange(coefs) // 2
    turns = (np.arange(planes)[:, None] * mode[None, :]) % planes
    angles = 2.0 * math.pi / planes * turns
    inverse = np.where(np.arange(coefs)[None, :] % 2 == 0, np.cos(angles), np.sin(angles))
    weight = np.where(mode == 0, 1.0, 2.0) / planes
    to_planes = np.concatenate(split_table(inverse.T.copy()), axis=0)
    to_coefs = np.concatenate(split_table(inverse * weight[None, :]), axis=0)
    phi = 2.0 * math.pi / planes * np.arange(planes)
    rows = np.zeros((8, planes), np.float32)
    rows[0] = -2.0 * tilt_factor * np.cos(phi)
    rows[1] = 2.0 * tilt_factor * np.sin(phi)
    rows[2] = -2.0 * axial_factor
    squares = np.zeros((8, coefs), np.float32)
    squares[:] = (mode * mode).astype(np.float32)[None, :]
    return to_planes, to_coefs, rows, squares


def halves(value):
    high = value.astype(bf16)
    return high, (value - high.astype(f32)).astype(bf16)


def dot(first, second):
    return lax.dot_general(first, second, (((1,), (0,)), ((), ())), preferred_element_type=f32)


def dot_nt(first, second):
    return lax.dot_general(first, second, (((1,), (1,)), ((), ())), preferred_element_type=f32)


def stacked_columns(value):
    high, low = halves(value)
    return jnp.concatenate([high, low, high], axis=1)


def stacked_rows(value):
    high, low = halves(value)
    return jnp.concatenate([high, high, low], axis=0)


def iota(shape, dim):
    return lax.broadcasted_iota(jnp.int32, shape, dim)


def one_hot(conn, first, count):
    row = iota((count, conn.shape[1]), 0) + first
    return jnp.concatenate([(row == conn[a : a + 1, :]).astype(bf16) for a in range(6)], axis=1)


def element_sides(conn, nodes, ghosts):
    own = jnp.max((conn < nodes).astype(f32), axis=0, keepdims=True)
    low = jnp.max(((conn >= nodes) & (conn < nodes + ghosts)).astype(f32), axis=0, keepdims=True)
    high = jnp.max((conn >= nodes + ghosts).astype(f32), axis=0, keepdims=True)
    return own, low, high


def eight_rows(items):
    row = iota((8, items[0].shape[1]), 0)
    total = jnp.zeros(row.shape, f32)
    for i, item in enumerate(items):
        total = jnp.where(row == i, item, total)
    return total


def pack_matrix(conn, odd, nodes, ghosts):
    _, low, high = element_sides(conn, nodes, ghosts)
    sides = eight_rows([low, high]).astype(bf16)
    sides = jnp.concatenate([sides] * 6, axis=1)
    named = dot_nt(sides, one_hot(conn, 0, nodes))
    flags = jnp.where(named > 0.0, 1.0, 0.0)
    before = (iota((nodes, nodes), 0) < iota((nodes, nodes), 1)).astype(bf16)
    ranks = dot(flags.astype(bf16), before).astype(jnp.int32)
    rows = iota((2 * ghosts, nodes), 0)
    picks = []
    odd = odd[:, :nodes].astype(jnp.int32)
    for side in range(2):
        offset = (1 - odd) * ghosts if side == 0 else odd * ghosts
        rank = ranks[side : side + 1, :]
        rank = jnp.where((flags[side : side + 1, :] > 0.0) & (rank < ghosts), rank + offset, -1)
        picks.append(rows == rank)
    return jnp.where(picks[0] | picks[1], 1.0, 0.0).astype(bf16)


def to_row(column, size):
    eye = iota((size, size), 0) == iota((size, size), 1)
    return jnp.sum(jnp.where(eye, column, 0.0), axis=0, keepdims=True)


def to_column(row, size):
    eye = iota((size, size), 0) == iota((size, size), 1)
    return jnp.sum(jnp.where(eye, row, 0.0), axis=1, keepdims=True)


def slot_matrix(conn, lists, info, nodes, ghosts):
    own, _, _ = element_sides(conn, nodes, ghosts)
    slot = iota((2 * ghosts, conn.shape[1]), 0) + nodes
    active = jnp.zeros((2 * ghosts, conn.shape[1]), f32)
    for a in range(conn.shape[0]):
        active = jnp.maximum(active, jnp.where(slot == conn[a : a + 1, :], own, 0.0))
    active = jnp.max(active, axis=1, keepdims=True)
    parts = []
    for side in range(2):
        flag = active[side * ghosts : (side + 1) * ghosts]
        node_row = lists[side : side + 1, :].astype(f32)
        node_column = to_column(node_row, ghosts)
        smaller = (node_row < node_column).astype(f32) * to_row(flag, ghosts)
        rank = jnp.sum(smaller, axis=1, keepdims=True).astype(jnp.int32)
        odd = info[0:1, : 2 * ghosts].astype(jnp.int32)
        offset = (1 - odd) * ghosts if side == 0 else odd * ghosts
        live = (flag > 0.0) & (info[1 + side : 2 + side, : 2 * ghosts] > 0.0)
        rows = iota((ghosts, 2 * ghosts), 1)
        parts.append(jnp.where(live & (rows == rank + offset), 1.0, 0.0))
    return jnp.concatenate(parts, axis=0).astype(bf16)


def pack_field(field, at, pick, near_ref, far_ref, state_ref):
    ghosts = near_ref.shape[1]
    for k in range(3):
        block = jnp.transpose(field[k])
        state_ref[at + k] = block
        first, rest = halves(block)
        second = (block - first.astype(f32) - rest.astype(f32)).astype(bf16)
        packed = dot(pick, first) + dot(pick, rest) + dot(pick, second)
        near_ref[at + k] = packed[:ghosts]
        far_ref[at + k] = packed[ghosts:]


def pick_kernel(info, conn_ref, pick_ref):
    rows, nodes = pick_ref.shape
    pick_ref[...] = pack_matrix(conn_ref[...], info[0:1, :], nodes, rows // 2)


def pack_velocity_kernel(velocity, pick_ref, near_ref, far_ref, state_ref):
    pack_field(velocity, 0, pick_ref[...], near_ref, far_ref, state_ref)


def pack_magnetic_kernel(
    magnetic, pick_ref, near_in, far_in, state_in, near_ref, far_ref, state_ref
):
    pack_field(magnetic, 3, pick_ref[...], near_ref, far_ref, state_ref)


def cross(a, b):
    return [
        a[1] * b[2] - a[2] * b[1],
        a[2] * b[0] - a[0] * b[2],
        a[0] * b[1] - a[1] * b[0],
    ]


def forcing(value, rows, planes_ref, coefs_ref, rotation_ref):
    coefs = value.shape[1]
    planes = planes_ref.shape[1]
    high, low = halves(value)
    part = planes // 2
    total = None
    for first in range(0, planes, part):
        lanes = slice(first, first + part)
        table = planes_ref[:coefs, lanes]
        phys = dot(high, table) + dot(low, table) + dot(high, planes_ref[coefs:, lanes])
        u = [phys[k * rows : (k + 1) * rows] for k in range(3)]
        b = [phys[(3 + k) * rows : (4 + k) * rows] for k in range(3)]
        turn = [rotation_ref[k : k + 1, lanes] for k in range(3)]
        induction = cross(u, b)
        twisted = cross(turn, u)
        lorentz = cross(b, induction)
        force = [twisted[k] - lorentz_factor * lorentz[k] for k in range(3)]
        item_high, item_low = halves(jnp.concatenate(force + induction, axis=0))
        table = coefs_ref[lanes]
        term = dot(item_high, table) + dot(item_low, table)
        term = term + dot(item_high, coefs_ref[planes + first : planes + first + part])
        total = term if total is None else total + term
    return total


def triple(pair):
    return jnp.concatenate([pair[0], pair[1], pair[0]], axis=1)


def build_kernel(
    info, pick_ref, mass_ref, stiff_ref, twist_ref, rates_ref, conn_ref, lists_ref, force, state, squares_ref,
    dense_ref, mass_ghost_ref, rest_ghost_ref, packed_ref, z_ref,
):
    nodes = pick_ref.shape[1]
    elements = conn_ref.shape[1]
    ghosts = lists_ref.shape[1]
    count = 2 * ghosts
    conn = conn_ref[...]
    pick = pick_ref[...]
    remap = slot_matrix(conn, lists_ref[...], info, nodes, ghosts)
    rates = rates_ref[0:1, :]
    step = 16
    for row in range(0, nodes, step):
        number = iota((step, elements), 0) + row
        hits = [(number == conn[a : a + 1, :]).astype(f32) for a in range(6)]
        for g, block in enumerate((mass_ref, stiff_ref, twist_ref)):
            for b in range(6):
                total = hits[0] * block[0, b : b + 1, :]
                for a in range(1, 6):
                    total = total + hits[a] * block[a, b : b + 1, :]
                lanes = pl.ds(b * elements, elements)
                z_ref[pl.ds(g * nodes + row, step), lanes] = total
                if g > 0:
                    z_ref[pl.ds((g + 2) * nodes + row, step), lanes] = total * rates
    arrives = lax.dot_general(
        remap, one_hot(conn, nodes, count), (((0,), (0,)), ((), ())), preferred_element_type=f32
    )
    column = jnp.concatenate([one_hot(conn, 0, nodes), arrives.astype(bf16)], axis=0)
    z = z_ref[...]
    first, second = halves(z)
    dense = dot_nt(first, column) + dot_nt(second, column)
    dense_ref[...] = dense
    high, low = halves(dense)
    pairs = []
    for g in range(5):
        rows = slice(g * nodes, (g + 1) * nodes)
        factor = residual_scale * (viscosity if g in (1, 2) else 1.0)
        pairs.append([(factor * dot(pick, item[rows])).astype(bf16) for item in (high, low)])

    def own_part(pair):
        return triple([item[:, :nodes] for item in pair])

    def ghost_part(pair):
        return triple([item[:, nodes:] for item in pair])

    mass_own = own_part(pairs[0])
    rest_own = []
    mass_ghost_ref[...] = ghost_part(pairs[0])
    for f in range(2):
        used = (pairs[1], pairs[2]) if f == 0 else (pairs[3], pairs[4])
        rest_own.append(jnp.concatenate([own_part(pair) for pair in used], axis=0))
        rest_ghost_ref[f] = jnp.concatenate([ghost_part(pair) for pair in used], axis=0)
    square = squares_ref[0:1, :]
    for k in range(6):
        from_force = dot(mass_own, stacked_rows(force[k]))
        from_state = dot(rest_own[k // 3], stacked_rows(state[k]))
        packed_ref[k] = from_force - (from_state[:count] + square * from_state[count:])


def force_kernel(state, planes_ref, coefs_ref, rotation_ref, force_ref):
    nodes = state.shape[1]
    value = state[...].reshape(6 * nodes, state.shape[2])
    force_ref[...] = forcing(value, nodes, planes_ref, coefs_ref, rotation_ref).reshape(force_ref.shape)


def ghost_block(info, near, far, k):
    distant = jnp.where(info[3:4, :] > 0.0, far[k], 0.0)
    return jnp.concatenate([near[k], distant], axis=0)


def start_kernel(
    info, far, near, packed, planes_ref, coefs_ref, rotation_ref, squares_ref, mass_ghost, rest_ghost,
    near_out, far_out, force_out,
):
    ghosts = near.shape[1]
    count = 2 * ghosts
    blocks = [ghost_block(info, near, far, k) for k in range(6)]
    value = jnp.concatenate(blocks, axis=0)
    force = forcing(value, count, planes_ref, coefs_ref, rotation_ref)
    square = squares_ref[0:1, :]
    for k in range(6):
        item = force[k * count : (k + 1) * count]
        force_out[k] = item
        from_force = dot(mass_ghost[...], stacked_rows(item))
        from_state = dot(rest_ghost[k // 3], stacked_rows(blocks[k]))
        total = packed[k] + from_force - (from_state[:count] + square * from_state[count:])
        near_out[k] = total[:ghosts]
        far_out[k] = total[ghosts:]


def apply_own(own, value, k, square, nodes, count):
    image = dot(own[k // 3], stacked_rows(value))
    full = image[:nodes] + square * image[nodes : 2 * nodes]
    packed = image[2 * nodes : 2 * nodes + count] + square * image[2 * nodes + count :]
    return full, packed


def first_kernel(
    info, far, near, force_ghost, force, state, dense_ref, pick_ref, squares_ref,
    own_ref, ghost_ref, back_ref, vector_out, image_out, packed_out, moments_out,
):
    nodes = state.shape[1]
    count = force_ghost.shape[1]
    square = squares_ref[0:1, :]
    pick = pick_ref[...]
    mass, stiff, twist, rate_stiff, rate_twist = [
        dense_ref[pl.ds(g * nodes, nodes), :] for g in range(5)
    ]
    mass_op = stacked_columns(residual_scale * mass)
    rest_ops = []
    for f in range(2):
        still = viscosity * stiff if f == 0 else rate_stiff
        turn = viscosity * twist if f == 0 else rate_twist
        rest = [stacked_columns(residual_scale * item) for item in (still, turn)]
        rest_ops.append(jnp.concatenate(rest, axis=0))
        image = (inverse_step * mass + still) * (1.0 / basis_scale)
        turn = turn * (1.0 / basis_scale)
        pairs = [halves(image), halves(turn)]
        pairs = pairs + [[dot(pick, item).astype(bf16) for item in pair] for pair in pairs]
        own_ref[f] = jnp.concatenate(
            [triple([item[:, :nodes] for item in pair]) for pair in pairs], axis=0
        )
        ghost_ref[f] = jnp.concatenate(
            [triple([item[:, nodes:] for item in pair]) for pair in pairs], axis=0
        )
        back = [jnp.transpose(item[:, nodes:]) for item in (image, turn)]
        back_ref[f] = jnp.concatenate([stacked_columns(item) for item in back], axis=0)
    for k in range(6):
        wide_force = jnp.concatenate([force[k], force_ghost[k]], axis=0)
        wide_state = jnp.concatenate([state[k], ghost_block(info, near, far, k)], axis=0)
        from_force = dot(mass_op, stacked_rows(wide_force))
        from_state = dot(rest_ops[k // 3], stacked_rows(wide_state))
        total = from_force - (from_state[:nodes] + square * from_state[nodes:])
        vector_out[k] = total
        full, packed = apply_own(own_ref, total, k, square, nodes, count)
        image_out[k] = full
        packed_out[k] = packed
        moments_out[k : k + 1, :] = jnp.sum(total * total, axis=0, keepdims=True)
    moments_out[6:8, :] = jnp.zeros((2, moments_out.shape[1]), f32)


def send_kernel(info, far, near, packed, ghost_ops, squares_ref, near_out, far_out):
    ghosts = near.shape[1]
    count = 2 * ghosts
    top = ghost_ops.shape[1] - 2 * count
    square = squares_ref[0:1, :]
    for k in range(6):
        image = dot(ghost_ops[k // 3, top:], stacked_rows(ghost_block(info, near, far, k)))
        total = packed[k] + image[:count] + square * image[count:]
        near_out[k] = total[:ghosts]
        far_out[k] = total[ghosts:]


def combine(image, square):
    half = image.shape[0] // 2
    return image[:half] + square * image[half:]


def near_only(near):
    return stacked_rows(jnp.concatenate([near, jnp.zeros_like(near)], axis=0))


def far_only(info, far):
    distant = jnp.where(info[3:4, :] > 0.0, far, 0.0)
    return stacked_rows(jnp.concatenate([jnp.zeros_like(far), distant], axis=0))


def second_kernel(
    info, far, near, near_next, image, before, own, ghost_ops, back_ops, squares_ref,
    vector_out, far_out, packed_near, image_out, back_out, moments_out,
):
    nodes = image.shape[1]
    ghosts = near.shape[1]
    square = squares_ref[0:1, :]
    for k in range(6):
        ops = ghost_ops[k // 3, : 2 * nodes]
        total = image[k] + combine(dot(ops, stacked_rows(ghost_block(info, near, far, k))), square)
        vector_out[k] = total
        rows = stacked_rows(total)
        after = dot(own[k // 3], rows) + dot(ghost_ops[k // 3], near_only(near_next[k]))
        image_out[k] = combine(after[: 2 * nodes], square)
        packed = combine(after[2 * nodes :], square)
        packed_near[k] = packed[:ghosts]
        far_out[k] = packed[ghosts:]
        back_out[k] = combine(dot(back_ops[k // 3], rows), square)[ghosts:]
        moments_out[k : k + 1, :] = jnp.sum(before[k] * total, axis=0, keepdims=True)
        moments_out[6 + k : 7 + k, :] = jnp.sum(total * total, axis=0, keepdims=True)
    moments_out[12:16, :] = jnp.zeros((4, moments_out.shape[1]), f32)


def third_kernel(info, far, image, packed_near, ghost_ops, squares_ref, vector_out, near_out):
    nodes = image.shape[1]
    ghosts = far.shape[1]
    square = squares_ref[0:1, :]
    for k in range(6):
        part = dot(ghost_ops[k // 3], far_only(info, far[k]))
        vector_out[k] = image[k] + combine(part[: 2 * nodes], square)
        near_out[k] = packed_near[k] + combine(part[2 * nodes :], square)[:ghosts]


def last_kernel(
    vector, before, own, back_ops, squares_ref, first, second, back_out, moments_out
):
    nodes = vector.shape[1]
    square = squares_ref[0:1, :]
    moments_out[0:6] = first[0:6]
    moments_out[6:18] = second[0:12]
    for k in range(6):
        value = vector[k]
        rows = stacked_rows(value)
        after = combine(dot(own[k // 3, : 2 * nodes], rows), square)
        back_out[k] = combine(dot(back_ops[k // 3], rows), square)
        moments_out[18 + k : 19 + k, :] = jnp.sum(before[k] * value, axis=0, keepdims=True)
        moments_out[24 + k : 25 + k, :] = jnp.sum(value * value, axis=0, keepdims=True)
        moments_out[30 + k : 31 + k, :] = jnp.sum(after * value, axis=0, keepdims=True)
    moments_out[36:40, :] = jnp.zeros((4, moments_out.shape[1]), f32)


def join_kernel(far_weight, near_weight, info, far, sent, near, back, moments, *rest):
    ghosts = near.shape[1]
    out = rest[-1]
    half = out.shape[1]
    total = moments[...]
    for other in rest[:-1]:
        total = total + other[...]
    out[0:36] = total[:36, :half]
    out[36:72] = total[:36, half:]
    for k in range(6):
        distant = jnp.where(info[3:4, :] > 0.0, far[k] + sent[k], 0.0)
        crossing = far_weight * jnp.sum(distant * back[k, ghosts:], axis=0, keepdims=True)
        crossing += near_weight * jnp.sum(near[k] * back[k, :ghosts], axis=0, keepdims=True)
        out[30 + k : 31 + k, :] += crossing[:, :half]
        out[66 + k : 67 + k, :] += crossing[:, half:]


def finish_kernel(moments, other, velocity, magnetic, first, second, third, velocity_out, magnetic_out):
    total = moments[...] + other[...]
    total = jnp.concatenate([total[:36], total[36:]], axis=1)
    m0, m1, m2, m3, m4, m5 = [total[6 * j : 6 * j + 6, :] for j in range(6)]
    scale = basis_scale
    small = epsilon * residual_scale * residual_scale
    alpha0 = m0 / (scale * m1 + small)
    q1 = -alpha0 * scale
    rr1 = jnp.maximum(m0 + 2.0 * q1 * m1 + q1 * q1 * m2, 0.0)
    beta0 = rr1 / (m0 + small)
    p0 = 1.0 + beta0
    p1 = q1
    alpha1 = rr1 / (scale * (p0 * p0 * m1 + 2.0 * p0 * p1 * m2 + p1 * p1 * m3) + small)
    step1 = alpha1 * scale
    r1 = q1 - step1 * p0
    r2 = -step1 * p1
    rr2 = m0 + r1 * r1 * m2 + r2 * r2 * m4 + 2.0 * (r1 * m1 + r2 * m2 + r1 * r2 * m3)
    rr2 = jnp.maximum(rr2, 0.0)
    beta1 = rr2 / (rr1 + small)
    d0 = 1.0 + beta1 * p0
    d1 = r1 + beta1 * p1
    d2 = r2
    curve = d0 * d0 * m1 + d1 * d1 * m3 + d2 * d2 * m5
    curve = curve + 2.0 * (d0 * d1 * m2 + d0 * d2 * m3 + d1 * d2 * m4)
    alpha2 = rr2 / (scale * curve + small)
    back = 1.0 / residual_scale
    c0 = back * (alpha0 + alpha1 * p0 + alpha2 * d0)
    c1 = back * (alpha1 * p1 + alpha2 * d1)
    c2 = back * (alpha2 * d2)
    for k in range(6):
        source, out = (velocity, velocity_out) if k < 3 else (magnetic, magnetic_out)
        change = (
            c0[k : k + 1, :] * first[k] + c1[k : k + 1, :] * second[k] + c2[k : k + 1, :] * third[k]
        )
        out[k % 3] = source[k % 3] + jnp.transpose(change)


def call(kernel, outs, operands, scratch=(), flops=0, limit=24, aliases=None, moved=None):
    single = not isinstance(outs, list)
    shapes = [outs] if single else outs
    moved = moved or sum(math.prod(o.shape) * o.dtype.itemsize for o in list(operands) + shapes)
    return pl.pallas_call(
        kernel,
        out_shape=outs,
        in_specs=[VMEM] * len(operands),
        out_specs=VMEM if single else [VMEM] * len(outs),
        scratch_shapes=list(scratch),
        input_output_aliases=aliases or {},
        compiler_params=pltpu.CompilerParams(vmem_limit_bytes=limit * 1024 * 1024),
        cost_estimate=pl.CostEstimate(flops=flops, bytes_accessed=moved, transcendentals=0),
    )(*operands)


def shape(*sizes, dtype=f32):
    return jax.ShapeDtypeStruct(sizes, dtype)


def involution(pairs):
    return [edge for a, b in pairs for edge in ((a, b), (b, a))]


def local(runs, count, velocity, magnetic, mass_blocks, stiff_blocks, twist_blocks, diffusivity, conn, lists):
    coefs, nodes = velocity.shape[1:]
    ghosts = lists.shape[1]
    elements = conn.shape[1]
    both = 2 * ghosts
    index = lax.axis_index("mesh")
    odd = index % 2
    low_valid = (index > 0).astype(jnp.int32)
    high_valid = (index < count - 1).astype(jnp.int32)
    far_valid = jnp.where(odd == 1, high_valid, low_valid)
    row = lax.broadcasted_iota(jnp.int32, (8, coefs), 0)
    flags = jnp.where(row == 0, odd, jnp.where(row == 1, low_valid, jnp.where(row == 2, high_valid, far_valid)))
    info = flags.astype(f32)

    near_pairs = [(i, i ^ 1) for i in range(count)]
    far_pairs = []
    for run in range(runs):
        base = run * count
        far_pairs += involution([(base + i, base + i + 1) for i in range(1, count - 1, 2)])
    if runs % 2 == 0:
        for run in range(0, runs, 2):
            for end in (0, count - 1):
                far_pairs += involution([(run * count + end, (run + 1) * count + end)])

    def swap_near(value):
        return lax.ppermute(value, "mesh", near_pairs)

    def swap_far(value):
        return lax.ppermute(value, ("runs", "mesh"), far_pairs)

    plane_table, coef_table, rotation, squares = transform_tables(coefs)
    plane_table, coef_table = jnp.asarray(plane_table), jnp.asarray(coef_table)
    rotation, squares = jnp.asarray(rotation), jnp.asarray(squares)
    ends = shape(6, ghosts, coefs)
    whole = shape(6, nodes, coefs)
    packs = shape(6, both, coefs)

    def swap_far_beside(value):
        return lax.ppermute(value, ("runs", "mesh"), far_pairs[::-1])

    def exchange(near, far):
        far = swap_far(far)
        return swap_near(near), far

    pick = call(pick_kernel, shape(both, nodes, dtype=bf16), [info, conn], flops=100_000_000, moved=1000)
    near, far, state = call(
        pack_velocity_kernel, [ends, ends, whole], [velocity, pick], flops=100_000_000, moved=1000
    )
    near, far, state = call(
        pack_magnetic_kernel,
        [ends, ends, whole],
        [magnetic, pick, near, far, state],
        aliases={2: 0, 3: 1, 4: 2},
        flops=100_000_000,
        moved=1000,
    )
    near_state, far_state = exchange(near, far)
    force = call(
        force_kernel, whole, [state, plane_table, coef_table, rotation], flops=2_000_000_000
    )
    dense, mass_ghost, rest_ghost, packed = call(
        build_kernel,
        [
            shape(5 * nodes, nodes + both),
            shape(both, 3 * both, dtype=bf16),
            shape(2, 2 * both, 3 * both, dtype=bf16),
            packs,
        ],
        [info, pick, mass_blocks, stiff_blocks, twist_blocks, diffusivity.reshape(1, elements), conn, lists]
        + [force, state, squares],
        scratch=[pltpu.VMEM((5 * nodes, 6 * elements), f32)],
        flops=1_000_000_000,
    )
    near, far, force_ghost = call(
        start_kernel,
        [ends, ends, packs],
        [info, far_state, near_state, packed, plane_table, coef_table, rotation, squares]
        + [mass_ghost, rest_ghost],
        flops=1_000_000_000,
    )
    near_now, far_now = exchange(near, far)
    own, ghost_ops, back_ops, vector0, image, packed, moments0 = call(
        first_kernel,
        [
            shape(2, 2 * nodes + 2 * both, 3 * nodes, dtype=bf16),
            shape(2, 2 * nodes + 2 * both, 3 * both, dtype=bf16),
            shape(2, 2 * both, 3 * nodes, dtype=bf16),
            whole,
            whole,
            packs,
            shape(8, coefs),
        ],
        [info, far_state, near_state, force_ghost, force, state, dense, pick, squares],
        flops=2_000_000_000,
    )
    near, far = call(
        send_kernel, [ends, ends], [info, far_now, near_now, packed, ghost_ops, squares], flops=100_000_000
    )
    near_next, far_next = exchange(near, far)
    vector1, far, packed_near, image, back1, moments1 = call(
        second_kernel,
        [whole, ends, ends, whole, ends, shape(16, coefs)],
        [info, far_now, near_now, near_next, image, vector0, own, ghost_ops, back_ops, squares],
        flops=1_000_000_000,
    )
    far_last = swap_far_beside(far)
    vector2, near = call(
        third_kernel, [whole, ends], [info, far_next, image, packed_near, ghost_ops, squares], flops=500_000_000
    )
    near_last = swap_near(near)
    back, moments = call(
        last_kernel,
        [packs, shape(40, coefs)],
        [vector2, vector1, own, back_ops, squares, moments0, moments1],
        flops=1_000_000_000,
    )
    if count % 8 == 0 and count <= 16:
        joined = call(
            functools.partial(join_kernel, 2.0, 2.0),
            shape(72, coefs // 2),
            [info, far_last, back1, near_last, back, moments, swap_near(moments)],
        )
        target = (2, 0, 3, 1)
        lines = count // 4
        half = None
        for step in range(lines):
            pairs = [(i, ((i // 4) ^ step) * 4 + target[i % 4]) for i in range(count)]
            term = lax.ppermute(joined, "mesh", pairs)
            half = term if half is None else half + term
        other = swap_near(half)
    else:
        joined = call(
            functools.partial(join_kernel, 1.0, 1.0), shape(72, coefs // 2), [info, far_last, back1, near_last, back, moments]
        )
        half = lax.psum(joined, "mesh")
        other = jnp.zeros_like(half)
    new_velocity, new_magnetic = call(
        finish_kernel,
        [shape(3, coefs, nodes), shape(3, coefs, nodes)],
        [half, other, velocity, magnetic, vector0, vector1, vector2],
        flops=10_000_000,
    )
    return new_velocity, new_magnetic


def solution(mesh):
    in_specs = (
        P("runs", None, "mesh"),
        P("runs", None, "mesh"),
        P(None, None, "mesh"),
        P(None, None, "mesh"),
        P(None, None, "mesh"),
        P(("runs", "mesh")),
        P(None, "mesh"),
        P(None, "mesh"),
    )
    out_specs = (P("runs", None, "mesh"), P("runs", None, "mesh"))
    sizes = dict(mesh.shape)
    step = functools.partial(local, sizes["runs"], sizes["mesh"])
    return jax.shard_map(step, mesh=mesh, in_specs=in_specs, out_specs=out_specs, check_vma=False)
```

```python
import functools
import math

import jax
import jax.numpy as jnp
import ml_dtypes
import numpy as np
from jax import lax
from jax.experimental import pallas as pl
from jax.experimental.pallas import tpu as pltpu
from jax.sharding import PartitionSpec as P

viscosity = 2.0
inverse_step = 10.0
tilt_factor = 0.5
axial_factor = 1.0
lorentz_factor = 0.005
epsilon = 1e-06
basis_scale = 512.0
residual_scale = 2.0**-8

f32 = jnp.float32
bf16 = jnp.bfloat16
VMEM = pl.BlockSpec(memory_space=pltpu.VMEM)


def split_table(table):
    high = table.astype(np.float32).astype(ml_dtypes.bfloat16)
    low = (table - high.astype(np.float64)).astype(np.float32).astype(ml_dtypes.bfloat16)
    return high, low


def transform_tables(coefs):
    planes = 2 * coefs
    mode = np.arange(coefs) // 2
    turns = (np.arange(planes)[:, None] * mode[None, :]) % planes
    angles = 2.0 * math.pi / planes * turns
    inverse = np.where(np.arange(coefs)[None, :] % 2 == 0, np.cos(angles), np.sin(angles))
    weight = np.where(mode == 0, 1.0, 2.0) / planes
    to_planes = np.concatenate(split_table(inverse.T.copy()), axis=0)
    to_coefs = np.concatenate(split_table(inverse * weight[None, :]), axis=0)
    phi = 2.0 * math.pi / planes * np.arange(planes)
    rows = np.zeros((8, planes), np.float32)
    rows[0] = -2.0 * tilt_factor * np.cos(phi)
    rows[1] = 2.0 * tilt_factor * np.sin(phi)
    rows[2] = -2.0 * axial_factor
    squares = np.zeros((8, coefs), np.float32)
    squares[:] = (mode * mode).astype(np.float32)[None, :]
    return to_planes, to_coefs, rows, squares


def halves(value):
    high = value.astype(bf16)
    return high, (value - high.astype(f32)).astype(bf16)


def dot(first, second):
    return lax.dot_general(first, second, (((1,), (0,)), ((), ())), preferred_element_type=f32)


def dot_nt(first, second):
    return lax.dot_general(first, second, (((1,), (1,)), ((), ())), preferred_element_type=f32)


def stacked_columns(value):
    high, low = halves(value)
    return jnp.concatenate([high, low, high], axis=1)


def stacked_rows(value):
    high, low = halves(value)
    return jnp.concatenate([high, high, low], axis=0)


def iota(shape, dim):
    return lax.broadcasted_iota(jnp.int32, shape, dim)


def one_hot(conn, first, count):
    row = iota((count, conn.shape[1]), 0) + first
    return jnp.concatenate([(row == conn[a : a + 1, :]).astype(bf16) for a in range(6)], axis=1)


def element_sides(conn, nodes, ghosts):
    own = jnp.max((conn < nodes).astype(f32), axis=0, keepdims=True)
    low = jnp.max(((conn >= nodes) & (conn < nodes + ghosts)).astype(f32), axis=0, keepdims=True)
    high = jnp.max((conn >= nodes + ghosts).astype(f32), axis=0, keepdims=True)
    return own, low, high


def eight_rows(items):
    row = iota((8, items[0].shape[1]), 0)
    total = jnp.zeros(row.shape, f32)
    for i, item in enumerate(items):
        total = jnp.where(row == i, item, total)
    return total


def pack_matrix(conn, odd, nodes, ghosts):
    _, low, high = element_sides(conn, nodes, ghosts)
    sides = eight_rows([low, high]).astype(bf16)
    sides = jnp.concatenate([sides] * 6, axis=1)
    named = dot_nt(sides, one_hot(conn, 0, nodes))
    flags = jnp.where(named > 0.0, 1.0, 0.0)
    before = (iota((nodes, nodes), 0) < iota((nodes, nodes), 1)).astype(bf16)
    ranks = dot(flags.astype(bf16), before).astype(jnp.int32)
    rows = iota((2 * ghosts, nodes), 0)
    picks = []
    odd = odd[:, :nodes].astype(jnp.int32)
    for side in range(2):
        offset = (1 - odd) * ghosts if side == 0 else odd * ghosts
        rank = ranks[side : side + 1, :]
        rank = jnp.where((flags[side : side + 1, :] > 0.0) & (rank < ghosts), rank + offset, -1)
        picks.append(rows == rank)
    return jnp.where(picks[0] | picks[1], 1.0, 0.0).astype(bf16)


def to_row(column, size):
    eye = iota((size, size), 0) == iota((size, size), 1)
    return jnp.sum(jnp.where(eye, column, 0.0), axis=0, keepdims=True)


def to_column(row, size):
    eye = iota((size, size), 0) == iota((size, size), 1)
    return jnp.sum(jnp.where(eye, row, 0.0), axis=1, keepdims=True)


def slot_matrix(conn, lists, info, nodes, ghosts):
    own, _, _ = element_sides(conn, nodes, ghosts)
    slot = iota((2 * ghosts, conn.shape[1]), 0) + nodes
    active = jnp.zeros((2 * ghosts, conn.shape[1]), f32)
    for a in range(conn.shape[0]):
        active = jnp.maximum(active, jnp.where(slot == conn[a : a + 1, :], own, 0.0))
    active = jnp.max(active, axis=1, keepdims=True)
    parts = []
    for side in range(2):
        flag = active[side * ghosts : (side + 1) * ghosts]
        node_row = lists[side : side + 1, :].astype(f32)
        node_column = to_column(node_row, ghosts)
        smaller = (node_row < node_column).astype(f32) * to_row(flag, ghosts)
        rank = jnp.sum(smaller, axis=1, keepdims=True).astype(jnp.int32)
        odd = info[0:1, : 2 * ghosts].astype(jnp.int32)
        offset = (1 - odd) * ghosts if side == 0 else odd * ghosts
        live = (flag > 0.0) & (info[1 + side : 2 + side, : 2 * ghosts] > 0.0)
        rows = iota((ghosts, 2 * ghosts), 1)
        parts.append(jnp.where(live & (rows == rank + offset), 1.0, 0.0))
    return jnp.concatenate(parts, axis=0).astype(bf16)


def pack_field(field, at, pick, near_ref, far_ref, state_ref):
    ghosts = near_ref.shape[1]
    for k in range(3):
        block = jnp.transpose(field[k])
        state_ref[at + k] = block
        first, rest = halves(block)
        packed = dot(pick, first) + dot(pick, rest)
        near_ref[at + k] = packed[:ghosts]
        far_ref[at + k] = packed[ghosts:]


def pick_kernel(info, conn_ref, pick_ref):
    rows, nodes = pick_ref.shape
    pick_ref[...] = pack_matrix(conn_ref[...], info[0:1, :], nodes, rows // 2)


def pack_velocity_kernel(velocity, pick_ref, near_ref, far_ref, state_ref):
    pack_field(velocity, 0, pick_ref[...], near_ref, far_ref, state_ref)


def pack_magnetic_kernel(
    magnetic, pick_ref, near_in, far_in, state_in, near_ref, far_ref, state_ref
):
    pack_field(magnetic, 3, pick_ref[...], near_ref, far_ref, state_ref)


def cross(a, b):
    return [
        a[1] * b[2] - a[2] * b[1],
        a[2] * b[0] - a[0] * b[2],
        a[0] * b[1] - a[1] * b[0],
    ]


def forcing(value, rows, planes_ref, coefs_ref, rotation_ref):
    coefs = value.shape[1]
    planes = planes_ref.shape[1]
    high, low = halves(value)
    part = planes // 2
    total = None
    for first in range(0, planes, part):
        lanes = slice(first, first + part)
        table = planes_ref[:coefs, lanes]
        phys = dot(high, table) + dot(low, table) + dot(high, planes_ref[coefs:, lanes])
        u = [phys[k * rows : (k + 1) * rows] for k in range(3)]
        b = [phys[(3 + k) * rows : (4 + k) * rows] for k in range(3)]
        turn = [rotation_ref[k : k + 1, lanes] for k in range(3)]
        induction = cross(u, b)
        twisted = cross(turn, u)
        lorentz = cross(b, induction)
        force = [twisted[k] - lorentz_factor * lorentz[k] for k in range(3)]
        item_high, item_low = halves(jnp.concatenate(force + induction, axis=0))
        table = coefs_ref[lanes]
        term = dot(item_high, table) + dot(item_low, table)
        term = term + dot(item_high, coefs_ref[planes + first : planes + first + part])
        total = term if total is None else total + term
    return total


def triple(pair):
    return jnp.concatenate([pair[0], pair[1], pair[0]], axis=1)


def build_kernel(
    info, pick_ref, mass_ref, stiff_ref, twist_ref, rates_ref, conn_ref, lists_ref,
    dense_ref, mass_own_ref, rest_own_ref, mass_ghost_ref, rest_ghost_ref, z_ref,
):
    nodes = pick_ref.shape[1]
    elements = conn_ref.shape[1]
    ghosts = lists_ref.shape[1]
    count = 2 * ghosts
    conn = conn_ref[...]
    pick = pick_ref[...]
    remap = slot_matrix(conn, lists_ref[...], info, nodes, ghosts)
    rates = rates_ref[0:1, :]
    step = 16
    for row in range(0, nodes, step):
        number = iota((step, elements), 0) + row
        hits = [(number == conn[a : a + 1, :]).astype(f32) for a in range(6)]
        for g, block in enumerate((mass_ref, stiff_ref, twist_ref)):
            for b in range(6):
                total = hits[0] * block[0, b : b + 1, :]
                for a in range(1, 6):
                    total = total + hits[a] * block[a, b : b + 1, :]
                lanes = pl.ds(b * elements, elements)
                z_ref[pl.ds(g * nodes + row, step), lanes] = total
                if g > 0:
                    z_ref[pl.ds((g + 2) * nodes + row, step), lanes] = total * rates
    arrives = lax.dot_general(
        remap, one_hot(conn, nodes, count), (((0,), (0,)), ((), ())), preferred_element_type=f32
    )
    column = jnp.concatenate([one_hot(conn, 0, nodes), arrives.astype(bf16)], axis=0)
    z = z_ref[...]
    first, second = halves(z)
    dense = dot_nt(first, column) + dot_nt(second, column)
    dense_ref[...] = dense
    high, low = halves(dense)
    pairs = []
    for g in range(5):
        rows = slice(g * nodes, (g + 1) * nodes)
        factor = residual_scale * (viscosity if g in (1, 2) else 1.0)
        pairs.append([(factor * dot(pick, item[rows])).astype(bf16) for item in (high, low)])

    def own_part(pair):
        return triple([item[:, :nodes] for item in pair])

    def ghost_part(pair):
        return triple([item[:, nodes:] for item in pair])

    mass_own_ref[...] = own_part(pairs[0])
    mass_ghost_ref[...] = ghost_part(pairs[0])
    for f in range(2):
        used = (pairs[1], pairs[2]) if f == 0 else (pairs[3], pairs[4])
        rest_own_ref[f] = jnp.concatenate([own_part(pair) for pair in used], axis=0)
        rest_ghost_ref[f] = jnp.concatenate([ghost_part(pair) for pair in used], axis=0)


def force_kernel(
    state, planes_ref, coefs_ref, rotation_ref, squares_ref, mass_own, rest_own,
    force_ref, packed_ref,
):
    nodes = state.shape[1]
    count = packed_ref.shape[1]
    value = state[...].reshape(6 * nodes, state.shape[2])
    force_ref[...] = forcing(
        value, nodes, planes_ref, coefs_ref, rotation_ref
    ).reshape(force_ref.shape)
    square = squares_ref[0:1, :]
    for k in range(6):
        from_force = dot(mass_own[...], stacked_rows(force_ref[k]))
        from_state = dot(rest_own[k // 3], stacked_rows(state[k]))
        packed_ref[k] = from_force - (from_state[:count] + square * from_state[count:])


def ghost_block(info, near, far, k):
    distant = jnp.where(info[3:4, :] > 0.0, far[k], 0.0)
    return jnp.concatenate([near[k], distant], axis=0)


def start_kernel(
    info, far, near, packed, planes_ref, coefs_ref, rotation_ref, squares_ref, mass_ghost, rest_ghost,
    near_out, far_out, force_out,
):
    ghosts = near.shape[1]
    count = 2 * ghosts
    blocks = [ghost_block(info, near, far, k) for k in range(6)]
    value = jnp.concatenate(blocks, axis=0)
    force = forcing(value, count, planes_ref, coefs_ref, rotation_ref)
    square = squares_ref[0:1, :]
    for k in range(6):
        item = force[k * count : (k + 1) * count]
        force_out[k] = item
        from_force = dot(mass_ghost[...], stacked_rows(item))
        from_state = dot(rest_ghost[k // 3], stacked_rows(blocks[k]))
        total = packed[k] + from_force - (from_state[:count] + square * from_state[count:])
        near_out[k] = total[:ghosts]
        far_out[k] = total[ghosts:]


def apply_own(own, value, k, square, nodes, count):
    image = dot(own[k // 3], stacked_rows(value))
    full = image[:nodes] + square * image[nodes : 2 * nodes]
    packed = image[2 * nodes : 2 * nodes + count] + square * image[2 * nodes + count :]
    return full, packed


def first_kernel(
    info, far, near, force_ghost, force, state, dense_ref, pick_ref, squares_ref,
    own_ref, ghost_ref, back_ref, vector_out, image_out, packed_out, moments_out,
):
    nodes = state.shape[1]
    count = force_ghost.shape[1]
    square = squares_ref[0:1, :]
    pick = pick_ref[...]
    mass, stiff, twist, rate_stiff, rate_twist = [
        dense_ref[pl.ds(g * nodes, nodes), :] for g in range(5)
    ]
    mass_op = stacked_columns(residual_scale * mass)
    rest_ops = []
    for f in range(2):
        still = viscosity * stiff if f == 0 else rate_stiff
        turn = viscosity * twist if f == 0 else rate_twist
        rest = [stacked_columns(residual_scale * item) for item in (still, turn)]
        rest_ops.append(jnp.concatenate(rest, axis=0))
        image = (inverse_step * mass + still) * (1.0 / basis_scale)
        turn = turn * (1.0 / basis_scale)
        pairs = [halves(image), halves(turn)]
        pairs = pairs + [[dot(pick, item).astype(bf16) for item in pair] for pair in pairs]
        own_ref[f] = jnp.concatenate(
            [triple([item[:, :nodes] for item in pair]) for pair in pairs], axis=0
        )
        ghost_ref[f] = jnp.concatenate(
            [triple([item[:, nodes:] for item in pair]) for pair in pairs], axis=0
        )
        back = [jnp.transpose(item[:, nodes:]) for item in (image, turn)]
        back_ref[f] = jnp.concatenate([stacked_columns(item) for item in back], axis=0)
    for k in range(6):
        wide_force = jnp.concatenate([force[k], force_ghost[k]], axis=0)
        wide_state = jnp.concatenate([state[k], ghost_block(info, near, far, k)], axis=0)
        from_force = dot(mass_op, stacked_rows(wide_force))
        from_state = dot(rest_ops[k // 3], stacked_rows(wide_state))
        total = from_force - (from_state[:nodes] + square * from_state[nodes:])
        vector_out[k] = total
        full, packed = apply_own(own_ref, total, k, square, nodes, count)
        image_out[k] = full
        packed_out[k] = packed
        moments_out[k : k + 1, :] = jnp.sum(total * total, axis=0, keepdims=True)
    moments_out[6:8, :] = jnp.zeros((2, moments_out.shape[1]), f32)


def send_kernel(info, far, near, packed, ghost_ops, squares_ref, near_out, far_out):
    ghosts = near.shape[1]
    count = 2 * ghosts
    top = ghost_ops.shape[1] - 2 * count
    square = squares_ref[0:1, :]
    for k in range(6):
        image = dot(ghost_ops[k // 3, top:], stacked_rows(ghost_block(info, near, far, k)))
        total = packed[k] + image[:count] + square * image[count:]
        near_out[k] = total[:ghosts]
        far_out[k] = total[ghosts:]


def combine(image, square):
    half = image.shape[0] // 2
    return image[:half] + square * image[half:]


def near_only(near):
    return stacked_rows(jnp.concatenate([near, jnp.zeros_like(near)], axis=0))


def far_only(info, far):
    distant = jnp.where(info[3:4, :] > 0.0, far, 0.0)
    return stacked_rows(jnp.concatenate([jnp.zeros_like(far), distant], axis=0))


def second_kernel(
    info, far, near, near_next, image, before, own, ghost_ops, back_ops, squares_ref,
    vector_out, far_out, packed_near, image_out, back_out, moments_out,
):
    nodes = image.shape[1]
    ghosts = near.shape[1]
    square = squares_ref[0:1, :]
    for k in range(6):
        ops = ghost_ops[k // 3, : 2 * nodes]
        total = image[k] + combine(dot(ops, stacked_rows(ghost_block(info, near, far, k))), square)
        vector_out[k] = total
        rows = stacked_rows(total)
        after = dot(own[k // 3], rows) + dot(ghost_ops[k // 3], near_only(near_next[k]))
        image_out[k] = combine(after[: 2 * nodes], square)
        packed = combine(after[2 * nodes :], square)
        packed_near[k] = packed[:ghosts]
        far_out[k] = packed[ghosts:]
        back_out[k] = combine(dot(back_ops[k // 3], rows), square)[ghosts:]
        moments_out[k : k + 1, :] = jnp.sum(before[k] * total, axis=0, keepdims=True)
        moments_out[6 + k : 7 + k, :] = jnp.sum(total * total, axis=0, keepdims=True)
    moments_out[12:16, :] = jnp.zeros((4, moments_out.shape[1]), f32)


def third_kernel(info, far, image, packed_near, ghost_ops, squares_ref, vector_out, near_out):
    nodes = image.shape[1]
    ghosts = far.shape[1]
    square = squares_ref[0:1, :]
    for k in range(6):
        part = dot(ghost_ops[k // 3], far_only(info, far[k]))
        vector_out[k] = image[k] + combine(part[: 2 * nodes], square)
        near_out[k] = packed_near[k] + combine(part[2 * nodes :], square)[:ghosts]


def last_kernel(
    vector, before, own, back_ops, squares_ref, first, second, back_out, moments_out
):
    nodes = vector.shape[1]
    square = squares_ref[0:1, :]
    moments_out[0:6] = first[0:6]
    moments_out[6:18] = second[0:12]
    for k in range(6):
        value = vector[k]
        rows = stacked_rows(value)
        after = combine(dot(own[k // 3, : 2 * nodes], rows), square)
        back_out[k] = combine(dot(back_ops[k // 3], rows), square)
        moments_out[18 + k : 19 + k, :] = jnp.sum(before[k] * value, axis=0, keepdims=True)
        moments_out[24 + k : 25 + k, :] = jnp.sum(value * value, axis=0, keepdims=True)
        moments_out[30 + k : 31 + k, :] = jnp.sum(after * value, axis=0, keepdims=True)
    moments_out[36:40, :] = jnp.zeros((4, moments_out.shape[1]), f32)


def join_kernel(far_weight, near_weight, info, far, sent, near, back, moments, *rest):
    ghosts = near.shape[1]
    out = rest[-1]
    half = out.shape[1]
    total = moments[...]
    for other in rest[:-1]:
        total = total + other[...]
    out[0:36] = total[:36, :half]
    out[36:72] = total[:36, half:]
    for k in range(6):
        distant = jnp.where(info[3:4, :] > 0.0, far[k] + sent[k], 0.0)
        crossing = far_weight * jnp.sum(distant * back[k, ghosts:], axis=0, keepdims=True)
        crossing += near_weight * jnp.sum(near[k] * back[k, :ghosts], axis=0, keepdims=True)
        out[30 + k : 31 + k, :] += crossing[:, :half]
        out[66 + k : 67 + k, :] += crossing[:, half:]


def finish_kernel(moments, other, velocity, magnetic, first, second, third, velocity_out, magnetic_out):
    total = moments[...] + other[...]
    total = jnp.concatenate([total[:36], total[36:]], axis=1)
    m0, m1, m2, m3, m4, m5 = [total[6 * j : 6 * j + 6, :] for j in range(6)]
    scale = basis_scale
    small = epsilon * residual_scale * residual_scale
    alpha0 = m0 / (scale * m1 + small)
    q1 = -alpha0 * scale
    rr1 = jnp.maximum(m0 + 2.0 * q1 * m1 + q1 * q1 * m2, 0.0)
    beta0 = rr1 / (m0 + small)
    p0 = 1.0 + beta0
    p1 = q1
    alpha1 = rr1 / (scale * (p0 * p0 * m1 + 2.0 * p0 * p1 * m2 + p1 * p1 * m3) + small)
    step1 = alpha1 * scale
    r1 = q1 - step1 * p0
    r2 = -step1 * p1
    rr2 = m0 + r1 * r1 * m2 + r2 * r2 * m4 + 2.0 * (r1 * m1 + r2 * m2 + r1 * r2 * m3)
    rr2 = jnp.maximum(rr2, 0.0)
    beta1 = rr2 / (rr1 + small)
    d0 = 1.0 + beta1 * p0
    d1 = r1 + beta1 * p1
    d2 = r2
    curve = d0 * d0 * m1 + d1 * d1 * m3 + d2 * d2 * m5
    curve = curve + 2.0 * (d0 * d1 * m2 + d0 * d2 * m3 + d1 * d2 * m4)
    alpha2 = rr2 / (scale * curve + small)
    back = 1.0 / residual_scale
    c0 = back * (alpha0 + alpha1 * p0 + alpha2 * d0)
    c1 = back * (alpha1 * p1 + alpha2 * d1)
    c2 = back * (alpha2 * d2)
    for k in range(6):
        source, out = (velocity, velocity_out) if k < 3 else (magnetic, magnetic_out)
        change = (
            c0[k : k + 1, :] * first[k] + c1[k : k + 1, :] * second[k] + c2[k : k + 1, :] * third[k]
        )
        out[k % 3] = source[k % 3] + jnp.transpose(change)


def call(kernel, outs, operands, scratch=(), flops=0, limit=24, aliases=None, moved=None):
    single = not isinstance(outs, list)
    shapes = [outs] if single else outs
    moved = moved or sum(math.prod(o.shape) * o.dtype.itemsize for o in list(operands) + shapes)
    return pl.pallas_call(
        kernel,
        out_shape=outs,
        in_specs=[VMEM] * len(operands),
        out_specs=VMEM if single else [VMEM] * len(outs),
        scratch_shapes=list(scratch),
        input_output_aliases=aliases or {},
        compiler_params=pltpu.CompilerParams(vmem_limit_bytes=limit * 1024 * 1024),
        cost_estimate=pl.CostEstimate(flops=flops, bytes_accessed=moved, transcendentals=0),
    )(*operands)


def shape(*sizes, dtype=f32):
    return jax.ShapeDtypeStruct(sizes, dtype)


def involution(pairs):
    return [edge for a, b in pairs for edge in ((a, b), (b, a))]


def local(runs, count, velocity, magnetic, mass_blocks, stiff_blocks, twist_blocks, diffusivity, conn, lists):
    coefs, nodes = velocity.shape[1:]
    ghosts = lists.shape[1]
    elements = conn.shape[1]
    both = 2 * ghosts
    index = lax.axis_index("mesh")
    odd = index % 2
    low_valid = (index > 0).astype(jnp.int32)
    high_valid = (index < count - 1).astype(jnp.int32)
    far_valid = jnp.where(odd == 1, high_valid, low_valid)
    row = lax.broadcasted_iota(jnp.int32, (8, coefs), 0)
    flags = jnp.where(row == 0, odd, jnp.where(row == 1, low_valid, jnp.where(row == 2, high_valid, far_valid)))
    info = flags.astype(f32)

    near_pairs = [(i, i ^ 1) for i in range(count)]
    far_pairs = []
    for run in range(runs):
        base = run * count
        far_pairs += involution([(base + i, base + i + 1) for i in range(1, count - 1, 2)])
    if runs % 2 == 0:
        for run in range(0, runs, 2):
            for end in (0, count - 1):
                far_pairs += involution([(run * count + end, (run + 1) * count + end)])

    def swap_near(value):
        return lax.ppermute(value, "mesh", near_pairs)

    def swap_far(value):
        return lax.ppermute(value, ("runs", "mesh"), far_pairs)

    plane_table, coef_table, rotation, squares = transform_tables(coefs)
    plane_table, coef_table = jnp.asarray(plane_table), jnp.asarray(coef_table)
    rotation, squares = jnp.asarray(rotation), jnp.asarray(squares)
    ends = shape(6, ghosts, coefs)
    whole = shape(6, nodes, coefs)
    packs = shape(6, both, coefs)

    def swap_far_beside(value):
        return lax.ppermute(value, ("runs", "mesh"), far_pairs[::-1])

    def exchange(near, far):
        far = swap_far(far)
        return swap_near(near), far

    pick = call(pick_kernel, shape(both, nodes, dtype=bf16), [info, conn], flops=100_000_000, moved=1000)
    near, far, state = call(
        pack_velocity_kernel, [ends, ends, whole], [velocity, pick], flops=100_000_000, moved=1000
    )
    near, far, state = call(
        pack_magnetic_kernel,
        [ends, ends, whole],
        [magnetic, pick, near, far, state],
        aliases={2: 0, 3: 1, 4: 2},
        flops=100_000_000,
        moved=1000,
    )
    near_state, far_state = exchange(near, far)
    dense, mass_own, rest_own, mass_ghost, rest_ghost = call(
        build_kernel,
        [
            shape(5 * nodes, nodes + both),
            shape(both, 3 * nodes, dtype=bf16),
            shape(2, 2 * both, 3 * nodes, dtype=bf16),
            shape(both, 3 * both, dtype=bf16),
            shape(2, 2 * both, 3 * both, dtype=bf16),
        ],
        [info, pick, mass_blocks, stiff_blocks, twist_blocks, diffusivity.reshape(1, elements), conn, lists],
        scratch=[pltpu.VMEM((5 * nodes, 6 * elements), f32)],
        flops=1_000_000_000,
    )
    force, packed = call(
        force_kernel,
        [whole, packs],
        [state, plane_table, coef_table, rotation, squares, mass_own, rest_own],
        flops=2_000_000_000,
    )
    near, far, force_ghost = call(
        start_kernel,
        [ends, ends, packs],
        [info, far_state, near_state, packed, plane_table, coef_table, rotation, squares]
        + [mass_ghost, rest_ghost],
        flops=1_000_000_000,
    )
    near_now, far_now = exchange(near, far)
    own, ghost_ops, back_ops, vector0, image, packed, moments0 = call(
        first_kernel,
        [
            shape(2, 2 * nodes + 2 * both, 3 * nodes, dtype=bf16),
            shape(2, 2 * nodes + 2 * both, 3 * both, dtype=bf16),
            shape(2, 2 * both, 3 * nodes, dtype=bf16),
            whole,
            whole,
            packs,
            shape(8, coefs),
        ],
        [info, far_state, near_state, force_ghost, force, state, dense, pick, squares],
        flops=2_000_000_000,
    )
    near, far = call(
        send_kernel, [ends, ends], [info, far_now, near_now, packed, ghost_ops, squares], flops=100_000_000
    )
    near_next, far_next = exchange(near, far)
    vector1, far, packed_near, image, back1, moments1 = call(
        second_kernel,
        [whole, ends, ends, whole, ends, shape(16, coefs)],
        [info, far_now, near_now, near_next, image, vector0, own, ghost_ops, back_ops, squares],
        flops=1_000_000_000,
    )
    far_last = swap_far_beside(far)
    vector2, near = call(
        third_kernel, [whole, ends], [info, far_next, image, packed_near, ghost_ops, squares], flops=500_000_000
    )
    near_last = swap_near(near)
    back, moments = call(
        last_kernel,
        [packs, shape(40, coefs)],
        [vector2, vector1, own, back_ops, squares, moments0, moments1],
        flops=1_000_000_000,
    )
    if count % 8 == 0 and count <= 16:
        joined = call(
            functools.partial(join_kernel, 2.0, 2.0),
            shape(72, coefs // 2),
            [info, far_last, back1, near_last, back, moments, swap_near(moments)],
        )
        target = (2, 0, 3, 1)
        lines = count // 4
        half = None
        for step in range(lines):
            pairs = [(i, ((i // 4) ^ step) * 4 + target[i % 4]) for i in range(count)]
            term = lax.ppermute(joined, "mesh", pairs)
            half = term if half is None else half + term
        other = swap_near(half)
    else:
        joined = call(
            functools.partial(join_kernel, 1.0, 1.0), shape(72, coefs // 2), [info, far_last, back1, near_last, back, moments]
        )
        half = lax.psum(joined, "mesh")
        other = jnp.zeros_like(half)
    new_velocity, new_magnetic = call(
        finish_kernel,
        [shape(3, coefs, nodes), shape(3, coefs, nodes)],
        [half, other, velocity, magnetic, vector0, vector1, vector2],
        flops=10_000_000,
    )
    return new_velocity, new_magnetic


def solution(mesh):
    in_specs = (
        P("runs", None, "mesh"),
        P("runs", None, "mesh"),
        P(None, None, "mesh"),
        P(None, None, "mesh"),
        P(None, None, "mesh"),
        P(("runs", "mesh")),
        P(None, "mesh"),
        P(None, "mesh"),
    )
    out_specs = (P("runs", None, "mesh"), P("runs", None, "mesh"))
    sizes = dict(mesh.shape)
    step = functools.partial(local, sizes["runs"], sizes["mesh"])
    return jax.shard_map(step, mesh=mesh, in_specs=in_specs, out_specs=out_specs, check_vma=False)
```
